32 devices in a mesh: rep: 8 (over z, y), fsdp: 4 (over x, core).
Axes of the slice: x: 2, y: 2, z: 4, core: 2. Of those that a mesh axis runs over, the one named last changes fastest.
Arguments:
- tokens: bfloat16 [8, 512, 512], P('rep', 'fsdp'), may hold values from -6 to 6
- states: bfloat16 [8, 256, 512], P('rep', 'fsdp'), may hold values from -6 to 6
- query_w: bfloat16 [512, 384], P('fsdp'), may hold values from -0.0625 to 0.0625
- key_w: bfloat16 [512, 384], P('fsdp'), may hold values from -0.25 to 0.25
- value_w: bfloat16 [512, 384], P('fsdp'), may hold values from -0.25 to 0.25
- out_w: bfloat16 [384, 512], P(None, 'fsdp'), may hold values from -0.875 to 0.875
- cross_query_w: bfloat16 [512, 384], P('fsdp'), may hold values from -0.0625 to 0.0625
- cross_key_w: bfloat16 [512, 384], P('fsdp'), may hold values from -0.25 to 0.25
- cross_value_w: bfloat16 [512, 384], P('fsdp'), may hold values from -0.25 to 0.25
- cross_out_w: bfloat16 [384, 512], P(None, 'fsdp'), may hold values from -0.875 to 0.875
- gate_w: bfloat16 [512, 1024], P('fsdp'), may hold values from -0.25 to 0.25
- up_w: bfloat16 [512, 1024], P('fsdp'), may hold values from -0.25 to 0.25
- down_w: bfloat16 [1024, 512], P('fsdp'), may hold values from -0.375 to 0.375
- self_gain: bfloat16 [512], P('fsdp'), may hold values from 0.5 to 1.5
- cross_gain: bfloat16 [512], P('fsdp'), may hold values from 0.5 to 1.5
- mlp_gain: bfloat16 [512], P('fsdp'), may hold values from 0.5 to 1.5
- bias_table: bfloat16 [32, 6], P('fsdp'), may hold values from -4 to 4
- cotangent: bfloat16 [8, 512, 512], P('rep', 'fsdp'), may hold values from -6 to 6
Outputs:
- output: bfloat16 [8, 512, 512], P('rep', 'fsdp')
- grad_tokens: float32 [8, 512, 512], P('rep', 'fsdp')
- grad_states: float32 [8, 256, 512], P('rep', 'fsdp')
- grad_query_w: float32 [512, 384], P('fsdp')
- grad_key_w: float32 [512, 384], P('fsdp')
- grad_value_w: float32 [512, 384], P('fsdp')
- grad_out_w: float32 [384, 512], P(None, 'fsdp')
- grad_cross_query_w: float32 [512, 384], P('fsdp')
- grad_cross_key_w: float32 [512, 384], P('fsdp')
- grad_cross_value_w: float32 [512, 384], P('fsdp')
- grad_cross_out_w: float32 [384, 512], P(None, 'fsdp')
- grad_gate_w: float32 [512, 1024], P('fsdp')
- grad_up_w: float32 [512, 1024], P('fsdp')
- grad_down_w: float32 [1024, 512], P('fsdp')
- grad_self_gain: float32 [512], P('fsdp')
- grad_cross_gain: float32 [512], P('fsdp')
- grad_mlp_gain: float32 [512], P('fsdp')
- grad_bias_table: float32 [32, 6], P('fsdp')
The draws below stay inside these ranges and needn't reach their ends.
All inputs are finite; a program needn't handle non-finite values.
Results may differ from the reference program's by a relative error of at most 0.028.
The reference program's roundings to bfloat16 on the way (of `normed_one`, `self_mixed`, `normed_two`, `cross_mixed`, `normed_three` and `units`) count: a program that leaves them out, or rounds other values in their place, can miss the bound.
Values may be sent and summed in bfloat16 or wider, within the bound.
No kernel may reach another device: no remote copies, remote signals or barrier semaphores. Data moves between devices by JAX's collectives and lax.ppermute only.
A program may use at most 128 MiB of HBM per device.

```python
import math
import jax
import jax.numpy as jnp
from jax import lax

D = 512
H = 6
DH = 64
FF = 1024
BUCKETS = 32
MAXDIST = 128
INNER = 384
LEN = 512
ENC = 256
SEQS = 8


def block_scale(stream_key, shape, pieces, low, top_value):
    level = 1.0
    for axis_at, blocks in pieces:
        steps = jax.random.uniform(jax.random.fold_in(jax.random.fold_in(stream_key, 6), axis_at), (blocks,), jnp.float32, low / len(pieces), top_value / len(pieces))
        level = level * jnp.repeat(jnp.exp(steps), shape[axis_at] // blocks).reshape((-1,) + (1,) * (len(shape) - 1 - axis_at))
    return level


def noise(own_key, dims, scale, limit, shards=(), held_as=jnp.bfloat16):
    loudness = block_scale(own_key, dims, shards, -0.22, 0.18) if shards else 1.0
    drawn = jax.random.normal(own_key, dims, jnp.float32) * scale * loudness
    return jnp.minimum(jnp.maximum(drawn, -limit), limit).astype(held_as)


def setup_inputs(seed: int = 0) -> dict:
    key_of = jax.random.split(jax.random.key(seed), 19)
    tokens = noise(key_of[0], (SEQS, LEN, D), 1.0, 6.0, ((0, 8), (1, 4)))
    states = noise(key_of[1], (SEQS, ENC, D), 1.0, 6.0, ((0, 8), (1, 4)))
    query_w = noise(key_of[2], (D, INNER), (16 * D) ** -0.5, 0.0625, ((0, 4),))
    key_w = noise(key_of[3], (D, INNER), D ** -0.5, 0.25, ((0, 4),))
    value_w = noise(key_of[4], (D, INNER), D ** -0.5, 0.25, ((0, 4),))
    out_w = noise(key_of[5], (INNER, D), (INNER // 8) ** -0.5, 0.875, ((1, 4),))
    cross_query_w = noise(key_of[6], (D, INNER), (16 * D) ** -0.5, 0.0625, ((0, 4),))
    cross_key_w = noise(key_of[7], (D, INNER), D ** -0.5, 0.25, ((0, 4),))
    cross_value_w = noise(key_of[8], (D, INNER), D ** -0.5, 0.25, ((0, 4),))
    cross_out_w = noise(key_of[9], (INNER, D), (INNER // 8) ** -0.5, 0.875, ((1, 4),))
    gate_w = noise(key_of[10], (D, FF), D ** -0.5, 0.25, ((0, 4),))
    up_w = noise(key_of[11], (D, FF), D ** -0.5, 0.25, ((0, 4),))
    down_w = noise(key_of[12], (FF, D), (FF // 4) ** -0.5, 0.375, ((0, 4),))
    self_gain = jnp.clip(1.0 + 0.1 * jax.random.normal(key_of[13], (D,), jnp.float32), 0.5, 1.5).astype(jnp.bfloat16)
    cross_gain = jnp.clip(1.0 + 0.1 * jax.random.normal(key_of[14], (D,), jnp.float32), 0.5, 1.5).astype(jnp.bfloat16)
    mlp_gain = jnp.clip(1.0 + 0.1 * jax.random.normal(key_of[15], (D,), jnp.float32), 0.5, 1.5).astype(jnp.bfloat16)
    bias_table = noise(key_of[16], (BUCKETS, H), 1.0, 4.0, ((0, 4),))
    cotangent = noise(key_of[17], (SEQS, LEN, D), 1.0, 6.0, ((0, 8), (1, 4)))
    return dict(tokens=tokens, states=states, query_w=query_w, key_w=key_w, value_w=value_w, out_w=out_w, cross_query_w=cross_query_w, cross_key_w=cross_key_w, cross_value_w=cross_value_w, cross_out_w=cross_out_w, gate_w=gate_w, up_w=up_w, down_w=down_w, self_gain=self_gain, cross_gain=cross_gain, mlp_gain=mlp_gain, bias_table=bias_table, cotangent=cotangent)


EPSILON = 1e-06
MASKED = -1000000000.0
HIGHEST = lax.Precision.HIGHEST

@jax.custom_vjp
def low(v):
    return lax.optimization_barrier(v.astype(jnp.bfloat16)).astype(jnp.float32)

@jax.custom_vjp
def low_back(v):
    return v

def low_keep(v):
    return (low(v), None)

def low_pass(kept, grad):
    return (grad,)

def back_keep(v):
    return (v, None)

def back_low(kept, grad):
    return (low(grad),)
low.defvjp(low_keep, low_pass)
low_back.defvjp(back_keep, back_low)

def rms_norm(row_block, gain_vec):
    inverse_rms = lax.rsqrt(lax.optimization_barrier(jnp.mean(row_block * row_block, axis=-1, keepdims=True)) + EPSILON)
    return row_block * inverse_rms * gain_vec

def gelu_tanh(values_in):
    return 0.5 * values_in * (1.0 + jnp.tanh(0.7978845608028654 * (values_in + 0.044715 * values_in * values_in * values_in)))

def glu_mix(gate_pre, up_pre):
    return gelu_tanh(gate_pre) * up_pre

def bucket_of(distance):
    exact_span = BUCKETS // 2
    bucket = jnp.minimum(distance, exact_span)
    for power in range(1, exact_span):
        threshold = math.ceil(exact_span * (MAXDIST / exact_span) ** (power / exact_span))
        bucket = bucket + (distance >= threshold).astype(jnp.int32)
    return bucket

def matmul(left_rows, right_rows):
    return jnp.dot(left_rows, right_rows, precision=HIGHEST, preferred_element_type=jnp.float32)

def attention(queries, keys_in, values_in, bias_block, allowed):
    query_heads = queries.reshape(queries.shape[0], H, DH)
    key_heads = keys_in.reshape(keys_in.shape[0], H, DH)
    value_heads = values_in.reshape(values_in.shape[0], H, DH)
    scores = low_back(jnp.einsum('qhd,khd->hqk', query_heads, key_heads, precision=HIGHEST))
    if bias_block is not None:
        scores = jnp.where(allowed[None], scores + bias_block, MASKED)
    shifted = scores - lax.optimization_barrier(jnp.max(scores, axis=-1, keepdims=True))
    lifted = jnp.exp(shifted)
    attn_probs = lifted / lax.optimization_barrier(jnp.sum(lifted, axis=-1, keepdims=True))
    mixed_heads = jnp.einsum('hqk,khd->qhd', low(attn_probs), value_heads, precision=HIGHEST)
    return low(low_back(mixed_heads.reshape(queries.shape[0], H * DH)))

def layer_one(tokens_f, states_f, weights_f):
    query_w, key_w, value_w, out_w, cross_query_w, cross_key_w, cross_value_w, cross_out_w, gate_w, up_w, down_w, self_gain, cross_gain, mlp_gain, bias_table = weights_f
    normed_one = low(rms_norm(tokens_f, self_gain))
    queries = low(low_back(matmul(normed_one, query_w)))
    keys_in = low(low_back(matmul(normed_one, key_w)))
    values_in = low(low_back(matmul(normed_one, value_w)))
    positions = jnp.arange(tokens_f.shape[0], dtype=jnp.int32)
    distance = positions[:, None] - positions[None, :]
    bias_block = jnp.transpose(bias_table[bucket_of(jnp.maximum(distance, 0))], (2, 0, 1))
    self_mixed = attention(queries, keys_in, values_in, bias_block, distance >= 0)
    hidden_one = tokens_f + low_back(matmul(self_mixed, out_w))
    normed_two = low(rms_norm(hidden_one, cross_gain))
    cross_queries = low(low_back(matmul(normed_two, cross_query_w)))
    cross_keys = low(low_back(matmul(states_f, cross_key_w)))
    cross_values = low(low_back(matmul(states_f, cross_value_w)))
    cross_mixed = attention(cross_queries, cross_keys, cross_values, None, None)
    hidden_two = hidden_one + low_back(matmul(cross_mixed, cross_out_w))
    normed_three = low(rms_norm(hidden_two, mlp_gain))
    gate_pre = low_back(matmul(normed_three, gate_w))
    up_pre = low_back(matmul(normed_three, up_w))
    units = low(glu_mix(gate_pre, up_pre))
    return hidden_two + low_back(matmul(units, down_w))

def reference(tokens, states, query_w, key_w, value_w, out_w, cross_query_w, cross_key_w, cross_value_w, cross_out_w, gate_w, up_w, down_w, self_gain, cross_gain, mlp_gain, bias_table, cotangent):
    weights_in = (query_w, key_w, value_w, out_w, cross_query_w, cross_key_w, cross_value_w, cross_out_w, gate_w, up_w, down_w, self_gain, cross_gain, mlp_gain, bias_table)
    weights_f = tuple((weight_arg.astype(jnp.float32) for weight_arg in weights_in))

    def forward(tokens_f, states_f, params_f):

        def one_sequence(packed):
            return layer_one(packed[0], packed[1], params_f)
        return lax.map(jax.checkpoint(one_sequence), (tokens_f, states_f))
    result, pullback = jax.vjp(forward, tokens.astype(jnp.float32), states.astype(jnp.float32), weights_f)
    grad_tokens, grad_states, grads = pullback(cotangent.astype(jnp.float32))
    return (result.astype(jnp.bfloat16), grad_tokens, grad_states, grads[0], grads[1], grads[2], grads[3], grads[4], grads[5], grads[6], grads[7], grads[8], grads[9], grads[10], grads[11], grads[12], grads[13], grads[14])
```

```python
import functools
import math

import jax
import jax.numpy as jnp
from jax import lax
from jax.experimental import pallas as pl
from jax.experimental.pallas import tpu as pltpu
from jax.sharding import PartitionSpec as P

H = 6
DH = 64
PAIRS = H // 2
BUCKETS = 32
MAXDIST = 128
EPSILON = 1e-06
MASKED = -1000000000.0
BLOCK = 128
HALF = 256
GROUP = 4
HIGHEST = lax.Precision.HIGHEST
F32 = jnp.float32
BF16 = jnp.bfloat16


def dot(a, b):
    return jnp.dot(a, b, preferred_element_type=F32)


def dot_t(a, b):
    return lax.dot_general(a, b, (((1,), (1,)), ((), ())), preferred_element_type=F32)


def t_dot(a, b):
    return lax.dot_general(a, b, (((0,), (0,)), ((), ())), preferred_element_type=F32)


def own(f, size):
    return pl.ds(pl.multiple_of(f * size, size), size)


def place_rows(dst, pieces, f, first, size):
    for k, piece in enumerate(pieces):
        dst[own(f ^ k, size), :] = piece[first : first + size, :].astype(dst.dtype)


def place_columns(dst, pieces, f, first, rows):
    for k, piece in enumerate(pieces):
        dst[:, own(f ^ k, piece.shape[1])] = piece[first : first + rows, :]


def bucket_of(distance):
    exact_span = BUCKETS // 2
    bucket = jnp.minimum(distance, exact_span)
    for power in range(1, exact_span):
        threshold = math.ceil(exact_span * (MAXDIST / exact_span) ** (power / exact_span))
        bucket = bucket + (distance >= threshold).astype(jnp.int32)
    return bucket


def offset_onehot(rows, axis):
    shape = (rows, 4 * BLOCK) if axis == 1 else (4 * BLOCK, rows)
    m = lax.broadcasted_iota(jnp.int32, shape, axis)
    n = jnp.where(m < 2 * BLOCK, BLOCK - m, 5 * BLOCK - m)
    bucket = bucket_of(jnp.maximum(n, 0))
    return (bucket == lax.broadcasted_iota(jnp.int32, shape, 1 - axis)).astype(F32)


def rms(v):
    return lax.rsqrt(jnp.mean(v * v, axis=-1, keepdims=True) + EPSILON)


def head_lanes(rows):
    lane = lax.broadcasted_iota(jnp.int32, (rows, 2 * DH), 1)
    return lane < DH


def only_head(pair, hd):
    low = head_lanes(pair.shape[0])
    zero = jnp.zeros_like(pair)
    return jnp.where(low, pair, zero) if hd == 0 else jnp.where(low, zero, pair)


def softmax(s):
    lifted = jnp.exp(s - jnp.max(s, axis=-1, keepdims=True))
    return lifted * (1.0 / jnp.sum(lifted, axis=-1, keepdims=True))


def norm_back(v, gain, q):
    r = rms(v)
    u = q * gain
    vr = v * r
    return r * (u - vr * jnp.mean(vr * u, axis=-1, keepdims=True)), q * vr


def self_forward(
    f_ref, t0, t1, t2, t3, w0, w1, w2, w3,
    normed_ref, qkv_ref, probs_ref, mixed_ref, aux_ref,
    x_s, w_s, band_s,
):
    f = f_ref[0]
    tokens, weights = (t0, t1, t2, t3), (w0, w1, w2, w3)
    length = x_s.shape[0]
    rows = length // GROUP
    inner = H * DH
    place_rows(x_s, tokens, f, 0, rows)
    place_rows(w_s, weights, f, 0, w0.shape[0])
    aux = sum(t[rows : rows + 16, :].astype(F32) for t in tokens)
    aux_ref[...] = aux
    for hb in range(length // HALF):
        at = slice(hb * HALF, (hb + 1) * HALF)
        x = x_s[at, :].astype(F32)
        normed = (x * rms(x) * aux[0:1, :]).astype(BF16)
        normed_ref[at, :] = normed
        qkv_ref[at, :] = dot(normed, w_s[...]).astype(BF16)
    per_offset = jnp.dot(
        aux[8:16, 0:BLOCK], offset_onehot(BLOCK, 1), precision=HIGHEST, preferred_element_type=F32
    )
    row = lax.broadcasted_iota(jnp.int32, (BLOCK, 2 * BLOCK), 0)
    col = lax.broadcasted_iota(jnp.int32, (BLOCK, 2 * BLOCK), 1)
    for h in range(H):
        spread = jnp.broadcast_to(per_offset[h : h + 1, :], (BLOCK, 4 * BLOCK))
        skewed = pltpu.roll(spread, 0, 1, stride=1, stride_axis=0)[:, : 2 * BLOCK]
        band_s[h] = jnp.where(col - BLOCK > row, MASKED, skewed)
    for p in range(PAIRS):
        k2 = qkv_ref[:, inner + p * BLOCK : inner + (p + 1) * BLOCK]
        v2 = qkv_ref[:, 2 * inner + p * BLOCK : 2 * inner + (p + 1) * BLOCK]
        v_only = [only_head(v2, hd) for hd in range(2)]
        for hb in range(length // HALF):
            q2 = qkv_ref[hb * HALF : (hb + 1) * HALF, p * BLOCK : (p + 1) * BLOCK]
            scores = [dot_t(only_head(q2, hd), k2[: (hb + 1) * HALF, :]) for hd in range(2)]
            for sub in range(2):
                rb = 2 * hb + sub
                seen = (rb + 1) * BLOCK
                out = jnp.zeros((BLOCK, BLOCK), F32)
                for hd in range(2):
                    h = 2 * p + hd
                    s = scores[hd][sub * BLOCK : (sub + 1) * BLOCK, :seen]
                    if rb == 0:
                        s = s + band_s[h, :, BLOCK:]
                    elif rb == 1:
                        s = s + band_s[h]
                    else:
                        far = seen - 2 * BLOCK
                        s = jnp.concatenate(
                            [s[:, :far] + per_offset[h : h + 1, 0:1], s[:, far:] + band_s[h]], axis=1
                        )
                    probs = softmax(s).astype(BF16)
                    probs_ref[h, rb * BLOCK : seen, :seen] = probs
                    out = out + dot(probs, v_only[hd][:seen, :])
                mixed_ref[rb * BLOCK : seen, p * BLOCK : (p + 1) * BLOCK] = out.astype(BF16)


def cross_forward(
    f_ref, t0, t1, t2, t3, mixed_ref, aux_ref, w0, w1, w2, w3, o0, o1, o2, o3, s0, s1, s2, s3,
    h1_ref, n2_ref, cq_ref, ckv_ref, probs_ref, cmixed_ref, h2_ref, n3_ref,
    x_s, w_s, out_s, co_s, states_s,
):
    f = f_ref[0]
    length = x_s.shape[0]
    inner = H * DH
    place_rows(x_s, (t0, t1, t2, t3), f, 0, length // GROUP)
    place_rows(w_s, (w0, w1, w2, w3), f, 0, w0.shape[0])
    place_columns(out_s, (o0, o1, o2, o3), f, 0, inner)
    place_columns(co_s, (o0, o1, o2, o3), f, inner, inner)
    place_rows(states_s, (s0, s1, s2, s3), f, 0, s0.shape[0])
    ckv_ref[...] = dot(states_s[...], w_s[:, inner:]).astype(BF16)
    for hb in range(length // HALF):
        at = slice(hb * HALF, (hb + 1) * HALF)
        hidden = x_s[at, :].astype(F32) + dot(mixed_ref[at, :], out_s[...])
        h1_ref[at, :] = hidden
        normed = (hidden * rms(hidden) * aux_ref[1:2, :]).astype(BF16)
        n2_ref[at, :] = normed
        cq_ref[at, :] = dot(normed, w_s[:, :inner]).astype(BF16)
    for p in range(PAIRS):
        k2 = ckv_ref[:, p * BLOCK : (p + 1) * BLOCK]
        v2 = ckv_ref[:, inner + p * BLOCK : inner + (p + 1) * BLOCK]
        v_only = [only_head(v2, hd) for hd in range(2)]
        for hb in range(length // HALF):
            at = slice(hb * HALF, (hb + 1) * HALF)
            q2 = cq_ref[at, p * BLOCK : (p + 1) * BLOCK]
            out = jnp.zeros((HALF, BLOCK), F32)
            for hd in range(2):
                probs = softmax(dot_t(only_head(q2, hd), k2)).astype(BF16)
                probs_ref[2 * p + hd, at, :] = probs
                out = out + dot(probs, v_only[hd])
            cmixed_ref[at, p * BLOCK : (p + 1) * BLOCK] = out.astype(BF16)
    for hb in range(length // HALF):
        at = slice(hb * HALF, (hb + 1) * HALF)
        hidden = h1_ref[at, :] + dot(cmixed_ref[at, :], co_s[...])
        h2_ref[at, :] = hidden
        n3_ref[at, :] = (hidden * rms(hidden) * aux_ref[2:3, :]).astype(BF16)


def feed_forward(
    f_ref, h2_ref, n3_ref, aux_ref, g0, g1, g2, g3, d0, d1, d2, d3,
    result_ref, grad_h2_ref, pack_ref, gain_ref,
    gu_s, down_s, cot_s, units_s, gate_s, up_s,
):
    f = f_ref[0]
    length, width = h2_ref.shape
    rows = length // GROUP
    hidden_units = down_s.shape[0]
    own_units = hidden_units // GROUP
    place_rows(gu_s, (g0, g1, g2, g3), f, 0, g0.shape[0])
    place_rows(down_s, (d0, d1, d2, d3), f, 0, own_units)
    place_rows(cot_s, (d0, d1, d2, d3), f, own_units, rows)
    gain = aux_ref[2:3, :]
    gain_sum = jnp.zeros((1, width), F32)
    for rb in range(length // BLOCK):
        at = slice(rb * BLOCK, (rb + 1) * BLOCK)
        pre = dot(n3_ref[at, :], gu_s[...])
        gate, up = pre[:, :hidden_units], pre[:, hidden_units:]
        grad_units = dot_t(cot_s[at, :], down_s[...])
        square = gate * gate
        tanh = jnp.tanh(0.7978845608028654 * (gate + 0.044715 * square * gate))
        half_gate = 0.5 * gate
        gelu = half_gate + half_gate * tanh
        slope = 0.5 + 0.5 * tanh + half_gate * (1.0 - tanh * tanh) * (
            0.7978845608028654 + (3 * 0.044715 * 0.7978845608028654) * square
        )
        units_s[at, :] = (gelu * up).astype(BF16)
        grad_gate = (grad_units * up * slope).astype(BF16)
        grad_up = (grad_units * gelu).astype(BF16)
        gate_s[at, :] = grad_gate
        up_s[at, :] = grad_up
        grad_normed = dot_t(grad_gate, gu_s[:, :hidden_units]) + dot_t(grad_up, gu_s[:, hidden_units:])
        piece, gain_part = norm_back(h2_ref[at, :], gain, grad_normed)
        grad_h2_ref[at, :] = cot_s[at, :].astype(F32) + piece
        gain_sum = gain_sum + jnp.sum(gain_part, axis=0, keepdims=True)
    gain_ref[...] = jnp.broadcast_to(gain_sum, gain_ref.shape)
    mine = own(f, rows)
    result_ref[...] = (h2_ref[mine, :] + dot(units_s[mine, :], down_s[...])).astype(BF16)
    own_rows = g0.shape[0]
    normed_own = n3_ref[:, own(f, own_rows)]
    pack_ref[:, :hidden_units] = t_dot(normed_own, gate_s[...]).astype(BF16)
    pack_ref[:, hidden_units : 2 * hidden_units] = t_dot(normed_own, up_s[...]).astype(BF16)
    grad_down = t_dot(units_s[:, own(f, own_units)], cot_s[...]).astype(BF16)
    for part in range(own_units // own_rows):
        first = 2 * hidden_units + part * width
        pack_ref[:, first : first + width] = grad_down[part * own_rows : (part + 1) * own_rows, :]


def cross_backward(
    f_ref, grad_h2_ref, h1_ref, n2_ref, cq_ref, ckv_ref, probs_ref, cmixed_ref, aux_ref,
    w0, w1, w2, w3, o0, o1, o2, o3, s0, s1, s2, s3,
    grad_h1_ref, grad_states_ref, pack_ref, gain_ref,
    w_s, co_s, states_s, low_s, mix_s, dq_s, dkv_s, ds_s,
):
    f = f_ref[0]
    length, width = h1_ref.shape
    inner = H * DH
    own_rows = w0.shape[0]
    place_rows(w_s, (w0, w1, w2, w3), f, 0, own_rows)
    place_columns(co_s, (o0, o1, o2, o3), f, inner, inner)
    place_rows(states_s, (s0, s1, s2, s3), f, 0, s0.shape[0])
    low = grad_h2_ref[...].astype(BF16)
    low_s[...] = low
    mix_s[...] = dot_t(low, co_s[...]).astype(BF16)
    grad_out = t_dot(cmixed_ref[...], low_s[:, own(f, o0.shape[1])]).astype(BF16)
    for part in range(inner // own_rows):
        first = inner * 3 + part * o0.shape[1]
        pack_ref[:, first : first + o0.shape[1]] = grad_out[part * own_rows : (part + 1) * own_rows, :]
    for p in range(PAIRS):
        lanes = slice(p * BLOCK, (p + 1) * BLOCK)
        k2 = ckv_ref[:, lanes]
        v2 = ckv_ref[:, inner + p * BLOCK : inner + (p + 1) * BLOCK]
        dq = jnp.zeros((length, BLOCK), F32)
        dk = jnp.zeros((k2.shape[0], BLOCK), F32)
        dv = jnp.zeros((k2.shape[0], BLOCK), F32)
        for hd in range(2):
            h = 2 * p + hd
            grad_mixed = only_head(mix_s[:, lanes], hd)
            for hb in range(length // HALF):
                at = slice(hb * HALF, (hb + 1) * HALF)
                probs = probs_ref[h, at, :].astype(F32)
                weighted = probs * dot_t(grad_mixed[at, :], v2)
                ds_s[at, :] = (weighted - probs * jnp.sum(weighted, axis=-1, keepdims=True)).astype(BF16)
            grad_scores = ds_s[...]
            dq = dq + dot(grad_scores, only_head(k2, hd))
            dk = dk + t_dot(grad_scores, only_head(cq_ref[:, lanes], hd))
            dv = dv + t_dot(probs_ref[h], grad_mixed)
        dq_s[:, lanes] = dq.astype(BF16)
        dkv_s[:, lanes] = dk.astype(BF16)
        dkv_s[:, inner + p * BLOCK : inner + (p + 1) * BLOCK] = dv.astype(BF16)
    gain = aux_ref[1:2, :]
    gain_sum = jnp.zeros((1, width), F32)
    for hb in range(length // HALF):
        at = slice(hb * HALF, (hb + 1) * HALF)
        grad_normed = dot_t(dq_s[at, :], w_s[:, :inner])
        piece, gain_part = norm_back(h1_ref[at, :], gain, grad_normed)
        grad_h1_ref[at, :] = grad_h2_ref[at, :] + piece
        gain_sum = gain_sum + jnp.sum(gain_part, axis=0, keepdims=True)
    gain_ref[...] = jnp.broadcast_to(gain_sum, gain_ref.shape)
    pack_ref[:, :inner] = t_dot(n2_ref[:, own(f, own_rows)], dq_s[...]).astype(BF16)
    pack_ref[:, inner : 3 * inner] = t_dot(states_s[:, own(f, own_rows)], dkv_s[...]).astype(BF16)
    grad_states_ref[...] = dot_t(dkv_s[own(f, s0.shape[0]), :], w_s[:, inner:])


def self_backward(
    f_ref, grad_h1_ref, normed_ref, qkv_ref, probs_ref, mixed_ref, aux_ref, gain2_ref, gain3_ref,
    t0, t1, t2, t3, w0, w1, w2, w3, o0, o1, o2, o3,
    grad_tokens_ref, pack_ref,
    x_s, w_s, out_s, low_s, mix_s, dqkv_s, ds_s, gain_s,
):
    f = f_ref[0]
    length, width = x_s.shape
    rows = length // GROUP
    inner = H * DH
    own_rows = w0.shape[0]
    place_rows(x_s, (t0, t1, t2, t3), f, 0, rows)
    place_rows(w_s, (w0, w1, w2, w3), f, 0, own_rows)
    place_columns(out_s, (o0, o1, o2, o3), f, 0, inner)
    low = grad_h1_ref[...].astype(BF16)
    low_s[...] = low
    mix_s[...] = dot_t(low, out_s[...]).astype(BF16)
    grad_out = t_dot(mixed_ref[...], low_s[:, own(f, o0.shape[1])]).astype(BF16)
    for part in range(inner // own_rows):
        first = inner * 3 + part * o0.shape[1]
        pack_ref[:, first : first + o0.shape[1]] = grad_out[part * own_rows : (part + 1) * own_rows, :]
    blocks = length // BLOCK
    row = lax.broadcasted_iota(jnp.int32, (BLOCK, 4 * BLOCK), 0)
    offset_sums, far_sums = [], []
    for p in range(PAIRS):
        lanes = slice(p * BLOCK, (p + 1) * BLOCK)
        k2 = qkv_ref[:, inner + p * BLOCK : inner + (p + 1) * BLOCK]
        v2 = qkv_ref[:, 2 * inner + p * BLOCK : 2 * inner + (p + 1) * BLOCK]
        q2 = qkv_ref[:, lanes]
        dq = [jnp.zeros((BLOCK, BLOCK), F32) for _ in range(blocks)]
        dk = [jnp.zeros((BLOCK, BLOCK), F32) for _ in range(blocks)]
        dv = [jnp.zeros((BLOCK, BLOCK), F32) for _ in range(blocks)]
        for hd in range(2):
            h = 2 * p + hd
            grad_mixed = only_head(mix_s[:, lanes], hd)
            k_only, q_only = only_head(k2, hd), only_head(q2, hd)
            near = jnp.zeros((BLOCK, BLOCK), F32)
            next_to = jnp.zeros((BLOCK, BLOCK), F32)
            far = jnp.zeros((BLOCK, BLOCK), F32)
            for rb in range(blocks):
                seen = (rb + 1) * BLOCK
                at = slice(rb * BLOCK, seen)
                probs = probs_ref[h, at, :seen].astype(F32)
                weighted = probs * dot_t(grad_mixed[at, :], v2[:seen, :])
                ds = weighted - probs * jnp.sum(weighted, axis=-1, keepdims=True)
                near = near + ds[:, rb * BLOCK :]
                if rb >= 1:
                    next_to = next_to + ds[:, (rb - 1) * BLOCK : rb * BLOCK]
                for c in range(rb - 1):
                    far = far + ds[:, c * BLOCK : (c + 1) * BLOCK]
                low_ds = ds.astype(BF16)
                ds_s[at, :seen] = low_ds
                dq[rb] = dq[rb] + dot(low_ds, k_only[:seen, :])
            for c in range(blocks):
                below, keys = slice(c * BLOCK, length), slice(c * BLOCK, (c + 1) * BLOCK)
                dk[c] = dk[c] + t_dot(ds_s[below, keys], q_only[below, :])
                dv[c] = dv[c] + t_dot(probs_ref[h, below, keys], grad_mixed[below, :])
            skew = jnp.concatenate([next_to, near, jnp.zeros((BLOCK, 2 * BLOCK), F32)], axis=1)
            for bit in range(BLOCK.bit_length() - 1):
                moved = pltpu.roll(skew, 4 * BLOCK - (1 << bit), 1)
                skew = jnp.where((row & (1 << bit)) != 0, moved, skew)
            offset_sums.append(jnp.sum(skew, axis=0, keepdims=True))
            far_sums.append(jnp.sum(jnp.sum(far, axis=0, keepdims=True), axis=1, keepdims=True))
        for c in range(blocks):
            at = slice(c * BLOCK, (c + 1) * BLOCK)
            dqkv_s[at, lanes] = dq[c].astype(BF16)
            dqkv_s[at, inner + p * BLOCK : inner + (p + 1) * BLOCK] = dk[c].astype(BF16)
            dqkv_s[at, 2 * inner + p * BLOCK : 2 * inner + (p + 1) * BLOCK] = dv[c].astype(BF16)
    per_offset = jnp.concatenate(offset_sums + [jnp.zeros((2, 4 * BLOCK), F32)], axis=0)
    per_bucket = jnp.dot(
        per_offset, offset_onehot(BLOCK, 0), precision=HIGHEST, preferred_element_type=F32
    )
    far_all = jnp.concatenate(far_sums + [jnp.zeros((2, 1), F32)], axis=0)
    lane = lax.broadcasted_iota(jnp.int32, (8, BLOCK), 1)
    per_bucket = per_bucket + jnp.where(lane == BUCKETS - 1, far_all, 0.0)

    gain = aux_ref[0:1, :]
    mine = own(f, rows)
    grad_normed = dot_t(dqkv_s[mine, :], w_s[...])
    piece, _ = norm_back(x_s[mine, :].astype(F32), gain, grad_normed)
    grad_tokens_ref[...] = grad_h1_ref[mine, :] + piece
    own_columns = own(f, own_rows)
    x = x_s[...].astype(F32)
    grad_own = dot_t(dqkv_s[...], w_s[own_columns, :])
    gain_own = jnp.sum(grad_own * x_s[:, own_columns].astype(F32) * rms(x), axis=0, keepdims=True)
    pack_ref[:, : 3 * inner] = t_dot(normed_ref[:, own_columns], dqkv_s[...]).astype(BF16)
    gain_s[0:8, :] = gain2_ref[...]
    gain_s[8:16, :] = gain3_ref[...]
    small = jnp.concatenate(
        [per_bucket, gain_own, gain_s[0:1, own_columns], gain_s[8:9, own_columns],
         jnp.zeros((BLOCK - 11, BLOCK), F32)], axis=0,
    )
    pack_ref[:, 4 * inner :] = small.astype(BF16)


VMEM = pl.BlockSpec(memory_space=pltpu.VMEM)


def call(kernel, name, out_shapes, scratch, args, flops):
    moved = sum(a.size * a.dtype.itemsize for a in args)
    return pl.pallas_call(
        kernel,
        name=name,
        out_shape=[jax.ShapeDtypeStruct(s, d) for s, d in out_shapes],
        in_specs=[pl.BlockSpec(memory_space=pltpu.SMEM)] + [VMEM] * (len(args) - 1),
        out_specs=[VMEM] * len(out_shapes),
        scratch_shapes=[pltpu.VMEM(s, d) for s, d in scratch],
        compiler_params=pltpu.CompilerParams(vmem_limit_bytes=56 * 1024 * 1024),
        cost_estimate=pl.CostEstimate(flops=flops, bytes_accessed=moved, transcendentals=0),
    )(*args)


def hop(x, axis, bits):
    size = lax.axis_size(axis)
    return lax.ppermute(x, axis, [(i, i ^ bits) for i in range(size)])


def gather_group(packs):
    across = [hop(pack, "fsdp", 2) for pack in packs]
    beside = [hop(pack, "fsdp", 1) for pack in packs]
    return [
        (pack, near, far, hop(far, "fsdp", 1)) for pack, near, far in zip(packs, beside, across)
    ]


def rep_stages():
    size = lax.axis_size("rep")
    stages, stride = [], 1
    while stride < size:
        ways = min(8, size // stride)
        stages.append((stride, ways))
        stride *= ways
    return stages


def sum_over_rep(pack):
    me = lax.axis_index("rep")
    part = pack
    stages = rep_stages()
    for stride, ways in stages:
        digit = (me // stride) % ways
        pieces = part.reshape((ways, part.shape[0] // ways) + part.shape[1:])
        total = lax.dynamic_index_in_dim(pieces, digit, 0, keepdims=False).astype(F32)
        arrived = [
            hop(lax.dynamic_index_in_dim(pieces, digit ^ k, 0, keepdims=False), "rep", k * stride)
            for k in range(1, ways)
        ]
        for piece in arrived:
            total = total + piece.astype(F32)
        part = total.astype(BF16)
    for stride, ways in reversed(stages):
        digit = (me // stride) % ways
        arrived = [part] + [hop(part, "rep", k * stride) for k in range(1, ways)]
        whole = jnp.zeros((ways,) + part.shape, BF16)
        for k, piece in enumerate(arrived):
            whole = lax.dynamic_update_index_in_dim(whole, piece, digit ^ k, 0)
        part = whole.reshape((ways * part.shape[0],) + part.shape[1:])
    return part.astype(F32)


def per_device(
    tokens,
    states,
    query_w,
    key_w,
    value_w,
    out_w,
    cross_query_w,
    cross_key_w,
    cross_value_w,
    cross_out_w,
    gate_w,
    up_w,
    down_w,
    self_gain,
    cross_gain,
    mlp_gain,
    bias_table,
    cotangent,
):
    seq_count, rows, width = tokens.shape
    enc = states.shape[1]
    own_rows, inner = query_w.shape
    hidden_units = gate_w.shape[1]
    length, enc_all = rows * GROUP, enc * GROUP
    f = lax.axis_index("fsdp")
    f_arg = f.astype(jnp.int32).reshape(1)

    gains = jnp.stack([self_gain, cross_gain, mlp_gain])
    aux = jnp.zeros((16, width), BF16)
    aux = lax.dynamic_update_slice(aux, gains, (0, f * own_rows))
    aux = lax.dynamic_update_slice(aux, bias_table.T, (8, f * bias_table.shape[0]))
    token_pack = jnp.concatenate([tokens[0], aux], axis=0)
    self_pack = jnp.concatenate([query_w, key_w, value_w], axis=1)
    out_pack = jnp.concatenate([out_w, cross_out_w], axis=0)
    cross_pack = jnp.concatenate([cross_query_w, cross_key_w, cross_value_w], axis=1)
    gate_pack = jnp.concatenate([gate_w, up_w], axis=1)
    down_pack = jnp.concatenate([down_w, cotangent[0]], axis=0)
    tok, self_ws, cross_ws, states_all, outs_ws, gates, downs = gather_group(
        [token_pack, self_pack, cross_pack, states[0], out_pack, gate_pack, down_pack]
    )

    normed_one, qkv, probs, mixed, aux_all = call(
        self_forward,
        "self_forward",
        [
            ((length, width), BF16),
            ((length, 3 * inner), BF16),
            ((H, length, length), BF16),
            ((length, inner), BF16),
            ((16, width), F32),
        ],
        [((length, width), BF16), ((width, 3 * inner), BF16), ((H, BLOCK, 2 * BLOCK), F32)],
        [f_arg, *tok, *self_ws],
        2 * 10**9,
    )
    hidden_one, normed_two, cross_q, cross_kv, cross_probs, cross_mixed, hidden_two, normed_three = call(
        cross_forward,
        "cross_forward",
        [
            ((length, width), F32),
            ((length, width), BF16),
            ((length, inner), BF16),
            ((enc_all, 2 * inner), BF16),
            ((H, length, enc_all), BF16),
            ((length, inner), BF16),
            ((length, width), F32),
            ((length, width), BF16),
        ],
        [
            ((length, width), BF16),
            ((width, 3 * inner), BF16),
            ((inner, width), BF16),
            ((inner, width), BF16),
            ((enc_all, width), BF16),
        ],
        [f_arg, *tok, mixed, aux_all, *cross_ws, *outs_ws, *states_all],
        2 * 10**9,
    )
    result, grad_hidden_two, ff_pack, mlp_gain_all = call(
        feed_forward,
        "feed_forward",
        [
            ((rows, width), BF16),
            ((length, width), F32),
            ((own_rows, 2 * hidden_units + down_w.size // own_rows), BF16),
            ((8, width), F32),
        ],
        [
            ((width, 2 * hidden_units), BF16),
            ((hidden_units, width), BF16),
            ((length, width), BF16),
            ((length, hidden_units), BF16),
            ((length, hidden_units), BF16),
            ((length, hidden_units), BF16),
        ],
        [f_arg, hidden_two, normed_three, aux_all, *gates, *downs],
        4 * 10**9,
    )
    grad_hidden_one, grad_states, cross_grads, cross_gain_all = call(
        cross_backward,
        "cross_backward",
        [
            ((length, width), F32),
            ((enc, width), F32),
            ((own_rows, 4 * inner), BF16),
            ((8, width), F32),
        ],
        [
            ((width, 3 * inner), BF16),
            ((inner, width), BF16),
            ((enc_all, width), BF16),
            ((length, width), BF16),
            ((length, inner), BF16),
            ((length, inner), BF16),
            ((enc_all, 2 * inner), BF16),
            ((length, enc_all), BF16),
        ],
        [
            f_arg, grad_hidden_two, hidden_one, normed_two, cross_q, cross_kv, cross_probs, cross_mixed,
            aux_all, *cross_ws, *outs_ws, *states_all,
        ],
        2 * 10**9,
    )
    grad_tokens, self_grads = call(
        self_backward,
        "self_backward",
        [((rows, width), F32), ((own_rows, 4 * inner + BLOCK), BF16)],
        [
            ((length, width), BF16),
            ((width, 3 * inner), BF16),
            ((inner, width), BF16),
            ((length, width), BF16),
            ((length, inner), BF16),
            ((length, 3 * inner), BF16),
            ((length, length), BF16),
            ((16, width), F32),
        ],
        [
            f_arg, grad_hidden_one, normed_one, qkv, probs, mixed, aux_all, cross_gain_all, mlp_gain_all,
            *tok, *self_ws, *outs_ws,
        ],
        3 * 10**9,
    )

    ff_sum = sum_over_rep(ff_pack)
    cross_sum = sum_over_rep(cross_grads)
    self_sum = sum_over_rep(self_grads)

    def down_grad():
        return jnp.concatenate(
            [ff_sum[:, 2 * hidden_units + i * width :][:, :width] for i in range(down_w.shape[0] // own_rows)]
        )

    def out_grad(total):
        return jnp.concatenate(
            [total[:, 3 * inner + i * own_rows :][:, :own_rows] for i in range(inner // own_rows)]
        )

    small = self_sum[:, 4 * inner :]
    table = lax.dynamic_slice(small[:H, :], (0, f * bias_table.shape[0]), (H, bias_table.shape[0]))
    return (
        result[None],
        grad_tokens[None],
        grad_states[None],
        self_sum[:, :inner],
        self_sum[:, inner : 2 * inner],
        self_sum[:, 2 * inner : 3 * inner],
        out_grad(self_sum),
        cross_sum[:, :inner],
        cross_sum[:, inner : 2 * inner],
        cross_sum[:, 2 * inner : 3 * inner],
        out_grad(cross_sum),
        ff_sum[:, :hidden_units],
        ff_sum[:, hidden_units : 2 * hidden_units],
        down_grad(),
        small[8],
        small[9],
        small[10],
        table.T,
    )


def solution(mesh):
    whole = P("rep", "fsdp", None)
    rows, columns, vector = P("fsdp", None), P(None, "fsdp"), P("fsdp")
    weights = (rows, rows, rows, columns, rows, rows, rows, columns, rows, rows, rows)
    small = (vector, vector, vector, rows)
    return jax.shard_map(
        per_device,
        mesh=mesh,
        in_specs=(whole, whole) + weights + small + (whole,),
        out_specs=(whole, whole, whole) + weights + small,
        check_vma=False,
    )
```

```python
import functools
import math

import jax
import jax.numpy as jnp
from jax import lax
from jax.experimental import pallas as pl
from jax.experimental.pallas import tpu as pltpu
from jax.sharding import PartitionSpec as P

H = 6
DH = 64
PAIRS = H // 2
BUCKETS = 32
MAXDIST = 128
EPSILON = 1e-06
MASKED = -1000000000.0
BLOCK = 128
HALF = 256
GROUP = 4
PIECES = 8
VMEM_BYTES = 32 * 1024 * 1024
HIGHEST = lax.Precision.HIGHEST
F32 = jnp.float32
BF16 = jnp.bfloat16


def dot(a, b):
    return jnp.dot(a, b, preferred_element_type=F32)


def dot_t(a, b):
    return lax.dot_general(a, b, (((1,), (1,)), ((), ())), preferred_element_type=F32)


def t_dot(a, b):
    return lax.dot_general(a, b, (((0,), (0,)), ((), ())), preferred_element_type=F32)


def own(f, size):
    return pl.ds(pl.multiple_of(f * size, size), size)


def place_rows(dst, pieces, f, first, size):
    for k, piece in enumerate(pieces):
        dst[own(f ^ k, size), :] = piece[first : first + size, :].astype(dst.dtype)


def place_mine(ref, f):
    return jnp.concatenate([ref[own(b, BLOCK), :] for b in my_blocks(f)], axis=0)


def my_blocks(f):
    a = (f ^ (f >> 1)) & 1
    return a, 3 - a


def split_pieces(pieces, f, half):
    for k, piece in enumerate(pieces[:2]):
        rows = piece.shape[0] // 2
        for h in range(2):
            yield f ^ k, h, piece, h * rows, rows
    for i, piece in enumerate(pieces[2:]):
        yield f ^ (2 + i // 2), half ^ (i % 2), piece, 0, piece.shape[0]


def place_split_rows(dst, pieces, f, half):
    for owner, h, piece, first, rows in split_pieces(pieces, f, half):
        dst[own(2 * owner + h, rows), :] = piece[first : first + rows, :]


def place_split_columns(dst, pieces, f, half):
    for owner, h, piece, first, rows in split_pieces(pieces, f, half):
        dst[own(h, rows), own(owner, piece.shape[1])] = piece[first : first + rows, :]


def bucket_of(distance):
    exact_span = BUCKETS // 2
    bucket = jnp.minimum(distance, exact_span)
    for power in range(1, exact_span):
        threshold = math.ceil(exact_span * (MAXDIST / exact_span) ** (power / exact_span))
        bucket = bucket + (distance >= threshold).astype(jnp.int32)
    return bucket


def offset_onehot(rows, axis):
    shape = (rows, 4 * BLOCK) if axis == 1 else (4 * BLOCK, rows)
    m = lax.broadcasted_iota(jnp.int32, shape, axis)
    n = jnp.where(m < 2 * BLOCK, BLOCK - m, 5 * BLOCK - m)
    bucket = bucket_of(jnp.maximum(n, 0))
    return (bucket == lax.broadcasted_iota(jnp.int32, shape, 1 - axis)).astype(F32)


def rms(v):
    return lax.rsqrt(jnp.mean(v * v, axis=-1, keepdims=True) + EPSILON)


def head_lanes(rows):
    lane = lax.broadcasted_iota(jnp.int32, (rows, 2 * DH), 1)
    return lane < DH


def only_head(pair, hd):
    low = head_lanes(pair.shape[0])
    zero = jnp.zeros_like(pair)
    return jnp.where(low, pair, zero) if hd == 0 else jnp.where(low, zero, pair)


def softmax(s):
    lifted = jnp.exp(s - jnp.max(s, axis=-1, keepdims=True))
    return lifted * (1.0 / jnp.sum(lifted, axis=-1, keepdims=True))


def norm_back(v, gain, q):
    r = rms(v)
    u = q * gain
    vr = v * r
    return r * (u - vr * jnp.mean(vr * u, axis=-1, keepdims=True)), q * vr


def stack_heads(pair):
    low = head_lanes(pair.shape[0])
    zero = jnp.zeros_like(pair)
    return jnp.concatenate([jnp.where(low, pair, zero), jnp.where(low, zero, pair)], axis=0)


def unstack_heads(stacked):
    rows = stacked.shape[0] // 2
    return jnp.where(head_lanes(rows), stacked[:rows, :], stacked[rows:, :])


def emit(keep_ref, send_ref, chip_s, first, f, order):
    core = f & 1
    rows = keep_ref.shape[0]
    piece = rows // PIECES
    columns = chip_s.shape[1]
    for q in range(PIECES):
        to = pl.ds(pl.multiple_of((q ^ order) * piece, piece), piece)
        for ref, which in ((keep_ref, core), (send_ref, 1 - core)):
            at = pl.ds(pl.multiple_of(which * rows + q * piece, piece), piece)
            ref[to, first : first + columns] = chip_s[at, :]


def pack_first(tokens_ref, q_ref, k_ref, v_ref, pack_ref, pack_s, sems):
    width, inner = tokens_ref.shape[1], q_ref.shape[1]
    copies, first = [], 0
    for i, ref in enumerate((tokens_ref, q_ref, k_ref, v_ref)):
        copies.append(pltpu.make_async_copy(ref, pack_s.at[:, first : first + ref.shape[1]], sems.at[i]))
        copies[-1].start()
        first += ref.shape[1]
    for c in copies:
        c.wait()
    out = pltpu.make_async_copy(pack_s, pack_ref, sems.at[4])
    out.start()
    out.wait()


def run_copies(pairs, sems):
    copies = [pltpu.make_async_copy(a, b, sems.at[i]) for i, (a, b) in enumerate(pairs)]
    for c in copies:
        c.start()
    for c in copies:
        c.wait()


def half_of(ref, half):
    rows = ref.shape[0] // 2
    return ref.at[pl.ds(pl.multiple_of(half * rows, rows), rows), :]


def pack_second(
    ids_ref, cq_ref, ck_ref, cv_ref, out_ref, co_ref, cross_ref, outs_ref, cross_half, out_half,
    cross_s, outs_s, in_sems, out_sems,
):
    half, inner = ids_ref[2], cq_ref.shape[1]
    run_copies(
        [(ref, cross_s.at[:, i * inner : (i + 1) * inner]) for i, ref in enumerate((cq_ref, ck_ref, cv_ref))]
        + [(ref, outs_s.at[i * inner : (i + 1) * inner, :]) for i, ref in enumerate((out_ref, co_ref))],
        in_sems,
    )
    run_copies(
        [(half_of(cross_s, half), cross_half), (half_of(outs_s, half), out_half), (cross_s, cross_ref), (outs_s, outs_ref)],
        out_sems,
    )


def pack_third(ids_ref, gate_ref, up_ref, down_ref, gu_ref, gu_half, down_half, gu_s, down_s, in_sems, out_sems):
    half, units = ids_ref[2], gate_ref.shape[1]
    run_copies([(gate_ref, gu_s.at[:, :units]), (up_ref, gu_s.at[:, units:]), (down_ref, down_s)], in_sems)
    run_copies([(half_of(gu_s, half), gu_half), (half_of(down_s, half), down_half), (gu_s, gu_ref)], out_sems)


def self_forward(
    ids_ref, w0, w1, w2, w3, a0, a1, a2, a3,
    x_ref, normed_ref, q_ref, kv_ref, pa_ref, pb_ref, mixed_ref, aux_ref,
    w_s, bias_a, bias_b,
):
    f = ids_ref[0]
    length, width = x_ref.shape
    inner = H * DH
    for k, piece in enumerate((w0, w1, w2, w3)):
        x_ref[own(f ^ k, w0.shape[0]), :] = piece[:, :width]
        w_s[own(f ^ k, w0.shape[0]), :] = piece[:, width:]
    aux = sum(a[...].astype(F32) for a in (a0, a1, a2, a3))
    aux_ref[...] = aux
    for hb in range(length // HALF):
        at = slice(hb * HALF, (hb + 1) * HALF)
        x = x_ref[at, :].astype(F32)
        normed = (x * rms(x) * aux[0:1, :]).astype(BF16)
        normed_ref[at, :] = normed
        kv_ref[at, :] = dot(normed, w_s[:, inner:]).astype(BF16)
    q_ref[...] = dot(place_mine(normed_ref, f), w_s[:, :inner]).astype(BF16)
    per_offset = jnp.dot(
        aux[8:16, 0:BLOCK], offset_onehot(BLOCK, 1), precision=HIGHEST, preferred_element_type=F32
    )
    first, second = my_blocks(f)
    row = lax.broadcasted_iota(jnp.int32, (BLOCK, 2 * BLOCK), 0)
    col = lax.broadcasted_iota(jnp.int32, (BLOCK, 2 * BLOCK), 1)
    lane = lax.broadcasted_iota(jnp.int32, (BLOCK, length), 1)
    is_far = lane < (second - 1) * BLOCK
    bias_a[:, :, 2 * BLOCK :] = jnp.full((PAIRS, 2 * BLOCK, BLOCK), MASKED, F32)
    for h in range(H):
        at = slice((h % 2) * BLOCK, (h % 2 + 1) * BLOCK)
        spread = jnp.broadcast_to(per_offset[h : h + 1, :], (BLOCK, 4 * BLOCK))
        skewed = pltpu.roll(spread, 0, 1, stride=1, stride_axis=0)[:, : 2 * BLOCK]
        band = jnp.where(col - BLOCK > row, MASKED, skewed)
        bias_a[h // 2, at, pl.ds(pl.multiple_of(first * BLOCK, BLOCK), 2 * BLOCK)] = band
        bias_b[h // 2, at, :] = jnp.where(is_far, per_offset[h : h + 1, 0:1], MASKED)
        bias_b[h // 2, at, pl.ds(pl.multiple_of((second - 1) * BLOCK, BLOCK), 2 * BLOCK)] = band
    for p in range(PAIRS):
        lanes = slice(p * BLOCK, (p + 1) * BLOCK)
        k2 = kv_ref[:, lanes]
        v2 = kv_ref[:, inner + p * BLOCK : inner + (p + 1) * BLOCK]
        for slot in range(2):
            at = slice(slot * BLOCK, (slot + 1) * BLOCK)
            bias = bias_a[p, :, BLOCK:] if slot == 0 else bias_b[p]
            seen = bias.shape[1]
            s = dot_t(stack_heads(q_ref[at, lanes]), k2[:seen, :]) + bias
            probs = softmax(s).astype(BF16)
            (pa_ref, pb_ref)[slot][p] = probs
            mixed_ref[at, lanes] = unstack_heads(dot(probs, v2[:seen, :])).astype(BF16)


def cross_forward(
    ids_ref, x_ref, mixed_ref, aux_ref,
    w0, w1, w2, w3, w4, w5, o0, o1, o2, o3, o4, o5, s0, s1, s2, s3,
    h1_ref, n2_ref, cq_ref, ckv_ref, probs_ref, cmixed_ref, h2_ref, n3_ref,
    w_s, outs_s, states_s,
):
    f = ids_ref[0]
    inner = H * DH
    half = ids_ref[2]
    place_split_rows(w_s, (w0, w1, w2, w3, w4, w5), f, half)
    place_split_columns(outs_s, (o0, o1, o2, o3, o4, o5), f, half)
    place_rows(states_s, (s0, s1, s2, s3), f, 0, s0.shape[0])
    hidden = place_mine(x_ref, f).astype(F32) + dot(mixed_ref[...], outs_s[:inner, :])
    h1_ref[...] = hidden
    normed = (hidden * rms(hidden) * aux_ref[1:2, :]).astype(BF16)
    n2_ref[...] = normed
    cq_ref[...] = dot(normed, w_s[:, :inner]).astype(BF16)
    ckv_ref[...] = dot(states_s[...], w_s[:, inner:]).astype(BF16)
    for p in range(PAIRS):
        lanes = slice(p * BLOCK, (p + 1) * BLOCK)
        v2 = ckv_ref[:, inner + p * BLOCK : inner + (p + 1) * BLOCK]
        probs = softmax(dot_t(stack_heads(cq_ref[:, lanes]), ckv_ref[:, lanes])).astype(BF16)
        probs_ref[p] = probs
        cmixed_ref[:, lanes] = unstack_heads(dot(probs, v2)).astype(BF16)
    hidden = h1_ref[...] + dot(cmixed_ref[...], outs_s[inner:, :])
    h2_ref[...] = hidden
    n3_ref[...] = (hidden * rms(hidden) * aux_ref[2:3, :]).astype(BF16)


def feed_forward(
    ids_ref, h2_ref, n3_ref, aux_ref,
    g0, g1, g2, g3, g4, g5, d0, d1, d2, d3, d4, d5, c0, c1, c2, c3,
    result_ref, grad_h2_ref, keep_ref, send_ref, gain_ref,
    gu_s, down_s, cot_s, cot_mine, units_s, gate_s, up_s, chip_s, down_chip_s,
):
    f, order = ids_ref[0], ids_ref[1]
    chip = f >> 1
    mine_rows, width = h2_ref.shape
    rows = cot_s.shape[0] // GROUP
    hidden_units = down_s.shape[0]
    own_units = hidden_units // GROUP
    half = ids_ref[2]
    place_split_rows(gu_s, (g0, g1, g2, g3, g4, g5), f, half)
    place_split_rows(down_s, (d0, d1, d2, d3, d4, d5), f, half)
    place_rows(cot_s, (c0, c1, c2, c3), f, 0, rows)
    cot_mine[...] = place_mine(cot_s, f)
    grad_normed = jnp.zeros((mine_rows, width), F32)
    chunk = 256
    for c in range(hidden_units // chunk):
        gate_at, up_at = slice(c * chunk, (c + 1) * chunk), slice(hidden_units + c * chunk, hidden_units + (c + 1) * chunk)
        gate, up = dot(n3_ref[...], gu_s[:, gate_at]), dot(n3_ref[...], gu_s[:, up_at])
        grad_units = dot_t(cot_mine[...], down_s[gate_at, :])
        square = gate * gate
        tanh = jnp.tanh(0.7978845608028654 * (gate + 0.044715 * square * gate))
        half_gate = 0.5 * gate
        gelu = half_gate + half_gate * tanh
        slope = 0.5 + 0.5 * tanh + half_gate * (1.0 - tanh * tanh) * (
            0.7978845608028654 + (3 * 0.044715 * 0.7978845608028654) * square
        )
        units_s[:, gate_at] = (gelu * up).astype(BF16)
        grad_gate = (grad_units * up * slope).astype(BF16)
        grad_up = (grad_units * gelu).astype(BF16)
        gate_s[:, gate_at] = grad_gate
        up_s[:, gate_at] = grad_up
        grad_normed = grad_normed + dot_t(grad_gate, gu_s[:, gate_at]) + dot_t(grad_up, gu_s[:, up_at])
    piece, gain_part = norm_back(h2_ref[...], aux_ref[2:3, :], grad_normed)
    grad_h2_ref[...] = cot_mine[...].astype(F32) + piece
    gain_ref[...] = jnp.broadcast_to(jnp.sum(gain_part, axis=0, keepdims=True), gain_ref.shape)
    mine = own(chip, rows)
    result_ref[...] = (h2_ref[mine, :] + dot(units_s[mine, :], down_s[...])).astype(BF16)
    chip_rows = 2 * g0.shape[0]
    normed_chip = n3_ref[:, own(chip, chip_rows)]
    chip_s[:, :hidden_units] = t_dot(normed_chip, gate_s[...]).astype(BF16)
    chip_s[:, hidden_units:] = t_dot(normed_chip, up_s[...]).astype(BF16)
    emit(keep_ref, send_ref, chip_s, 0, f, order)
    grad_down = t_dot(units_s[:, own(chip, 2 * own_units)], cot_mine[...]).astype(BF16)
    parts = own_units // g0.shape[0]
    for which in range(2):
        for part in range(parts):
            at = slice((which * parts + part) * g0.shape[0], (which * parts + part + 1) * g0.shape[0])
            down_chip_s[which * g0.shape[0] : (which + 1) * g0.shape[0], part * width : (part + 1) * width] = grad_down[at, :]
    emit(keep_ref, send_ref, down_chip_s, 2 * hidden_units, f, order)


def put_columns(chip_s, first, grad, own_rows):
    columns = grad.shape[1] // 2
    for which in range(2):
        for part in range(grad.shape[0] // own_rows):
            chip_s[which * own_rows : (which + 1) * own_rows, first + part * columns : first + (part + 1) * columns] = (
                grad[part * own_rows : (part + 1) * own_rows, which * columns : (which + 1) * columns]
            )


def cross_backward(
    ids_ref, grad_h2_ref, h1_ref, n2_ref, cq_ref, ckv_ref, probs_ref, cmixed_ref, mixed_ref, aux_ref,
    w0, w1, w2, w3, w4, w5, o0, o1, o2, o3, o4, o5, s0, s1, s2, s3,
    grad_h1_ref, mix_ref, states_keep, states_send, keep_ref, send_ref, gain_ref,
    w_s, outs_s, states_s, low_s, dq_s, dkv_s, chip_s, states_chip,
):
    f, order = ids_ref[0], ids_ref[1]
    chip, core = f >> 1, f & 1
    inner = H * DH
    own_rows = w0.shape[0]
    chip_columns = own(chip, 2 * own_rows)
    half = ids_ref[2]
    place_split_rows(w_s, (w0, w1, w2, w3, w4, w5), f, half)
    place_split_columns(outs_s, (o0, o1, o2, o3, o4, o5), f, half)
    place_rows(states_s, (s0, s1, s2, s3), f, 0, s0.shape[0])
    low = grad_h2_ref[...].astype(BF16)
    low_s[...] = low
    grad_mixed = dot_t(low, outs_s[inner:, :]).astype(BF16)
    put_columns(chip_s, 3 * inner, t_dot(cmixed_ref[...], low_s[:, chip_columns]).astype(BF16), own_rows)
    for p in range(PAIRS):
        lanes = slice(p * BLOCK, (p + 1) * BLOCK)
        v_lanes = slice(inner + p * BLOCK, inner + (p + 1) * BLOCK)
        stacked = stack_heads(grad_mixed[:, lanes])
        probs = probs_ref[p].astype(F32)
        weighted = probs * dot_t(stacked, ckv_ref[:, v_lanes])
        ds = (weighted - probs * jnp.sum(weighted, axis=-1, keepdims=True)).astype(BF16)
        dq_s[:, lanes] = unstack_heads(dot(ds, ckv_ref[:, lanes])).astype(BF16)
        dkv_s[:, lanes] = t_dot(ds, stack_heads(cq_ref[:, lanes])).astype(BF16)
        dkv_s[:, v_lanes] = t_dot(probs_ref[p], stacked).astype(BF16)
    grad_normed = dot_t(dq_s[...], w_s[:, :inner])
    piece, gain_part = norm_back(h1_ref[...], aux_ref[1:2, :], grad_normed)
    grad_h1 = grad_h2_ref[...] + piece
    grad_h1_ref[...] = grad_h1
    gain_ref[...] = jnp.broadcast_to(jnp.sum(gain_part, axis=0, keepdims=True), gain_ref.shape)
    low = grad_h1.astype(BF16)
    low_s[...] = low
    mix_ref[...] = dot_t(low, outs_s[:inner, :]).astype(BF16)
    put_columns(chip_s, 4 * inner, t_dot(mixed_ref[...], low_s[:, chip_columns]).astype(BF16), own_rows)
    chip_s[:, :inner] = t_dot(n2_ref[:, chip_columns], dq_s[...]).astype(BF16)
    chip_s[:, inner : 3 * inner] = t_dot(states_s[:, chip_columns], dkv_s[...]).astype(BF16)
    emit(keep_ref, send_ref, chip_s, 0, f, order)
    enc = s0.shape[0]
    states_chip[...] = dot_t(dkv_s[own(chip, 2 * enc), :], w_s[:, inner:])
    states_keep[...] = states_chip[own(core, enc), :]
    states_send[...] = states_chip[own(1 - core, enc), :]


def self_backward(
    ids_ref, grad_h1_ref, mix_ref, x_ref, normed_ref, q_ref, kv_ref, pa_ref, pb_ref, aux_ref, gain2_ref, gain3_ref,
    w0, w1, w2, w3,
    tokens_keep, tokens_send, keep_ref, send_ref,
    w_s, dq_s, dkv_s, ds_a, ds_b, chip_s, small_s, gain_s, table_s,
):
    f, order = ids_ref[0], ids_ref[1]
    chip, core = f >> 1, f & 1
    length, width = x_ref.shape
    rows = length // GROUP
    inner = H * DH
    own_rows = w0.shape[0]
    chip_columns = own(chip, 2 * own_rows)
    for k, piece in enumerate((w0, w1, w2, w3)):
        w_s[own(f ^ k, own_rows), :] = piece[:, width:]
    first, second = my_blocks(f)
    row = lax.broadcasted_iota(jnp.int32, (2 * BLOCK, 4 * BLOCK), 0)
    ds_a[:, 0:BLOCK] = jnp.zeros((2 * BLOCK, BLOCK), F32)
    offset_sums, far_sums = [], []
    for p in range(PAIRS):
        lanes = slice(p * BLOCK, (p + 1) * BLOCK)
        v_lanes = slice(inner + p * BLOCK, inner + (p + 1) * BLOCK)
        k2, v2 = kv_ref[:, lanes], kv_ref[:, v_lanes]
        dk, dv = [], []
        for slot in range(2):
            at = slice(slot * BLOCK, (slot + 1) * BLOCK)
            probs_low = (pa_ref, pb_ref)[slot][p]
            seen = probs_low.shape[1]
            stacked = stack_heads(mix_ref[at, lanes])
            probs = probs_low.astype(F32)
            weighted = probs * dot_t(stacked, v2[:seen, :])
            ds = weighted - probs * jnp.sum(weighted, axis=-1, keepdims=True)
            if slot == 0:
                ds_a[:, BLOCK:] = ds
            else:
                ds_b[...] = ds
            low = ds.astype(BF16)
            dq_s[at, lanes] = unstack_heads(dot(low, k2[:seen, :])).astype(BF16)
            dk.append(t_dot(low, stack_heads(q_ref[at, lanes])))
            dv.append(t_dot(probs_low, stacked))
        for total, to in ((dk, lanes), (dv, v_lanes)):
            seen = total[0].shape[0]
            dkv_s[:seen, to] = (total[0] + total[1][:seen, :]).astype(BF16)
            dkv_s[seen:, to] = total[1][seen:, :].astype(BF16)
        band_b = ds_b[:, pl.ds(pl.multiple_of((second - 1) * BLOCK, BLOCK), 2 * BLOCK)]
        band_a = ds_a[:, pl.ds(pl.multiple_of(first * BLOCK, BLOCK), 2 * BLOCK)]
        far = jnp.sum(ds_b[...], axis=1, keepdims=True) - jnp.sum(band_b, axis=1, keepdims=True)
        skew = jnp.concatenate([band_a + band_b, jnp.zeros((2 * BLOCK, 2 * BLOCK), F32)], axis=1)
        for bit in range(BLOCK.bit_length() - 1):
            moved = pltpu.roll(skew, 4 * BLOCK - (1 << bit), 1)
            skew = jnp.where((row & (1 << bit)) != 0, moved, skew)
        for hd in range(2):
            at = slice(hd * BLOCK, (hd + 1) * BLOCK)
            offset_sums.append(jnp.sum(skew[at, :], axis=0, keepdims=True))
            far_sums.append(jnp.sum(far[at, :], axis=0, keepdims=True))
    per_offset = jnp.concatenate(offset_sums + [jnp.zeros((BLOCK - H, 4 * BLOCK), F32)], axis=0)
    far_all = jnp.concatenate(far_sums + [jnp.zeros((BLOCK - H, 1), F32)], axis=0)
    per_offset = per_offset + jnp.where(
        lax.broadcasted_iota(jnp.int32, (BLOCK, 4 * BLOCK), 1) == 0, far_all, 0.0
    )
    table_s[...] = lax.dot_general(
        offset_onehot(BLOCK, 1), per_offset, (((1,), (1,)), ((), ())),
        precision=HIGHEST, preferred_element_type=F32,
    )

    gain = aux_ref[0:1, :]
    mine, block = own(chip, rows), own(f, rows)
    others = own(f ^ 1, rows)
    grad_normed = dot_t(dq_s[mine, :], w_s[:, :inner]) + dot_t(dkv_s[block, :], w_s[:, inner:])
    piece, _ = norm_back(x_ref[block, :].astype(F32), gain, grad_normed)
    tokens_keep[...] = grad_h1_ref[mine, :] + piece
    piece, _ = norm_back(x_ref[others, :].astype(F32), gain, dot_t(dkv_s[others, :], w_s[:, inner:]))
    tokens_send[...] = piece
    chip_w = w_s[chip_columns, :]
    gain_sum = jnp.zeros((1, 2 * own_rows), F32)
    for hb in range(length // HALF):
        at = slice(hb * HALF, (hb + 1) * HALF)
        scaled = x_ref[at, chip_columns].astype(F32) * rms(x_ref[at, :].astype(F32))
        gain_sum = gain_sum + jnp.sum(dot_t(dkv_s[at, :], chip_w[:, inner:]) * scaled, axis=0, keepdims=True)
    grad_q = dot_t(dq_s[...], chip_w[:, :inner])
    for slot, b in enumerate((first, second)):
        scaled = x_ref[own(b, BLOCK), chip_columns].astype(F32) * rms(x_ref[own(b, BLOCK), :].astype(F32))
        gain_sum = gain_sum + jnp.sum(grad_q[slot * BLOCK : (slot + 1) * BLOCK, :] * scaled, axis=0, keepdims=True)
    normed_mine = jnp.concatenate([normed_ref[own(b, BLOCK), chip_columns] for b in (first, second)], axis=0)
    chip_s[:, :inner] = t_dot(normed_mine, dq_s[...]).astype(BF16)
    chip_s[:, inner:] = t_dot(normed_ref[:, chip_columns], dkv_s[...]).astype(BF16)
    emit(keep_ref, send_ref, chip_s, 0, f, order)
    gain_s[0:8, :] = gain2_ref[...]
    gain_s[8:16, :] = gain3_ref[...]
    buckets = BUCKETS // GROUP
    for which in range(2):
        owner = 2 * chip + which
        small = jnp.concatenate(
            [
                table_s[own(owner, buckets), :],
                gain_sum[:, which * own_rows : (which + 1) * own_rows],
                gain_s[0:1, own(owner, own_rows)],
                gain_s[8:9, own(owner, own_rows)],
                jnp.zeros((own_rows - buckets - 3, BLOCK), F32),
            ],
            axis=0,
        )
        small_s[which * own_rows : (which + 1) * own_rows, :] = small.astype(BF16)
    emit(keep_ref, send_ref, small_s, 3 * inner, f, order)


def fold(keep_ref, arrived_ref, *out_refs):
    total = (keep_ref[...].astype(F32) + arrived_ref[...].astype(F32)).astype(BF16)
    rows = total.shape[0] // len(out_refs)
    for i, ref in enumerate(out_refs):
        ref[...] = total[i * rows : (i + 1) * rows, :]


def pieces_of(ids_ref, halves):
    order = ids_ref[1]
    for i, half in enumerate(halves):
        piece = half.shape[0] * len(halves) // PIECES
        here = PIECES // len(halves)
        for j in range(here):
            q = (i * here + j) ^ order
            yield q * piece, piece, half[j * piece : (j + 1) * piece, :].astype(F32)


def unpack_feed(ids_ref, low_ref, high_ref, gate_ref, up_ref, down_ref):
    units, width, own_rows = gate_ref.shape[1], down_ref.shape[1], gate_ref.shape[0]
    for at, size, rows in pieces_of(ids_ref, (low_ref, high_ref)):
        to = pl.ds(pl.multiple_of(at, size), size)
        gate_ref[to, :] = rows[:, :units]
        up_ref[to, :] = rows[:, units : 2 * units]
        for part in range(down_ref.shape[0] // own_rows):
            first = 2 * units + part * width
            down_ref[pl.ds(pl.multiple_of(part * own_rows + at, size), size), :] = rows[:, first : first + width]


def unpack_cross(ids_ref, low_ref, high_ref, cq_ref, ck_ref, cv_ref, co_ref, out_ref):
    own_rows, inner = cq_ref.shape
    for at, size, rows in pieces_of(ids_ref, (low_ref, high_ref)):
        to = pl.ds(pl.multiple_of(at, size), size)
        for i, ref in enumerate((cq_ref, ck_ref, cv_ref)):
            ref[to, :] = rows[:, i * inner : (i + 1) * inner]
        for i, ref in enumerate((co_ref, out_ref)):
            columns = ref.shape[1]
            for part in range(inner // own_rows):
                first = (3 + i) * inner + part * columns
                ref[pl.ds(pl.multiple_of(part * own_rows + at, size), size), :] = rows[:, first : first + columns]


def unpack_self(ids_ref, low_ref, high_ref, q_ref, k_ref, v_ref, g1_ref, g2_ref, g3_ref, table_ref, small_s):
    inner = q_ref.shape[1]
    for at, size, rows in pieces_of(ids_ref, (low_ref, high_ref)):
        to = pl.ds(pl.multiple_of(at, size), size)
        for i, ref in enumerate((q_ref, k_ref, v_ref)):
            ref[to, :] = rows[:, i * inner : (i + 1) * inner]
        small_s[to, :] = rows[:, 3 * inner :]
    buckets, heads = table_ref.shape
    table_ref[...] = small_s[0:buckets, 0:heads]
    for i, ref in enumerate((g1_ref, g2_ref, g3_ref)):
        ref[...] = small_s[buckets + i : buckets + i + 1, :]


VMEM = pl.BlockSpec(memory_space=pltpu.VMEM)
SMEM = pl.BlockSpec(memory_space=pltpu.SMEM)


def call(kernel, name, out_shapes, scratch, args, flops, with_ids=True, place=VMEM):
    moved = sum(a.size * a.dtype.itemsize for a in args)
    return pl.pallas_call(
        kernel,
        name=name,
        out_shape=[jax.ShapeDtypeStruct(s, d) for s, d in out_shapes],
        in_specs=([SMEM] if with_ids else []) + [place] * (len(args) - with_ids),
        out_specs=[place] * len(out_shapes),
        scratch_shapes=[pltpu.VMEM(*s) if isinstance(s, tuple) else s for s in scratch],
        compiler_params=pltpu.CompilerParams(vmem_limit_bytes=VMEM_BYTES if place is VMEM else 56 * 1024 * 1024),
        cost_estimate=pl.CostEstimate(flops=flops, bytes_accessed=moved, transcendentals=0),
    )(*args)


def hop(x, axis, bits):
    size = lax.axis_size(axis)
    return lax.ppermute(x, axis, [(i, i ^ bits) for i in range(size)])


def all_after(arrays, earlier):
    return lax.optimization_barrier((tuple(arrays), tuple(earlier)))[0]


def beside(pack, far):
    return pack, hop(pack, "fsdp", 1), far, hop(far, "fsdp", 1)


def beside_split(pack, far, far_other):
    return pack, hop(pack, "fsdp", 1), far, far_other, hop(far, "fsdp", 1), hop(far_other, "fsdp", 1)


class Sum:
    def __init__(self, name, keep, send, steps):
        self.name, self.keep, self.steps, self.at = name, keep, steps, 0
        self.arrived = hop(send, "fsdp", 1)

    def fold(self, earlier):
        keep, arrived = all_after((self.keep, self.arrived), earlier)
        halving = self.at < len(self.steps) and (1 << self.at) < PIECES
        shape = (keep.shape[0] // 2, keep.shape[1]) if halving else keep.shape
        out = call(fold, f"{self.name}_fold", [(shape, BF16)] * (1 + halving), [], [keep, arrived], 0, False)
        self.keep = out[0]
        if self.at < len(self.steps):
            self.arrived = hop(out[-1], "rep", self.steps[self.at])
        else:
            self.back = [i for i in range(len(self.steps)) if (1 << i) < PIECES]
            self.arrived = hop(self.keep, "rep", self.steps[self.back[-1]])
        self.at += 1
        return self.keep

    def widen(self, earlier):
        keep, arrived = all_after((self.keep, self.arrived), earlier)
        self.back.pop()
        self.keep = jnp.concatenate((keep, arrived))
        self.arrived = hop(self.keep, "rep", self.steps[self.back[-1]])
        return self.keep

    def halves(self, earlier):
        return all_after((self.keep, self.arrived), earlier)


def per_device(
    tokens,
    states,
    query_w,
    key_w,
    value_w,
    out_w,
    cross_query_w,
    cross_key_w,
    cross_value_w,
    cross_out_w,
    gate_w,
    up_w,
    down_w,
    self_gain,
    cross_gain,
    mlp_gain,
    bias_table,
    cotangent,
):
    seq_count, rows, width = tokens.shape
    enc = states.shape[1]
    own_rows, inner = query_w.shape
    hidden_units = gate_w.shape[1]
    length, enc_all, mine = rows * GROUP, enc * GROUP, 2 * BLOCK
    f = lax.axis_index("fsdp").astype(jnp.int32)
    replica = lax.axis_index("rep").astype(jnp.int32)
    steps = [1 << i for i in range((lax.axis_size("rep") - 1).bit_length())]
    order = ((replica & 1) << 2) | (replica & 2) | ((replica >> 2) & 1)
    half = replica & 1
    ids = jnp.stack([f, order, half])

    hbm = pl.BlockSpec(memory_space=pl.ANY)
    (first_pack,) = call(
        pack_first,
        "pack_first",
        [((rows, width + 3 * inner), BF16)],
        [((rows, width + 3 * inner), BF16), pltpu.SemaphoreType.DMA((5,))],
        [tokens[0], query_w, key_w, value_w],
        0,
        False,
        hbm,
    )
    aux = jnp.zeros((16, width), BF16)
    aux = lax.dynamic_update_slice(aux, jnp.stack([self_gain, cross_gain, mlp_gain]), (0, f * own_rows))
    aux = lax.dynamic_update_slice(aux, bias_table.T, (8, f * bias_table.shape[0]))
    (aux,) = all_after((aux,), (first_pack,))
    (second_ids,) = all_after((ids,), (aux,))
    cross_pack, out_pack, cross_half, out_half = call(
        pack_second,
        "pack_second",
        [
            ((own_rows, 3 * inner), BF16),
            ((2 * inner, own_rows), BF16),
            ((own_rows // 2, 3 * inner), BF16),
            ((inner, own_rows), BF16),
        ],
        [
            ((own_rows, 3 * inner), BF16),
            ((2 * inner, own_rows), BF16),
            pltpu.SemaphoreType.DMA((5,)),
            pltpu.SemaphoreType.DMA((4,)),
        ],
        [second_ids, cross_query_w, cross_key_w, cross_value_w, out_w, cross_out_w],
        0,
        place=hbm,
    )
    third_ids, states_own = all_after((ids, states[0]), (cross_pack,))
    gate_pack, gate_half, down_half = call(
        pack_third,
        "pack_third",
        [
            ((own_rows, 2 * hidden_units), BF16),
            ((own_rows // 2, 2 * hidden_units), BF16),
            ((down_w.shape[0] // 2, width), BF16),
        ],
        [
            ((own_rows, 2 * hidden_units), BF16),
            (down_w.shape, BF16),
            pltpu.SemaphoreType.DMA((3,)),
            pltpu.SemaphoreType.DMA((3,)),
        ],
        [third_ids, gate_w, up_w, down_w],
        0,
        place=hbm,
    )
    (cot_own,) = all_after((cotangent[0],), (gate_pack,))
    first_far = hop(first_pack, "fsdp", 2)
    aux_far = hop(aux, "fsdp", 2)
    out_far, cross_far, states_far = (hop(a, "fsdp", 2) for a in (out_half, cross_half, states_own))
    gate_far, down_far, cot_far = (hop(a, "fsdp", 2) for a in (gate_half, down_half, cot_own))
    first_far, aux_far = all_after((first_far, aux_far), (gate_pack,))
    first_packs, aux_ws = beside(first_pack, first_far), beside(aux, aux_far)

    x, normed_one, q, kv, probs_a, probs_b, mixed, aux = call(
        self_forward,
        "self_forward",
        [
            ((length, width), BF16),
            ((length, width), BF16),
            ((mine, inner), BF16),
            ((length, 2 * inner), BF16),
            ((PAIRS, 2 * BLOCK, 2 * BLOCK), BF16),
            ((PAIRS, 2 * BLOCK, length), BF16),
            ((mine, inner), BF16),
            ((16, width), F32),
        ],
        [
            ((width, 3 * inner), BF16),
            ((PAIRS, 2 * BLOCK, 3 * BLOCK), F32),
            ((PAIRS, 2 * BLOCK, length), F32),
        ],
        [ids, *first_packs, *aux_ws],
        2 * 10**9,
    )
    out_far, cross_far, states_far, gate_far = all_after((out_far, cross_far, states_far, gate_far), (aux,))
    out_other, cross_other, gate_other = (hop(a, "rep", 1) for a in (out_far, cross_far, gate_far))
    outs_ws = beside_split(out_pack, out_far, out_other)
    cross_ws = beside_split(cross_pack, cross_far, cross_other)
    states_all = beside(states[0], states_far)
    hidden_one, normed_two, cross_q, cross_kv, cross_probs, cross_mixed, hidden_two, normed_three = call(
        cross_forward,
        "cross_forward",
        [
            ((mine, width), F32),
            ((mine, width), BF16),
            ((mine, inner), BF16),
            ((enc_all, 2 * inner), BF16),
            ((PAIRS, 2 * mine, enc_all), BF16),
            ((mine, inner), BF16),
            ((mine, width), F32),
            ((mine, width), BF16),
        ],
        [
            ((width, 3 * inner), BF16),
            ((2 * inner, width), BF16),
            ((enc_all, width), BF16),
        ],
        [ids, x, mixed, aux, *cross_ws, *outs_ws, *states_all],
        2 * 10**9,
    )
    gate_far, gate_other, down_far, cot_far = all_after((gate_far, gate_other, down_far, cot_far), (normed_three,))
    down_other = hop(down_far, "rep", 1)
    gates = beside_split(gate_pack, gate_far, gate_other)
    downs = beside_split(down_w, down_far, down_other)
    cots = beside(cotangent[0], cot_far)
    down_columns = down_w.size // own_rows
    result, grad_hidden_two, ff_keep, ff_send, mlp_gain_sum = call(
        feed_forward,
        "feed_forward",
        [
            ((rows, width), BF16),
            ((mine, width), F32),
            ((own_rows, 2 * hidden_units + down_columns), BF16),
            ((own_rows, 2 * hidden_units + down_columns), BF16),
            ((8, width), F32),
        ],
        [
            ((width, 2 * hidden_units), BF16),
            ((hidden_units, width), BF16),
            ((length, width), BF16),
            ((mine, width), BF16),
            ((mine, hidden_units), BF16),
            ((mine, hidden_units), BF16),
            ((mine, hidden_units), BF16),
            ((2 * own_rows, 2 * hidden_units), BF16),
            ((2 * own_rows, down_columns), BF16),
        ],
        [ids, hidden_two, normed_three, aux, *gates, *downs, *cots],
        4 * 10**9,
    )
    ff_sum = Sum("feed", ff_keep, ff_send, steps)
    grad_hidden_one, grad_mixed, states_keep, states_send, cross_keep, cross_send, cross_gain_sum = call(
        cross_backward,
        "cross_backward",
        [
            ((mine, width), F32),
            ((mine, inner), BF16),
            ((enc, width), F32),
            ((enc, width), F32),
            ((own_rows, 5 * inner), BF16),
            ((own_rows, 5 * inner), BF16),
            ((8, width), F32),
        ],
        [
            ((width, 3 * inner), BF16),
            ((2 * inner, width), BF16),
            ((enc_all, width), BF16),
            ((mine, width), BF16),
            ((mine, inner), BF16),
            ((enc_all, 2 * inner), BF16),
            ((2 * own_rows, 5 * inner), BF16),
            ((2 * enc, width), F32),
        ],
        [
            ids, grad_hidden_two, hidden_one, normed_two, cross_q, cross_kv, cross_probs, cross_mixed, mixed,
            aux, *cross_ws, *outs_ws, *states_all,
        ],
        2 * 10**9,
    )
    cross_sum = Sum("cross", cross_keep, cross_send, steps)
    done = ff_sum.fold((grad_hidden_one,))
    done = cross_sum.fold((done,))
    (grad_hidden_one,) = all_after((grad_hidden_one,), (done,))
    tokens_keep, tokens_send, self_keep, self_send = call(
        self_backward,
        "self_backward",
        [
            ((rows, width), F32),
            ((rows, width), F32),
            ((own_rows, 3 * inner + BLOCK), BF16),
            ((own_rows, 3 * inner + BLOCK), BF16),
        ],
        [
            ((width, 3 * inner), BF16),
            ((mine, inner), BF16),
            ((length, 2 * inner), BF16),
            ((2 * BLOCK, 3 * BLOCK), F32),
            ((2 * BLOCK, length), F32),
            ((2 * own_rows, 3 * inner), BF16),
            ((2 * own_rows, BLOCK), BF16),
            ((16, width), F32),
            ((BLOCK, BLOCK), F32),
        ],
        [
            ids, grad_hidden_one, grad_mixed, x, normed_one, q, kv, probs_a, probs_b, aux,
            cross_gain_sum, mlp_gain_sum, *first_packs,
        ],
        3 * 10**9,
    )
    self_sum = Sum("self", self_keep, self_send, steps)
    grad_states = states_keep + hop(states_send, "fsdp", 1)
    grad_tokens = tokens_keep + hop(tokens_send, "fsdp", 1)

    done = ff_sum.fold((tokens_keep,))
    order_of_sums = (self_sum, cross_sum, ff_sum)
    for _ in range(len(steps) - 1):
        for part in order_of_sums:
            done = part.fold((done,))
    for part in (self_sum, cross_sum):
        done = part.fold((done,))
    widenings = len(ff_sum.back) - 1
    done = ff_sum.widen((done,)) if widenings else done
    done = self_sum.fold((done,))
    for i in range(widenings):
        done = cross_sum.widen((done,))
        if i + 1 < widenings:
            done = ff_sum.widen((done,))
        done = self_sum.widen((done,))
    grad_gate, grad_up, grad_down = call(
        unpack_feed,
        "unpack_feed",
        [(gate_w.shape, F32), (up_w.shape, F32), (down_w.shape, F32)],
        [],
        [ids, *ff_sum.halves((done,))],
        0,
    )
    grad_cross_query, grad_cross_key, grad_cross_value, grad_cross_out, grad_out = call(
        unpack_cross,
        "unpack_cross",
        [(query_w.shape, F32)] * 3 + [(out_w.shape, F32)] * 2,
        [],
        [ids, *cross_sum.halves((grad_gate,))],
        0,
    )
    grad_query, grad_key, grad_value, grad_g1, grad_g2, grad_g3, grad_table = call(
        unpack_self,
        "unpack_self",
        [(query_w.shape, F32)] * 3 + [((1, own_rows), F32)] * 3 + [(bias_table.shape, F32)],
        [((own_rows, BLOCK), F32)],
        [ids, *self_sum.halves((grad_cross_query,))],
        0,
    )
    return (
        result[None],
        grad_tokens[None],
        grad_states[None],
        grad_query,
        grad_key,
        grad_value,
        grad_out,
        grad_cross_query,
        grad_cross_key,
        grad_cross_value,
        grad_cross_out,
        grad_gate,
        grad_up,
        grad_down,
        grad_g1[0],
        grad_g2[0],
        grad_g3[0],
        grad_table,
    )


def solution(mesh):
    whole = P("rep", "fsdp", None)
    rows, columns, vector = P("fsdp", None), P(None, "fsdp"), P("fsdp")
    weights = (rows, rows, rows, columns, rows, rows, rows, columns, rows, rows, rows)
    small = (vector, vector, vector, rows)
    return jax.shard_map(
        per_device,
        mesh=mesh,
        in_specs=(whole, whole) + weights + small + (whole,),
        out_specs=(whole, whole, whole) + weights + small,
        check_vma=False,
    )
```

```python
import functools
import itertools
import math

import jax
import jax.numpy as jnp
from jax import lax
from jax.experimental import pallas as pl
from jax.experimental.pallas import tpu as pltpu
from jax.sharding import PartitionSpec as P

H = 6
DH = 64
PAIRS = H // 2
BUCKETS = 32
MAXDIST = 128
EPSILON = 1e-06
MASKED = -1000000000.0
BLOCK = 128
HALF = 256
GROUP = 4
PIECES = 4
EARLY = "F"
TURNS = "XFSTCFSCSFCSCS"
SELF_HALVINGS = 2
SELF_ORDER = PIECES - (PIECES >> SELF_HALVINGS)
VMEM_BYTES = 32 * 1024 * 1024
HIGHEST = lax.Precision.HIGHEST
F32 = jnp.float32
BF16 = jnp.bfloat16


def dot(a, b):
    return jnp.dot(a, b, preferred_element_type=F32)


def dot_t(a, b):
    return lax.dot_general(a, b, (((1,), (1,)), ((), ())), preferred_element_type=F32)


def t_dot(a, b):
    return lax.dot_general(a, b, (((0,), (0,)), ((), ())), preferred_element_type=F32)


def own(f, size):
    return pl.ds(pl.multiple_of(f * size, size), size)


def place_rows(dst, pieces, f, first, size):
    for k, piece in enumerate(pieces):
        dst[own(f ^ k, size), :] = piece[first : first + size, :].astype(dst.dtype)


def place_mine(ref, f):
    return jnp.concatenate([ref[own(b, BLOCK), :] for b in my_blocks(f)], axis=0)


def my_blocks(f):
    a = (f ^ (f >> 1)) & 1
    return a, 3 - a


def split_pieces(pieces, f, half):
    for k, piece in enumerate(pieces[:2]):
        yield f ^ k, 0, piece.shape[0], piece
    parts = (len(pieces) - 2) // 2
    for k in range(2):
        far = pieces[2 + k * parts : 2 + (k + 1) * parts]
        rows = far[0].shape[0]
        for i, start in enumerate((half * rows, (1 - half) * rows, 2 * rows)[:parts]):
            yield f ^ (2 + k), start, far[i].shape[0], far[i]


def place_rows_of(dst, start, size, piece):
    dst[pl.ds(pl.multiple_of(start, 16), size), :] = piece


def bucket_of(distance):
    exact_span = BUCKETS // 2
    bucket = jnp.minimum(distance, exact_span)
    for power in range(1, exact_span):
        threshold = math.ceil(exact_span * (MAXDIST / exact_span) ** (power / exact_span))
        bucket = bucket + (distance >= threshold).astype(jnp.int32)
    return bucket


def offset_onehot(rows, axis):
    shape = (rows, 4 * BLOCK) if axis == 1 else (4 * BLOCK, rows)
    m = lax.broadcasted_iota(jnp.int32, shape, axis)
    n = jnp.where(m < 2 * BLOCK, BLOCK - m, 5 * BLOCK - m)
    bucket = bucket_of(jnp.maximum(n, 0))
    return (bucket == lax.broadcasted_iota(jnp.int32, shape, 1 - axis)).astype(F32)


def rms(v):
    return lax.rsqrt(jnp.mean(v * v, axis=-1, keepdims=True) + EPSILON)


def head_lanes(rows):
    lane = lax.broadcasted_iota(jnp.int32, (rows, 2 * DH), 1)
    return lane < DH


def only_head(pair, hd):
    low = head_lanes(pair.shape[0])
    zero = jnp.zeros_like(pair)
    return jnp.where(low, pair, zero) if hd == 0 else jnp.where(low, zero, pair)


def softmax(s):
    lifted = jnp.exp(s - jnp.max(s, axis=-1, keepdims=True))
    return lifted * (1.0 / jnp.sum(lifted, axis=-1, keepdims=True))


def norm_back(v, gain, q):
    r = rms(v)
    u = q * gain
    vr = v * r
    return r * (u - vr * jnp.mean(vr * u, axis=-1, keepdims=True)), q * vr


def stack_heads(pair):
    low = head_lanes(pair.shape[0])
    zero = jnp.zeros_like(pair)
    return jnp.concatenate([jnp.where(low, pair, zero), jnp.where(low, zero, pair)], axis=0)


def unstack_heads(stacked):
    rows = stacked.shape[0] // 2
    return jnp.where(head_lanes(rows), stacked[:rows, :], stacked[rows:, :])


def emit(keep_ref, send_ref, chip_s, first, f, orders):
    core = f & 1
    rows = keep_ref.shape[0]
    piece = rows // PIECES
    columns = chip_s.shape[1]
    for q in range(PIECES):
        for ref, which, order in ((keep_ref, core, orders[0]), (send_ref, 1 - core, orders[1])):
            to = pl.ds(pl.multiple_of((q ^ order) * piece, piece), piece)
            at = pl.ds(pl.multiple_of(which * rows + q * piece, piece), piece)
            ref[to, first : first + columns] = chip_s[at, :]


def pack_first(
    tokens_ref, q_ref, k_ref, v_ref, states_ref, g1_ref, g2_ref, g3_ref, table_ref,
    pack_ref, pack_s, g1_s, g2_s, g3_s, table_s, wide_s, sems,
):
    rows = pack_s.shape[0]
    pairs = side_by_side((tokens_ref, q_ref, k_ref, v_ref), rows, pack_s)
    first = sum(ref.shape[1] for ref in (tokens_ref, q_ref, k_ref, v_ref))
    enc, columns = states_ref.shape[0], states_ref.shape[1] * states_ref.shape[0] // rows
    for i in range(rows // enc):
        pairs.append((
            states_ref.at[:, i * columns : (i + 1) * columns],
            pack_s.at[i * enc : (i + 1) * enc, first : first + columns],
        ))
    first += columns
    pairs += [(g1_ref, g1_s), (g2_ref, g2_s), (g3_ref, g3_s), (table_ref, table_s)]
    wide_s[...] = jnp.zeros_like(wide_s)
    run_copies(pairs, sems)
    for i, gain in enumerate((g1_s, g2_s, g3_s)):
        wide_s[i : i + 1, :] = gain[...].astype(F32)
    wide_s[8:16, 0 : table_s.shape[1]] = table_s[...].astype(F32)
    pack_s[0:16, first:] = wide_s[...].astype(BF16)
    run_copies([(pack_s, pack_ref)], sems)


def run_copies(pairs, sems):
    copies = [pltpu.make_async_copy(a, b, sems.at[i]) for i, (a, b) in enumerate(pairs)]
    for c in copies:
        c.start()
    for c in copies:
        c.wait()


def side_by_side(refs, rows, target):
    pairs, first = [], 0
    for ref in refs:
        for b in range(ref.shape[0] // rows):
            pairs.append((ref.at[b * rows : (b + 1) * rows, :], target.at[:, first : first + ref.shape[1]]))
            first += ref.shape[1]
    return pairs


def pack_weights(count, ids_ref, *refs):
    weights, (whole_ref, *part_refs, whole_s, in_sems, out_sems) = refs[:count], refs[count:]
    run_copies(side_by_side(weights, whole_s.shape[0], whole_s), in_sems)
    rows = part_refs[0].shape[0]
    starts = (pl.multiple_of(ids_ref[2] * rows, rows), 2 * rows)
    parts = [(whole_s.at[pl.ds(a, ref.shape[0]), :], ref) for a, ref in zip(starts, part_refs)]
    run_copies(parts + [(whole_s, whole_ref)], out_sems)


def self_forward(
    ids_ref, w0, w1, w2, w3,
    x_ref, states_ref, normed_ref, q_ref, kv_ref, pa_ref, pb_ref, mixed_ref, aux_ref,
    w_s, bias_a, bias_b, table_s,
):
    f = ids_ref[0]
    length, width = x_ref.shape
    inner = H * DH
    enc = states_ref.shape[0] // GROUP
    after_weights = width + w_s.shape[1]
    columns = width * enc // w0.shape[0]
    for k, piece in enumerate((w0, w1, w2, w3)):
        x_ref[own(f ^ k, w0.shape[0]), :] = piece[:, :width]
        w_s[own(f ^ k, w0.shape[0]), :] = piece[:, width:after_weights]
        for i in range(width // columns):
            states_ref[own(f ^ k, enc), i * columns : (i + 1) * columns] = (
                piece[i * enc : (i + 1) * enc, after_weights : after_weights + columns]
            )
        small = piece[0:16, after_weights + columns :].astype(F32)
        aux_ref[:, own(f ^ k, BLOCK)] = small[0:8, :]
        table_s[own(f ^ k, 8), :] = small[8:16, :]
    for hb in range(length // HALF):
        at = slice(hb * HALF, (hb + 1) * HALF)
        x = x_ref[at, :].astype(F32)
        normed = (x * rms(x) * aux_ref[0:1, :]).astype(BF16)
        normed_ref[at, :] = normed
        kv_ref[at, :] = dot(normed, w_s[:, inner:]).astype(BF16)
    q_ref[...] = dot(place_mine(normed_ref, f), w_s[:, :inner]).astype(BF16)
    per_offset = lax.dot_general(
        table_s[...], offset_onehot(BUCKETS, 1), (((0,), (0,)), ((), ())),
        precision=HIGHEST, preferred_element_type=F32,
    )
    first, second = my_blocks(f)
    row = lax.broadcasted_iota(jnp.int32, (BLOCK, 2 * BLOCK), 0)
    col = lax.broadcasted_iota(jnp.int32, (BLOCK, 2 * BLOCK), 1)
    lane = lax.broadcasted_iota(jnp.int32, (BLOCK, length), 1)
    is_far = lane < (second - 1) * BLOCK
    bias_a[:, :, 2 * BLOCK :] = jnp.full((PAIRS, 2 * BLOCK, BLOCK), MASKED, F32)
    for h in range(H):
        at = slice((h % 2) * BLOCK, (h % 2 + 1) * BLOCK)
        spread = jnp.broadcast_to(per_offset[h : h + 1, :], (BLOCK, 4 * BLOCK))
        skewed = pltpu.roll(spread, 0, 1, stride=1, stride_axis=0)[:, : 2 * BLOCK]
        band = jnp.where(col - BLOCK > row, MASKED, skewed)
        bias_a[h // 2, at, pl.ds(pl.multiple_of(first * BLOCK, BLOCK), 2 * BLOCK)] = band
        bias_b[h // 2, at, :] = jnp.where(is_far, per_offset[h : h + 1, 0:1], MASKED)
        bias_b[h // 2, at, pl.ds(pl.multiple_of((second - 1) * BLOCK, BLOCK), 2 * BLOCK)] = band
    for p in range(PAIRS):
        lanes = slice(p * BLOCK, (p + 1) * BLOCK)
        k2 = kv_ref[:, lanes]
        v2 = kv_ref[:, inner + p * BLOCK : inner + (p + 1) * BLOCK]
        for slot in range(2):
            at = slice(slot * BLOCK, (slot + 1) * BLOCK)
            bias = bias_a[p, :, BLOCK:] if slot == 0 else bias_b[p]
            seen = bias.shape[1]
            s = dot_t(stack_heads(q_ref[at, lanes]), k2[:seen, :]) + bias
            probs = softmax(s).astype(BF16)
            (pa_ref, pb_ref)[slot][p] = probs
            mixed_ref[at, lanes] = unstack_heads(dot(probs, v2[:seen, :])).astype(BF16)


def place_cross(w_s, outs_s, pieces, f, half):
    first = w_s.shape[1]
    own_rows = pieces[0].shape[0]
    for owner, start, rows, piece in split_pieces(pieces, f, half):
        place_rows_of(w_s, owner * own_rows + start, rows, piece[:, :first])
        for b in range(outs_s.shape[0] // own_rows):
            to = pl.ds(pl.multiple_of(b * own_rows + start, 16), rows)
            outs_s[to, own(owner, BLOCK)] = piece[:, first + b * BLOCK : first + (b + 1) * BLOCK]


def cross_forward(
    ids_ref, x_ref, mixed_ref, aux_ref,
    w0, w1, w2, w3, w4, w5, states_s,
    h1_ref, n2_ref, cq_ref, ckv_ref, probs_ref, cmixed_ref, h2_ref, n3_ref,
    w_s, outs_s,
):
    f = ids_ref[0]
    inner = H * DH
    half = ids_ref[2]
    place_cross(w_s, outs_s, (w0, w1, w2, w3, w4, w5), f, half)
    hidden = place_mine(x_ref, f).astype(F32) + dot(mixed_ref[...], outs_s[:inner, :])
    h1_ref[...] = hidden
    normed = (hidden * rms(hidden) * aux_ref[1:2, :]).astype(BF16)
    n2_ref[...] = normed
    cq_ref[...] = dot(normed, w_s[:, :inner]).astype(BF16)
    ckv_ref[...] = dot(states_s[...], w_s[:, inner:]).astype(BF16)
    for p in range(PAIRS):
        lanes = slice(p * BLOCK, (p + 1) * BLOCK)
        v2 = ckv_ref[:, inner + p * BLOCK : inner + (p + 1) * BLOCK]
        probs = softmax(dot_t(stack_heads(cq_ref[:, lanes]), ckv_ref[:, lanes])).astype(BF16)
        probs_ref[p] = probs
        cmixed_ref[:, lanes] = unstack_heads(dot(probs, v2)).astype(BF16)
    hidden = h1_ref[...] + dot(cmixed_ref[...], outs_s[inner:, :])
    h2_ref[...] = hidden
    n3_ref[...] = (hidden * rms(hidden) * aux_ref[2:3, :]).astype(BF16)


def feed_forward(
    ids_ref, h2_ref, n3_ref, aux_ref,
    g0, g1, g2, g3, g4, g5, g6, g7, c0, c1, c2, c3,
    result_ref, grad_h2_ref, keep_ref, send_ref, gain_ref,
    gu_s, down_s, cot_s, cot_mine, units_s, gate_s, up_s, chip_s, down_chip_s,
):
    f, orders = ids_ref[0], (ids_ref[1], ids_ref[3])
    chip = f >> 1
    mine_rows, width = h2_ref.shape
    rows = cot_s.shape[0] // GROUP
    hidden_units = down_s.shape[0]
    own_units = hidden_units // GROUP
    half = ids_ref[2]
    own_rows = g0.shape[0]
    for owner, start, size, piece in split_pieces((g0, g1, g2, g3, g4, g5, g6, g7), f, half):
        place_rows_of(gu_s, owner * own_rows + start, size, piece[:, : 2 * hidden_units])
        for b in range(own_units // own_rows):
            first = 2 * hidden_units + b * width
            place_rows_of(down_s, owner * own_units + b * own_rows + start, size, piece[:, first : first + width])
    place_rows(cot_s, (c0, c1, c2, c3), f, 0, rows)
    cot_mine[...] = place_mine(cot_s, f)
    grad_normed = jnp.zeros((mine_rows, width), F32)
    chunk = 256
    for c in range(hidden_units // chunk):
        gate_at, up_at = slice(c * chunk, (c + 1) * chunk), slice(hidden_units + c * chunk, hidden_units + (c + 1) * chunk)
        gate, up = dot(n3_ref[...], gu_s[:, gate_at]), dot(n3_ref[...], gu_s[:, up_at])
        grad_units = dot_t(cot_mine[...], down_s[gate_at, :])
        square = gate * gate
        tanh = jnp.tanh(0.7978845608028654 * (gate + 0.044715 * square * gate))
        half_gate = 0.5 * gate
        gelu = half_gate + half_gate * tanh
        slope = 0.5 + 0.5 * tanh + half_gate * (1.0 - tanh * tanh) * (
            0.7978845608028654 + (3 * 0.044715 * 0.7978845608028654) * square
        )
        units_s[:, gate_at] = (gelu * up).astype(BF16)
        grad_gate = (grad_units * up * slope).astype(BF16)
        grad_up = (grad_units * gelu).astype(BF16)
        gate_s[:, gate_at] = grad_gate
        up_s[:, gate_at] = grad_up
        grad_normed = grad_normed + dot_t(grad_gate, gu_s[:, gate_at]) + dot_t(grad_up, gu_s[:, up_at])
    piece, gain_part = norm_back(h2_ref[...], aux_ref[2:3, :], grad_normed)
    grad_h2_ref[...] = cot_mine[...].astype(F32) + piece
    gain_ref[...] = jnp.broadcast_to(jnp.sum(gain_part, axis=0, keepdims=True), gain_ref.shape)
    mine = own(chip, rows)
    result_ref[...] = (h2_ref[mine, :] + dot(units_s[mine, :], down_s[...])).astype(BF16)
    chip_rows = 2 * g0.shape[0]
    normed_chip = n3_ref[:, own(chip, chip_rows)]
    chip_s[:, :hidden_units] = t_dot(normed_chip, gate_s[...]).astype(BF16)
    chip_s[:, hidden_units:] = t_dot(normed_chip, up_s[...]).astype(BF16)
    emit(keep_ref, send_ref, chip_s, 0, f, orders)
    grad_down = t_dot(units_s[:, own(chip, 2 * own_units)], cot_mine[...]).astype(BF16)
    parts = own_units // g0.shape[0]
    for which in range(2):
        for part in range(parts):
            at = slice((which * parts + part) * g0.shape[0], (which * parts + part + 1) * g0.shape[0])
            down_chip_s[which * g0.shape[0] : (which + 1) * g0.shape[0], part * width : (part + 1) * width] = grad_down[at, :]
    emit(keep_ref, send_ref, down_chip_s, 2 * hidden_units, f, orders)


def put_columns(chip_s, first, grad, own_rows):
    columns = grad.shape[1] // 2
    for which in range(2):
        for part in range(grad.shape[0] // own_rows):
            chip_s[which * own_rows : (which + 1) * own_rows, first + part * columns : first + (part + 1) * columns] = (
                grad[part * own_rows : (part + 1) * own_rows, which * columns : (which + 1) * columns]
            )


def cross_backward(
    ids_ref, grad_h2_ref, h1_ref, n2_ref, cq_ref, ckv_ref, probs_ref, cmixed_ref, mixed_ref, aux_ref,
    w0, w1, w2, w3, w4, w5, states_s,
    grad_h1_ref, mix_ref, states_keep, states_send, keep_ref, send_ref, gain_ref,
    w_s, outs_s, low_s, dq_s, dkv_s, chip_s, states_chip,
):
    f, orders = ids_ref[0], (ids_ref[1], ids_ref[3])
    chip, core = f >> 1, f & 1
    inner = H * DH
    own_rows = w0.shape[0]
    chip_columns = own(chip, 2 * own_rows)
    half = ids_ref[2]
    place_cross(w_s, outs_s, (w0, w1, w2, w3, w4, w5), f, half)
    low = grad_h2_ref[...].astype(BF16)
    low_s[...] = low
    grad_mixed = dot_t(low, outs_s[inner:, :]).astype(BF16)
    put_columns(chip_s, 3 * inner, t_dot(cmixed_ref[...], low_s[:, chip_columns]).astype(BF16), own_rows)
    for p in range(PAIRS):
        lanes = slice(p * BLOCK, (p + 1) * BLOCK)
        v_lanes = slice(inner + p * BLOCK, inner + (p + 1) * BLOCK)
        stacked = stack_heads(grad_mixed[:, lanes])
        probs = probs_ref[p].astype(F32)
        weighted = probs * dot_t(stacked, ckv_ref[:, v_lanes])
        ds = (weighted - probs * jnp.sum(weighted, axis=-1, keepdims=True)).astype(BF16)
        dq_s[:, lanes] = unstack_heads(dot(ds, ckv_ref[:, lanes])).astype(BF16)
        dkv_s[:, lanes] = t_dot(ds, stack_heads(cq_ref[:, lanes])).astype(BF16)
        dkv_s[:, v_lanes] = t_dot(probs_ref[p], stacked).astype(BF16)
    grad_normed = dot_t(dq_s[...], w_s[:, :inner])
    piece, gain_part = norm_back(h1_ref[...], aux_ref[1:2, :], grad_normed)
    grad_h1 = grad_h2_ref[...] + piece
    grad_h1_ref[...] = grad_h1
    gain_ref[...] = jnp.broadcast_to(jnp.sum(gain_part, axis=0, keepdims=True), gain_ref.shape)
    low = grad_h1.astype(BF16)
    low_s[...] = low
    mix_ref[...] = dot_t(low, outs_s[:inner, :]).astype(BF16)
    put_columns(chip_s, 4 * inner, t_dot(mixed_ref[...], low_s[:, chip_columns]).astype(BF16), own_rows)
    chip_s[:, :inner] = t_dot(n2_ref[:, chip_columns], dq_s[...]).astype(BF16)
    chip_s[:, inner : 3 * inner] = t_dot(states_s[:, chip_columns], dkv_s[...]).astype(BF16)
    emit(keep_ref, send_ref, chip_s, 0, f, orders)
    enc = states_s.shape[0] // GROUP
    states_chip[...] = dot_t(dkv_s[own(chip, 2 * enc), :], w_s[:, inner:])
    states_keep[...] = states_chip[own(core, enc), :]
    states_send[...] = states_chip[own(1 - core, enc), :]


def self_backward(ids_ref, mix_ref, q_ref, kv_ref, pa_ref, pb_ref, dq_s, dkv_s, table_s, ds_a, ds_b):
    inner = H * DH
    first, second = my_blocks(ids_ref[0])
    row = lax.broadcasted_iota(jnp.int32, (2 * BLOCK, 4 * BLOCK), 0)
    ds_a[:, 0:BLOCK] = jnp.zeros((2 * BLOCK, BLOCK), F32)
    offset_sums, far_sums = [], []
    for p in range(PAIRS):
        lanes = slice(p * BLOCK, (p + 1) * BLOCK)
        v_lanes = slice(inner + p * BLOCK, inner + (p + 1) * BLOCK)
        k2, v2 = kv_ref[:, lanes], kv_ref[:, v_lanes]
        dk, dv = [], []
        for slot in range(2):
            at = slice(slot * BLOCK, (slot + 1) * BLOCK)
            probs_low = (pa_ref, pb_ref)[slot][p]
            seen = probs_low.shape[1]
            stacked = stack_heads(mix_ref[at, lanes])
            probs = probs_low.astype(F32)
            weighted = probs * dot_t(stacked, v2[:seen, :])
            ds = weighted - probs * jnp.sum(weighted, axis=-1, keepdims=True)
            if slot == 0:
                ds_a[:, BLOCK:] = ds
            else:
                ds_b[...] = ds
            low = ds.astype(BF16)
            dq_s[at, lanes] = unstack_heads(dot(low, k2[:seen, :])).astype(BF16)
            dk.append(t_dot(low, stack_heads(q_ref[at, lanes])))
            dv.append(t_dot(probs_low, stacked))
        for total, to in ((dk, lanes), (dv, v_lanes)):
            seen = total[0].shape[0]
            dkv_s[:seen, to] = (total[0] + total[1][:seen, :]).astype(BF16)
            dkv_s[seen:, to] = total[1][seen:, :].astype(BF16)
        band_b = ds_b[:, pl.ds(pl.multiple_of((second - 1) * BLOCK, BLOCK), 2 * BLOCK)]
        band_a = ds_a[:, pl.ds(pl.multiple_of(first * BLOCK, BLOCK), 2 * BLOCK)]
        far = jnp.sum(ds_b[...], axis=1, keepdims=True) - jnp.sum(band_b, axis=1, keepdims=True)
        skew = jnp.concatenate([band_a + band_b, jnp.zeros((2 * BLOCK, 2 * BLOCK), F32)], axis=1)
        for bit in range(BLOCK.bit_length() - 1):
            moved = pltpu.roll(skew, 4 * BLOCK - (1 << bit), 1)
            skew = jnp.where((row & (1 << bit)) != 0, moved, skew)
        for hd in range(2):
            at = slice(hd * BLOCK, (hd + 1) * BLOCK)
            offset_sums.append(jnp.sum(skew[at, :], axis=0, keepdims=True))
            far_sums.append(jnp.sum(far[at, :], axis=0, keepdims=True))
    per_offset = jnp.concatenate(offset_sums + [jnp.zeros((BLOCK - H, 4 * BLOCK), F32)], axis=0)
    far_all = jnp.concatenate(far_sums + [jnp.zeros((BLOCK - H, 1), F32)], axis=0)
    per_offset = per_offset + jnp.where(
        lax.broadcasted_iota(jnp.int32, (BLOCK, 4 * BLOCK), 1) == 0, far_all, 0.0
    )
    table_s[...] = lax.dot_general(
        offset_onehot(BLOCK, 1), per_offset, (((1,), (1,)), ((), ())),
        precision=HIGHEST, preferred_element_type=F32,
    )


def self_gradients(
    ids_ref, grad_h1_ref, x_ref, normed_ref, aux_ref, gain2_ref, gain3_ref, dq_s, dkv_s, table_s, w0, w1, w2, w3,
    tokens_keep, tokens_send, keep_ref, send_ref,
    w_s, chip_s, small_s, gain_s,
):
    f, orders = ids_ref[0], (ids_ref[1] & SELF_ORDER, ids_ref[3] & SELF_ORDER)
    chip = f >> 1
    length, width = x_ref.shape
    rows = length // GROUP
    inner = H * DH
    own_rows = w0.shape[0]
    chip_columns = own(chip, 2 * own_rows)
    first, second = my_blocks(f)
    for k, piece in enumerate((w0, w1, w2, w3)):
        w_s[own(f ^ k, own_rows), :] = piece[:, width : width + 3 * inner]
    gain = aux_ref[0:1, :]
    mine, block = own(chip, rows), own(f, rows)
    others = own(f ^ 1, rows)
    grad_normed = dot_t(dq_s[mine, :], w_s[:, :inner]) + dot_t(dkv_s[block, :], w_s[:, inner:])
    piece, _ = norm_back(x_ref[block, :].astype(F32), gain, grad_normed)
    tokens_keep[...] = grad_h1_ref[mine, :] + piece
    piece, _ = norm_back(x_ref[others, :].astype(F32), gain, dot_t(dkv_s[others, :], w_s[:, inner:]))
    tokens_send[...] = piece
    chip_w = w_s[chip_columns, :]
    gain_sum = jnp.zeros((1, 2 * own_rows), F32)
    for hb in range(length // HALF):
        at = slice(hb * HALF, (hb + 1) * HALF)
        scaled = x_ref[at, chip_columns].astype(F32) * rms(x_ref[at, :].astype(F32))
        gain_sum = gain_sum + jnp.sum(dot_t(dkv_s[at, :], chip_w[:, inner:]) * scaled, axis=0, keepdims=True)
    grad_q = dot_t(dq_s[...], chip_w[:, :inner])
    for slot, b in enumerate((first, second)):
        scaled = x_ref[own(b, BLOCK), chip_columns].astype(F32) * rms(x_ref[own(b, BLOCK), :].astype(F32))
        gain_sum = gain_sum + jnp.sum(grad_q[slot * BLOCK : (slot + 1) * BLOCK, :] * scaled, axis=0, keepdims=True)
    normed_mine = jnp.concatenate([normed_ref[own(b, BLOCK), chip_columns] for b in (first, second)], axis=0)
    chip_s[:, :inner] = t_dot(normed_mine, dq_s[...]).astype(BF16)
    chip_s[:, inner:] = t_dot(normed_ref[:, chip_columns], dkv_s[...]).astype(BF16)
    emit(keep_ref, send_ref, chip_s, 0, f, orders)
    gain_s[0:8, :] = gain2_ref[...]
    gain_s[8:16, :] = gain3_ref[...]
    buckets = BUCKETS // GROUP
    for which in range(2):
        owner = 2 * chip + which
        small = jnp.concatenate(
            [
                table_s[own(owner, buckets), :],
                gain_sum[:, which * own_rows : (which + 1) * own_rows],
                gain_s[0:1, own(owner, own_rows)],
                gain_s[8:9, own(owner, own_rows)],
                jnp.zeros((own_rows - buckets - 3, BLOCK), F32),
            ],
            axis=0,
        )
        small_s[which * own_rows : (which + 1) * own_rows, :] = small.astype(BF16)
    emit(keep_ref, send_ref, small_s, 3 * inner, f, orders)


def fold(keep_ref, arrived_ref, *out_refs):
    total = (keep_ref[...].astype(F32) + arrived_ref[...].astype(F32)).astype(BF16)
    rows = total.shape[0] // len(out_refs)
    for i, ref in enumerate(out_refs):
        ref[...] = total[i * rows : (i + 1) * rows, :]


def pieces_of(ids_ref, halves, mask=PIECES - 1):
    order = ids_ref[1] & mask
    for i, half in enumerate(halves):
        piece = half.shape[0] * len(halves) // PIECES
        here = PIECES // len(halves)
        for j in range(here):
            q = (i * here + j) ^ order
            yield q * piece, piece, half[j * piece : (j + 1) * piece, :].astype(F32)


def unpack_feed(ids_ref, low_ref, high_ref, gate_ref, up_ref, down_ref):
    units, width, own_rows = gate_ref.shape[1], down_ref.shape[1], gate_ref.shape[0]
    for at, size, rows in pieces_of(ids_ref, (low_ref, high_ref)):
        to = pl.ds(pl.multiple_of(at, size), size)
        gate_ref[to, :] = rows[:, :units]
        up_ref[to, :] = rows[:, units : 2 * units]
        for part in range(down_ref.shape[0] // own_rows):
            first = 2 * units + part * width
            down_ref[pl.ds(pl.multiple_of(part * own_rows + at, size), size), :] = rows[:, first : first + width]


def unpack_cross(ids_ref, low_ref, high_ref, cq_ref, ck_ref, cv_ref, co_ref, out_ref):
    own_rows, inner = cq_ref.shape
    for at, size, rows in pieces_of(ids_ref, (low_ref, high_ref)):
        to = pl.ds(pl.multiple_of(at, size), size)
        for i, ref in enumerate((cq_ref, ck_ref, cv_ref)):
            ref[to, :] = rows[:, i * inner : (i + 1) * inner]
        for i, ref in enumerate((co_ref, out_ref)):
            columns = ref.shape[1]
            for part in range(inner // own_rows):
                first = (3 + i) * inner + part * columns
                ref[pl.ds(pl.multiple_of(part * own_rows + at, size), size), :] = rows[:, first : first + columns]


def unpack_self(ids_ref, low_ref, high_ref, q_ref, k_ref, v_ref, g1_ref, g2_ref, g3_ref, table_ref, small_s):
    inner = q_ref.shape[1]
    for at, size, rows in pieces_of(ids_ref, (low_ref, high_ref), SELF_ORDER):
        to = pl.ds(pl.multiple_of(at, size), size)
        for i, ref in enumerate((q_ref, k_ref, v_ref)):
            ref[to, :] = rows[:, i * inner : (i + 1) * inner]
        small_s[to, :] = rows[:, 3 * inner :]
    buckets, heads = table_ref.shape
    table_ref[...] = small_s[0:buckets, 0:heads]
    for i, ref in enumerate((g1_ref, g2_ref, g3_ref)):
        ref[...] = small_s[buckets + i : buckets + i + 1, :]


VMEM = pl.BlockSpec(memory_space=pltpu.VMEM)
SMEM = pl.BlockSpec(memory_space=pltpu.SMEM)


def call(kernel, name, out_shapes, scratch, args, with_ids=True, place=VMEM):
    return pl.pallas_call(
        kernel,
        name=name,
        out_shape=[jax.ShapeDtypeStruct(s, d) for s, d in out_shapes],
        in_specs=([SMEM] if with_ids else []) + [place] * (len(args) - with_ids),
        out_specs=[place] * len(out_shapes),
        scratch_shapes=[pltpu.VMEM(*s) if isinstance(s, tuple) else s for s in scratch],
        compiler_params=pltpu.CompilerParams(vmem_limit_bytes=VMEM_BYTES if place is VMEM else 56 * 1024 * 1024),
        cost_estimate=pl.CostEstimate(flops=1, bytes_accessed=1, transcendentals=0),
    )(*args)


def hop(x, axis, bits):
    size = lax.axis_size(axis)
    return lax.ppermute(x, axis, [(i, i ^ bits) for i in range(size)])


def all_after(arrays, earlier):
    return lax.optimization_barrier((tuple(arrays), tuple(earlier)))[0]


def beside(pack, far):
    return pack, hop(pack, "fsdp", 1), far, hop(far, "fsdp", 1)


def beside_split(pack, far, far_other, *rest):
    parts = (far, far_other, *rest)
    return pack, hop(pack, "fsdp", 1), *parts, *(hop(a, "fsdp", 1) for a in parts)


def rep_hop(x, bits):
    replicas, group = lax.axis_size("rep"), lax.axis_size("fsdp")
    pairs = [(r * group + f, (r ^ bits[f & 1]) * group + f) for r in range(replicas) for f in range(group)]
    return lax.ppermute(x, ("rep", "fsdp"), pairs)


class Sum:
    def __init__(self, name, keep, send, halvings):
        bits = (lax.axis_size("rep") - 1).bit_length()
        self.name, self.keep, self.at = name, keep, 0
        self.arrived = hop(send, "fsdp", 1)
        self.steps = [(1, 2), (2, 1)] + [(1 << i, 1 << i) for i in range(2, bits)]
        self.back = self.steps[:halvings]
        self.halvings = halvings

    def fold(self, earlier):
        keep, arrived = all_after((self.keep, self.arrived), earlier)
        halving = self.at < self.halvings
        total = (keep.astype(F32) + arrived.astype(F32)).astype(BF16)
        middle = total.shape[0] // 2
        out = (total[:middle], total[middle:]) if halving else (total,)
        self.keep = out[0]
        if self.at < len(self.steps):
            self.arrived = rep_hop(out[-1], self.steps[self.at])
        else:
            self.arrived = rep_hop(self.keep, self.back[-1])
        self.at += 1
        return self.keep

    def widen(self, earlier):
        keep, arrived = all_after((self.keep, self.arrived), earlier)
        self.back.pop()
        self.keep = jnp.concatenate((keep, arrived))
        self.arrived = rep_hop(self.keep, self.back[-1])
        return self.keep

    def halves(self, earlier):
        return all_after((self.keep, self.arrived), earlier)

    def actions(self):
        return [self.fold] * (len(self.steps) + 1 - self.at) + [self.widen] * (len(self.back) - 1)


def per_device(
    tokens,
    states,
    query_w,
    key_w,
    value_w,
    out_w,
    cross_query_w,
    cross_key_w,
    cross_value_w,
    cross_out_w,
    gate_w,
    up_w,
    down_w,
    self_gain,
    cross_gain,
    mlp_gain,
    bias_table,
    cotangent,
):
    seq_count, rows, width = tokens.shape
    enc = states.shape[1]
    own_rows, inner = query_w.shape
    hidden_units = gate_w.shape[1]
    length, enc_all, mine = rows * GROUP, enc * GROUP, 2 * BLOCK
    f = lax.axis_index("fsdp").astype(jnp.int32)
    replica = lax.axis_index("rep").astype(jnp.int32)
    order_0 = ((replica & 1) << 1) | ((replica >> 1) & 1)
    order_1 = replica & 3
    core = f & 1
    ids = jnp.stack([f, jnp.where(core == 0, order_0, order_1), replica & 1, jnp.where(core == 0, order_1, order_0)])

    hbm = pl.BlockSpec(memory_space=pl.ANY)
    first_columns = width + 3 * inner + enc * width // rows + BLOCK
    (first_pack,) = call(
        pack_first,
        "pack_first",
        [((rows, first_columns), BF16)],
        [
            ((rows, first_columns), BF16),
            ((1, own_rows), BF16),
            ((1, own_rows), BF16),
            ((1, own_rows), BF16),
            (bias_table.shape, BF16),
            ((16, BLOCK), F32),
            pltpu.SemaphoreType.DMA((8 + rows // enc,)),
        ],
        [tokens[0], query_w, key_w, value_w, states[0], self_gain[None], cross_gain[None], mlp_gain[None], bias_table],
        False,
        hbm,
    )
    (second_ids,) = all_after((ids,), (first_pack,))

    def packed(name, ids, weights, parts):
        columns = sum(w.size for w in weights) // own_rows
        return call(
            functools.partial(pack_weights, len(weights)),
            name,
            [((rows, columns), BF16) for rows in (own_rows, *parts)],
            [
                ((own_rows, columns), BF16),
                pltpu.SemaphoreType.DMA((sum(w.shape[0] for w in weights) // own_rows,)),
                pltpu.SemaphoreType.DMA((1 + len(parts),)),
            ],
            [ids, *weights],
            place=hbm,
        )

    second_pack, second_half = packed(
        "pack_second", second_ids, [cross_query_w, cross_key_w, cross_value_w, out_w, cross_out_w], [own_rows // 2]
    )
    (third_ids,) = all_after((ids,), (second_pack,))
    part = 3 * own_rows // 8
    third_pack, third_part, third_rest = packed(
        "pack_third", third_ids, [gate_w, up_w, down_w], [part, own_rows - 2 * part]
    )
    first_far, second_far = hop(first_pack, "fsdp", 2), hop(second_half, "fsdp", 2)
    (first_far,) = all_after((first_far,), (third_pack,))
    first_packs = beside(first_pack, first_far)

    x, states_all, normed_one, q, kv, probs_a, probs_b, mixed, aux = call(
        self_forward,
        "self_forward",
        [
            ((length, width), BF16),
            ((enc_all, width), BF16),
            ((length, width), BF16),
            ((mine, inner), BF16),
            ((length, 2 * inner), BF16),
            ((PAIRS, 2 * BLOCK, 2 * BLOCK), BF16),
            ((PAIRS, 2 * BLOCK, length), BF16),
            ((mine, inner), BF16),
            ((8, width), F32),
        ],
        [
            ((width, 3 * inner), BF16),
            ((PAIRS, 2 * BLOCK, 3 * BLOCK), F32),
            ((PAIRS, 2 * BLOCK, length), F32),
            ((BUCKETS, BLOCK), F32),
        ],
        [ids, *first_packs],
    )
    (cot_own,) = all_after((cotangent[0],), (first_far,))
    second_far, second_pack, third_pack, third_part, third_rest = all_after(
        (second_far, second_pack, third_pack, third_part, third_rest), (aux,)
    )
    third_far = hop(third_part, "fsdp", 2)
    second_other = hop(second_far, "rep", 1)
    rest_far = hop(third_rest, "fsdp", 2)
    cot_far = hop(cot_own, "fsdp", 2)
    seconds = beside_split(second_pack, second_far, second_other)
    cots = beside(cot_own, cot_far)
    (cross_ids,) = all_after((ids,), (third_far, cots[3]))
    hidden_one, normed_two, cross_q, cross_kv, cross_probs, cross_mixed, hidden_two, normed_three = call(
        cross_forward,
        "cross_forward",
        [
            ((mine, width), F32),
            ((mine, width), BF16),
            ((mine, inner), BF16),
            ((enc_all, 2 * inner), BF16),
            ((PAIRS, 2 * mine, enc_all), BF16),
            ((mine, inner), BF16),
            ((mine, width), F32),
            ((mine, width), BF16),
        ],
        [
            ((width, 3 * inner), BF16),
            ((2 * inner, width), BF16),
        ],
        [cross_ids, x, mixed, aux, *seconds, states_all],
    )
    third_other = hop(third_far, "rep", 1)
    third_far, third_other, rest_far = all_after((third_far, third_other, rest_far), (normed_three,))
    thirds = beside_split(third_pack, third_far, third_other, rest_far)
    down_columns = down_w.size // own_rows
    result, grad_hidden_two, ff_keep, ff_send, mlp_gain_sum = call(
        feed_forward,
        "feed_forward",
        [
            ((rows, width), BF16),
            ((mine, width), F32),
            ((own_rows, 2 * hidden_units + down_columns), BF16),
            ((own_rows, 2 * hidden_units + down_columns), BF16),
            ((8, width), F32),
        ],
        [
            ((width, 2 * hidden_units), BF16),
            ((hidden_units, width), BF16),
            ((length, width), BF16),
            ((mine, width), BF16),
            ((mine, hidden_units), BF16),
            ((mine, hidden_units), BF16),
            ((mine, hidden_units), BF16),
            ((2 * own_rows, 2 * hidden_units), BF16),
            ((2 * own_rows, down_columns), BF16),
        ],
        [ids, hidden_two, normed_three, aux, *thirds, *cots],
    )
    ff_sum = Sum("feed", ff_keep, ff_send, 2)
    grad_hidden_one, grad_mixed, states_keep, states_send, cross_keep, cross_send, cross_gain_sum = call(
        cross_backward,
        "cross_backward",
        [
            ((mine, width), F32),
            ((mine, inner), BF16),
            ((enc, width), F32),
            ((enc, width), F32),
            ((own_rows, 5 * inner), BF16),
            ((own_rows, 5 * inner), BF16),
            ((8, width), F32),
        ],
        [
            ((width, 3 * inner), BF16),
            ((2 * inner, width), BF16),
            ((mine, width), BF16),
            ((mine, inner), BF16),
            ((enc_all, 2 * inner), BF16),
            ((2 * own_rows, 5 * inner), BF16),
            ((2 * enc, width), F32),
        ],
        [
            ids, grad_hidden_two, hidden_one, normed_two, cross_q, cross_kv, cross_probs, cross_mixed, mixed,
            aux, *seconds, states_all,
        ],
    )
    cross_sum = Sum("cross", cross_keep, cross_send, 2)
    sums = {"F": ff_sum, "C": cross_sum}
    done = ff_sum.fold((grad_hidden_one,))
    done = cross_sum.fold((done,))
    (grad_mixed,) = all_after((grad_mixed,), (done,))
    grad_q, grad_kv, table_sums = call(
        self_backward,
        "self_backward",
        [((mine, inner), BF16), ((length, 2 * inner), BF16), ((BLOCK, BLOCK), F32)],
        [((2 * BLOCK, 3 * BLOCK), F32), ((2 * BLOCK, length), F32)],
        [ids, grad_mixed, q, kv, probs_a, probs_b],
    )
    done = grad_q
    for turn in EARLY:
        done = sums[turn].fold((done,))
    (late_ids,) = all_after((ids,), (done,))
    tokens_keep, tokens_send, self_keep, self_send = call(
        self_gradients,
        "self_gradients",
        [
            ((rows, width), F32),
            ((rows, width), F32),
            ((own_rows, 3 * inner + BLOCK), BF16),
            ((own_rows, 3 * inner + BLOCK), BF16),
        ],
        [
            ((width, 3 * inner), BF16),
            ((2 * own_rows, 3 * inner), BF16),
            ((2 * own_rows, BLOCK), BF16),
            ((16, width), F32),
        ],
        [
            late_ids, grad_hidden_one, x, normed_one, aux, cross_gain_sum, mlp_gain_sum,
            grad_q, grad_kv, table_sums, *first_packs,
        ],
    )
    done = tokens_keep
    for turn in TURNS:
        if turn == "X":
            self_keep, self_send = all_after((self_keep, self_send), (done,))
            self_sum = sums["S"] = Sum("self", self_keep, self_send, SELF_HALVINGS)
        elif turn == "T":
            states_send, tokens_send = all_after((states_send, tokens_send), (done,))
            grad_states = states_keep + hop(states_send, "fsdp", 1)
            grad_tokens = tokens_keep + hop(tokens_send, "fsdp", 1)
        elif sums[turn].actions():
            done = sums[turn].actions()[0]((done,))
    while any(part.actions() for part in sums.values()):
        for part in sums.values():
            done = part.actions()[0]((done,)) if part.actions() else done
    grad_gate, grad_up, grad_down = call(
        unpack_feed,
        "unpack_feed",
        [(gate_w.shape, F32), (up_w.shape, F32), (down_w.shape, F32)],
        [],
        [ids, *ff_sum.halves((done,))],
    )
    grad_cross_query, grad_cross_key, grad_cross_value, grad_cross_out, grad_out = call(
        unpack_cross,
        "unpack_cross",
        [(query_w.shape, F32)] * 3 + [(out_w.shape, F32)] * 2,
        [],
        [ids, *cross_sum.halves((grad_gate,))],
    )
    grad_query, grad_key, grad_value, grad_g1, grad_g2, grad_g3, grad_table = call(
        unpack_self,
        "unpack_self",
        [(query_w.shape, F32)] * 3 + [((1, own_rows), F32)] * 3 + [(bias_table.shape, F32)],
        [((own_rows, BLOCK), F32)],
        [ids, *self_sum.halves((grad_cross_query,))],
    )
    return (
        result[None],
        grad_tokens[None],
        grad_states[None],
        grad_query,
        grad_key,
        grad_value,
        grad_out,
        grad_cross_query,
        grad_cross_key,
        grad_cross_value,
        grad_cross_out,
        grad_gate,
        grad_up,
        grad_down,
        grad_g1[0],
        grad_g2[0],
        grad_g3[0],
        grad_table,
    )


def solution(mesh):
    whole = P("rep", "fsdp", None)
    rows, columns, vector = P("fsdp", None), P(None, "fsdp"), P("fsdp")
    weights = (rows, rows, rows, columns, rows, rows, rows, columns, rows, rows, rows)
    small = (vector, vector, vector, rows)
    return jax.shard_map(
        per_device,
        mesh=mesh,
        in_specs=(whole, whole) + weights + small + (whole,),
        out_specs=(whole, whole, whole) + weights + small,
        check_vma=False,
    )
```

```python
import functools
import itertools
import math

import jax
import jax.numpy as jnp
from jax import lax
from jax.experimental import pallas as pl
from jax.experimental.pallas import tpu as pltpu
from jax.sharding import PartitionSpec as P

H = 6
DH = 64
PAIRS = H // 2
BUCKETS = 32
MAXDIST = 128
EPSILON = 1e-06
MASKED = -1000000000.0
BLOCK = 128
HALF = 256
GROUP = 4
PIECES = 4
EARLY = "F"
TURNS = "XFSTCFCSSFCSCS"
SELF_HALVINGS = 2
SELF_ORDER = PIECES - (PIECES >> SELF_HALVINGS)
VMEM_BYTES = 32 * 1024 * 1024
HIGHEST = lax.Precision.HIGHEST
F32 = jnp.float32
BF16 = jnp.bfloat16


def dot(a, b):
    return jnp.dot(a, b, preferred_element_type=F32)


def dot_t(a, b):
    return lax.dot_general(a, b, (((1,), (1,)), ((), ())), preferred_element_type=F32)


def t_dot(a, b):
    return lax.dot_general(a, b, (((0,), (0,)), ((), ())), preferred_element_type=F32)


def own(f, size):
    return pl.ds(pl.multiple_of(f * size, size), size)


def place_rows(dst, pieces, f, first, size):
    for k, piece in enumerate(pieces):
        dst[own(f ^ k, size), :] = piece[first : first + size, :].astype(dst.dtype)


def place_mine(ref, f):
    return jnp.concatenate([ref[own(b, BLOCK), :] for b in my_blocks(f)], axis=0)


def my_blocks(f):
    a = (f ^ (f >> 1)) & 1
    return a, 3 - a


def split_pieces(pieces, f, half):
    for k, piece in enumerate(pieces[:2]):
        yield f ^ k, 0, piece.shape[0], piece
    parts = (len(pieces) - 2) // 2
    for k in range(2):
        far = pieces[2 + k * parts : 2 + (k + 1) * parts]
        rows = far[0].shape[0]
        for i, start in enumerate((half * rows, (1 - half) * rows, 2 * rows)[:parts]):
            yield f ^ (2 + k), start, far[i].shape[0], far[i]


def place_rows_of(dst, start, size, piece):
    dst[pl.ds(pl.multiple_of(start, 16), size), :] = piece


def bucket_of(distance):
    exact_span = BUCKETS // 2
    bucket = jnp.minimum(distance, exact_span)
    for power in range(1, exact_span):
        threshold = math.ceil(exact_span * (MAXDIST / exact_span) ** (power / exact_span))
        bucket = bucket + (distance >= threshold).astype(jnp.int32)
    return bucket


def offset_onehot(rows, axis):
    shape = (rows, 4 * BLOCK) if axis == 1 else (4 * BLOCK, rows)
    m = lax.broadcasted_iota(jnp.int32, shape, axis)
    n = jnp.where(m < 2 * BLOCK, BLOCK - m, 5 * BLOCK - m)
    bucket = bucket_of(jnp.maximum(n, 0))
    return (bucket == lax.broadcasted_iota(jnp.int32, shape, 1 - axis)).astype(F32)


def rms(v):
    return lax.rsqrt(jnp.mean(v * v, axis=-1, keepdims=True) + EPSILON)


def head_lanes(rows):
    lane = lax.broadcasted_iota(jnp.int32, (rows, 2 * DH), 1)
    return lane < DH


def only_head(pair, hd):
    low = head_lanes(pair.shape[0])
    zero = jnp.zeros_like(pair)
    return jnp.where(low, pair, zero) if hd == 0 else jnp.where(low, zero, pair)


def softmax(s):
    lifted = jnp.exp(s - jnp.max(s, axis=-1, keepdims=True))
    return lifted * (1.0 / jnp.sum(lifted, axis=-1, keepdims=True))


def norm_back(v, gain, q):
    r = rms(v)
    u = q * gain
    vr = v * r
    return r * (u - vr * jnp.mean(vr * u, axis=-1, keepdims=True)), q * vr


def stack_heads(pair):
    low = head_lanes(pair.shape[0])
    zero = jnp.zeros_like(pair)
    return jnp.concatenate([jnp.where(low, pair, zero), jnp.where(low, zero, pair)], axis=0)


def unstack_heads(stacked):
    rows = stacked.shape[0] // 2
    return jnp.where(head_lanes(rows), stacked[:rows, :], stacked[rows:, :])


def emit(keep_ref, send_ref, chip_s, first, f, orders):
    core = f & 1
    rows = keep_ref.shape[0]
    piece = rows // PIECES
    columns = chip_s.shape[1]
    for q in range(PIECES):
        for ref, which, order in ((keep_ref, core, orders[0]), (send_ref, 1 - core, orders[1])):
            to = pl.ds(pl.multiple_of((q ^ order) * piece, piece), piece)
            at = pl.ds(pl.multiple_of(which * rows + q * piece, piece), piece)
            ref[to, first : first + columns] = chip_s[at, :]


def pack_first(
    tokens_ref, q_ref, k_ref, v_ref, states_ref, g1_ref, g2_ref, g3_ref, table_ref,
    pack_ref, pack_s, g1_s, g2_s, g3_s, table_s, wide_s, sems,
):
    rows = pack_s.shape[0]
    pairs = side_by_side((tokens_ref, q_ref, k_ref, v_ref), rows, pack_s)
    first = sum(ref.shape[1] for ref in (tokens_ref, q_ref, k_ref, v_ref))
    enc, columns = states_ref.shape[0], states_ref.shape[1] * states_ref.shape[0] // rows
    for i in range(rows // enc):
        pairs.append((
            states_ref.at[:, i * columns : (i + 1) * columns],
            pack_s.at[i * enc : (i + 1) * enc, first : first + columns],
        ))
    first += columns
    pairs += [(g1_ref, g1_s), (g2_ref, g2_s), (g3_ref, g3_s), (table_ref, table_s)]
    wide_s[...] = jnp.zeros_like(wide_s)
    run_copies(pairs, sems)
    for i, gain in enumerate((g1_s, g2_s, g3_s)):
        wide_s[i : i + 1, :] = gain[...].astype(F32)
    wide_s[8:16, 0 : table_s.shape[1]] = table_s[...].astype(F32)
    pack_s[0:16, first:] = wide_s[...].astype(BF16)
    run_copies([(pack_s, pack_ref)], sems)


def run_copies(pairs, sems):
    copies = [pltpu.make_async_copy(a, b, sems.at[i]) for i, (a, b) in enumerate(pairs)]
    for c in copies:
        c.start()
    for c in copies:
        c.wait()


def side_by_side(refs, rows, target):
    pairs, first = [], 0
    for ref in refs:
        for b in range(ref.shape[0] // rows):
            pairs.append((ref.at[b * rows : (b + 1) * rows, :], target.at[:, first : first + ref.shape[1]]))
            first += ref.shape[1]
    return pairs


def pack_weights(count, bit, ids_ref, *refs):
    weights, (whole_ref, *part_refs, whole_s, in_sems, out_sems) = refs[:count], refs[count:]
    run_copies(side_by_side(weights, whole_s.shape[0], whole_s), in_sems)
    rows = part_refs[0].shape[0]
    starts = (pl.multiple_of(ids_ref[bit] * rows, rows), 2 * rows)
    parts = [(whole_s.at[pl.ds(a, ref.shape[0]), :], ref) for a, ref in zip(starts, part_refs)]
    run_copies(parts + [(whole_s, whole_ref)], out_sems)


def self_forward(
    ids_ref, w0, w1, w2, w3,
    x_ref, states_ref, normed_ref, q_ref, kv_ref, pa_ref, pb_ref, mixed_ref, aux_ref,
    w_s, bias_a, bias_b, table_s,
):
    f = ids_ref[0]
    length, width = x_ref.shape
    inner = H * DH
    enc = states_ref.shape[0] // GROUP
    after_weights = width + w_s.shape[1]
    columns = width * enc // w0.shape[0]
    for k, piece in enumerate((w0, w1, w2, w3)):
        x_ref[own(f ^ k, w0.shape[0]), :] = piece[:, :width]
        w_s[own(f ^ k, w0.shape[0]), :] = piece[:, width:after_weights]
        for i in range(width // columns):
            states_ref[own(f ^ k, enc), i * columns : (i + 1) * columns] = (
                piece[i * enc : (i + 1) * enc, after_weights : after_weights + columns]
            )
        small = piece[0:16, after_weights + columns :].astype(F32)
        aux_ref[:, own(f ^ k, BLOCK)] = small[0:8, :]
        table_s[own(f ^ k, 8), :] = small[8:16, :]
    for hb in range(length // HALF):
        at = slice(hb * HALF, (hb + 1) * HALF)
        x = x_ref[at, :].astype(F32)
        normed = (x * rms(x) * aux_ref[0:1, :]).astype(BF16)
        normed_ref[at, :] = normed
        kv_ref[at, :] = dot(normed, w_s[:, inner:]).astype(BF16)
    q_ref[...] = dot(place_mine(normed_ref, f), w_s[:, :inner]).astype(BF16)
    per_offset = lax.dot_general(
        table_s[...], offset_onehot(BUCKETS, 1), (((0,), (0,)), ((), ())),
        precision=HIGHEST, preferred_element_type=F32,
    )
    first, second = my_blocks(f)
    row = lax.broadcasted_iota(jnp.int32, (BLOCK, 2 * BLOCK), 0)
    col = lax.broadcasted_iota(jnp.int32, (BLOCK, 2 * BLOCK), 1)
    lane = lax.broadcasted_iota(jnp.int32, (BLOCK, length), 1)
    is_far = lane < (second - 1) * BLOCK
    bias_a[:, :, 2 * BLOCK :] = jnp.full((PAIRS, 2 * BLOCK, BLOCK), MASKED, F32)
    for h in range(H):
        at = slice((h % 2) * BLOCK, (h % 2 + 1) * BLOCK)
        spread = jnp.broadcast_to(per_offset[h : h + 1, :], (BLOCK, 4 * BLOCK))
        skewed = pltpu.roll(spread, 0, 1, stride=1, stride_axis=0)[:, : 2 * BLOCK]
        band = jnp.where(col - BLOCK > row, MASKED, skewed)
        bias_a[h // 2, at, pl.ds(pl.multiple_of(first * BLOCK, BLOCK), 2 * BLOCK)] = band
        bias_b[h // 2, at, :] = jnp.where(is_far, per_offset[h : h + 1, 0:1], MASKED)
        bias_b[h // 2, at, pl.ds(pl.multiple_of((second - 1) * BLOCK, BLOCK), 2 * BLOCK)] = band
    for p in range(PAIRS):
        lanes = slice(p * BLOCK, (p + 1) * BLOCK)
        k2 = kv_ref[:, lanes]
        v2 = kv_ref[:, inner + p * BLOCK : inner + (p + 1) * BLOCK]
        for slot in range(2):
            at = slice(slot * BLOCK, (slot + 1) * BLOCK)
            bias = bias_a[p, :, BLOCK:] if slot == 0 else bias_b[p]
            seen = bias.shape[1]
            s = dot_t(stack_heads(q_ref[at, lanes]), k2[:seen, :]) + bias
            probs = softmax(s).astype(BF16)
            (pa_ref, pb_ref)[slot][p] = probs
            mixed_ref[at, lanes] = unstack_heads(dot(probs, v2[:seen, :])).astype(BF16)


def place_cross(w_s, outs_s, pieces, f, half):
    first = w_s.shape[1]
    own_rows = pieces[0].shape[0]
    for owner, start, rows, piece in split_pieces(pieces, f, half):
        place_rows_of(w_s, owner * own_rows + start, rows, piece[:, :first])
        for b in range(outs_s.shape[0] // own_rows):
            to = pl.ds(pl.multiple_of(b * own_rows + start, 16), rows)
            outs_s[to, own(owner, BLOCK)] = piece[:, first + b * BLOCK : first + (b + 1) * BLOCK]


def cross_forward(
    ids_ref, x_ref, mixed_ref, aux_ref,
    w0, w1, w2, w3, w4, w5, states_s,
    h1_ref, n2_ref, cq_ref, ckv_ref, probs_ref, cmixed_ref, h2_ref, n3_ref,
    w_s, outs_s,
):
    f = ids_ref[0]
    inner = H * DH
    half = ids_ref[4]
    place_cross(w_s, outs_s, (w0, w1, w2, w3, w4, w5), f, half)
    hidden = place_mine(x_ref, f).astype(F32) + dot(mixed_ref[...], outs_s[:inner, :])
    h1_ref[...] = hidden
    normed = (hidden * rms(hidden) * aux_ref[1:2, :]).astype(BF16)
    n2_ref[...] = normed
    cq_ref[...] = dot(normed, w_s[:, :inner]).astype(BF16)
    ckv_ref[...] = dot(states_s[...], w_s[:, inner:]).astype(BF16)
    for p in range(PAIRS):
        lanes = slice(p * BLOCK, (p + 1) * BLOCK)
        v2 = ckv_ref[:, inner + p * BLOCK : inner + (p + 1) * BLOCK]
        probs = softmax(dot_t(stack_heads(cq_ref[:, lanes]), ckv_ref[:, lanes])).astype(BF16)
        probs_ref[p] = probs
        cmixed_ref[:, lanes] = unstack_heads(dot(probs, v2)).astype(BF16)
    hidden = h1_ref[...] + dot(cmixed_ref[...], outs_s[inner:, :])
    h2_ref[...] = hidden
    n3_ref[...] = (hidden * rms(hidden) * aux_ref[2:3, :]).astype(BF16)


def feed_forward(
    ids_ref, h2_ref, n3_ref, aux_ref,
    g0, g1, g2, g3, g4, g5, g6, g7, c0, c1, c2, c3,
    result_ref, grad_h2_ref, keep_ref, send_ref, gain_ref,
    gu_s, down_s, cot_s, cot_mine, units_s, gate_s, up_s, chip_s, down_chip_s,
):
    f, orders = ids_ref[0], (ids_ref[1], ids_ref[3])
    chip = f >> 1
    mine_rows, width = h2_ref.shape
    rows = cot_s.shape[0] // GROUP
    hidden_units = down_s.shape[0]
    own_units = hidden_units // GROUP
    half = ids_ref[2]
    own_rows = g0.shape[0]
    for owner, start, size, piece in split_pieces((g0, g1, g2, g3, g4, g5, g6, g7), f, half):
        place_rows_of(gu_s, owner * own_rows + start, size, piece[:, : 2 * hidden_units])
        for b in range(own_units // own_rows):
            first = 2 * hidden_units + b * width
            place_rows_of(down_s, owner * own_units + b * own_rows + start, size, piece[:, first : first + width])
    place_rows(cot_s, (c0, c1, c2, c3), f, 0, rows)
    cot_mine[...] = place_mine(cot_s, f)
    grad_normed = jnp.zeros((mine_rows, width), F32)
    chunk = 256
    for c in range(hidden_units // chunk):
        gate_at, up_at = slice(c * chunk, (c + 1) * chunk), slice(hidden_units + c * chunk, hidden_units + (c + 1) * chunk)
        gate, up = dot(n3_ref[...], gu_s[:, gate_at]), dot(n3_ref[...], gu_s[:, up_at])
        grad_units = dot_t(cot_mine[...], down_s[gate_at, :])
        square = gate * gate
        tanh = jnp.tanh(0.7978845608028654 * (gate + 0.044715 * square * gate))
        half_gate = 0.5 * gate
        gelu = half_gate + half_gate * tanh
        slope = 0.5 + 0.5 * tanh + half_gate * (1.0 - tanh * tanh) * (
            0.7978845608028654 + (3 * 0.044715 * 0.7978845608028654) * square
        )
        units_s[:, gate_at] = (gelu * up).astype(BF16)
        grad_gate = (grad_units * up * slope).astype(BF16)
        grad_up = (grad_units * gelu).astype(BF16)
        gate_s[:, gate_at] = grad_gate
        up_s[:, gate_at] = grad_up
        grad_normed = grad_normed + dot_t(grad_gate, gu_s[:, gate_at]) + dot_t(grad_up, gu_s[:, up_at])
    piece, gain_part = norm_back(h2_ref[...], aux_ref[2:3, :], grad_normed)
    grad_h2_ref[...] = cot_mine[...].astype(F32) + piece
    gain_ref[...] = jnp.broadcast_to(jnp.sum(gain_part, axis=0, keepdims=True), gain_ref.shape)
    mine = own(chip, rows)
    result_ref[...] = (h2_ref[mine, :] + dot(units_s[mine, :], down_s[...])).astype(BF16)
    chip_rows = 2 * g0.shape[0]
    normed_chip = n3_ref[:, own(chip, chip_rows)]
    chip_s[:, :hidden_units] = t_dot(normed_chip, gate_s[...]).astype(BF16)
    chip_s[:, hidden_units:] = t_dot(normed_chip, up_s[...]).astype(BF16)
    emit(keep_ref, send_ref, chip_s, 0, f, orders)
    grad_down = t_dot(units_s[:, own(chip, 2 * own_units)], cot_mine[...]).astype(BF16)
    parts = own_units // g0.shape[0]
    for which in range(2):
        for part in range(parts):
            at = slice((which * parts + part) * g0.shape[0], (which * parts + part + 1) * g0.shape[0])
            down_chip_s[which * g0.shape[0] : (which + 1) * g0.shape[0], part * width : (part + 1) * width] = grad_down[at, :]
    emit(keep_ref, send_ref, down_chip_s, 2 * hidden_units, f, orders)


def put_columns(chip_s, first, grad, own_rows):
    columns = grad.shape[1] // 2
    for which in range(2):
        for part in range(grad.shape[0] // own_rows):
            chip_s[which * own_rows : (which + 1) * own_rows, first + part * columns : first + (part + 1) * columns] = (
                grad[part * own_rows : (part + 1) * own_rows, which * columns : (which + 1) * columns]
            )


def cross_backward(
    ids_ref, grad_h2_ref, h1_ref, n2_ref, cq_ref, ckv_ref, probs_ref, cmixed_ref, mixed_ref, aux_ref,
    w0, w1, w2, w3, w4, w5, states_s,
    grad_h1_ref, mix_ref, states_keep, states_send, keep_ref, send_ref, gain_ref,
    w_s, outs_s, low_s, dq_s, dkv_s, chip_s, states_chip,
):
    f, orders = ids_ref[0], (ids_ref[1], ids_ref[3])
    chip, core = f >> 1, f & 1
    inner = H * DH
    own_rows = w0.shape[0]
    chip_columns = own(chip, 2 * own_rows)
    half = ids_ref[4]
    place_cross(w_s, outs_s, (w0, w1, w2, w3, w4, w5), f, half)
    low = grad_h2_ref[...].astype(BF16)
    low_s[...] = low
    grad_mixed = dot_t(low, outs_s[inner:, :]).astype(BF16)
    put_columns(chip_s, 3 * inner, t_dot(cmixed_ref[...], low_s[:, chip_columns]).astype(BF16), own_rows)
    for p in range(PAIRS):
        lanes = slice(p * BLOCK, (p + 1) * BLOCK)
        v_lanes = slice(inner + p * BLOCK, inner + (p + 1) * BLOCK)
        stacked = stack_heads(grad_mixed[:, lanes])
        probs = probs_ref[p].astype(F32)
        weighted = probs * dot_t(stacked, ckv_ref[:, v_lanes])
        ds = (weighted - probs * jnp.sum(weighted, axis=-1, keepdims=True)).astype(BF16)
        dq_s[:, lanes] = unstack_heads(dot(ds, ckv_ref[:, lanes])).astype(BF16)
        dkv_s[:, lanes] = t_dot(ds, stack_heads(cq_ref[:, lanes])).astype(BF16)
        dkv_s[:, v_lanes] = t_dot(probs_ref[p], stacked).astype(BF16)
    grad_normed = dot_t(dq_s[...], w_s[:, :inner])
    piece, gain_part = norm_back(h1_ref[...], aux_ref[1:2, :], grad_normed)
    grad_h1 = grad_h2_ref[...] + piece
    grad_h1_ref[...] = grad_h1
    gain_ref[...] = jnp.broadcast_to(jnp.sum(gain_part, axis=0, keepdims=True), gain_ref.shape)
    low = grad_h1.astype(BF16)
    low_s[...] = low
    mix_ref[...] = dot_t(low, outs_s[:inner, :]).astype(BF16)
    put_columns(chip_s, 4 * inner, t_dot(mixed_ref[...], low_s[:, chip_columns]).astype(BF16), own_rows)
    chip_s[:, :inner] = t_dot(n2_ref[:, chip_columns], dq_s[...]).astype(BF16)
    chip_s[:, inner : 3 * inner] = t_dot(states_s[:, chip_columns], dkv_s[...]).astype(BF16)
    emit(keep_ref, send_ref, chip_s, 0, f, orders)
    enc = states_s.shape[0] // GROUP
    states_chip[...] = dot_t(dkv_s[own(chip, 2 * enc), :], w_s[:, inner:])
    states_keep[...] = states_chip[own(core, enc), :]
    states_send[...] = states_chip[own(1 - core, enc), :]


def self_backward(ids_ref, mix_ref, q_ref, kv_ref, pa_ref, pb_ref, dq_s, dkv_s, table_s, ds_a, ds_b):
    inner = H * DH
    first, second = my_blocks(ids_ref[0])
    row = lax.broadcasted_iota(jnp.int32, (2 * BLOCK, 4 * BLOCK), 0)
    ds_a[:, 0:BLOCK] = jnp.zeros((2 * BLOCK, BLOCK), F32)
    offset_sums, far_sums = [], []
    for p in range(PAIRS):
        lanes = slice(p * BLOCK, (p + 1) * BLOCK)
        v_lanes = slice(inner + p * BLOCK, inner + (p + 1) * BLOCK)
        k2, v2 = kv_ref[:, lanes], kv_ref[:, v_lanes]
        dk, dv = [], []
        for slot in range(2):
            at = slice(slot * BLOCK, (slot + 1) * BLOCK)
            probs_low = (pa_ref, pb_ref)[slot][p]
            seen = probs_low.shape[1]
            stacked = stack_heads(mix_ref[at, lanes])
            probs = probs_low.astype(F32)
            weighted = probs * dot_t(stacked, v2[:seen, :])
            ds = weighted - probs * jnp.sum(weighted, axis=-1, keepdims=True)
            if slot == 0:
                ds_a[:, BLOCK:] = ds
            else:
                ds_b[...] = ds
            low = ds.astype(BF16)
            dq_s[at, lanes] = unstack_heads(dot(low, k2[:seen, :])).astype(BF16)
            dk.append(t_dot(low, stack_heads(q_ref[at, lanes])))
            dv.append(t_dot(probs_low, stacked))
        for total, to in ((dk, lanes), (dv, v_lanes)):
            seen = total[0].shape[0]
            dkv_s[:seen, to] = (total[0] + total[1][:seen, :]).astype(BF16)
            dkv_s[seen:, to] = total[1][seen:, :].astype(BF16)
        band_b = ds_b[:, pl.ds(pl.multiple_of((second - 1) * BLOCK, BLOCK), 2 * BLOCK)]
        band_a = ds_a[:, pl.ds(pl.multiple_of(first * BLOCK, BLOCK), 2 * BLOCK)]
        far = jnp.sum(ds_b[...], axis=1, keepdims=True) - jnp.sum(band_b, axis=1, keepdims=True)
        skew = jnp.concatenate([band_a + band_b, jnp.zeros((2 * BLOCK, 2 * BLOCK), F32)], axis=1)
        for bit in range(BLOCK.bit_length() - 1):
            moved = pltpu.roll(skew, 4 * BLOCK - (1 << bit), 1)
            skew = jnp.where((row & (1 << bit)) != 0, moved, skew)
        for hd in range(2):
            at = slice(hd * BLOCK, (hd + 1) * BLOCK)
            offset_sums.append(jnp.sum(skew[at, :], axis=0, keepdims=True))
            far_sums.append(jnp.sum(far[at, :], axis=0, keepdims=True))
    per_offset = jnp.concatenate(offset_sums + [jnp.zeros((BLOCK - H, 4 * BLOCK), F32)], axis=0)
    far_all = jnp.concatenate(far_sums + [jnp.zeros((BLOCK - H, 1), F32)], axis=0)
    per_offset = per_offset + jnp.where(
        lax.broadcasted_iota(jnp.int32, (BLOCK, 4 * BLOCK), 1) == 0, far_all, 0.0
    )
    table_s[...] = lax.dot_general(
        offset_onehot(BLOCK, 1), per_offset, (((1,), (1,)), ((), ())),
        precision=HIGHEST, preferred_element_type=F32,
    )


def self_gradients(
    ids_ref, grad_h1_ref, x_ref, normed_ref, aux_ref, gain2_ref, gain3_ref, dq_s, dkv_s, table_s, w0, w1, w2, w3,
    tokens_keep, tokens_send, keep_ref, send_ref,
    w_s, chip_s, small_s, gain_s,
):
    f, orders = ids_ref[0], (ids_ref[1] & SELF_ORDER, ids_ref[3] & SELF_ORDER)
    chip = f >> 1
    length, width = x_ref.shape
    rows = length // GROUP
    inner = H * DH
    own_rows = w0.shape[0]
    chip_columns = own(chip, 2 * own_rows)
    first, second = my_blocks(f)
    for k, piece in enumerate((w0, w1, w2, w3)):
        w_s[own(f ^ k, own_rows), :] = piece[:, width : width + 3 * inner]
    gain = aux_ref[0:1, :]
    mine, block = own(chip, rows), own(f, rows)
    others = own(f ^ 1, rows)
    grad_normed = dot_t(dq_s[mine, :], w_s[:, :inner]) + dot_t(dkv_s[block, :], w_s[:, inner:])
    piece, _ = norm_back(x_ref[block, :].astype(F32), gain, grad_normed)
    tokens_keep[...] = grad_h1_ref[mine, :] + piece
    piece, _ = norm_back(x_ref[others, :].astype(F32), gain, dot_t(dkv_s[others, :], w_s[:, inner:]))
    tokens_send[...] = piece
    chip_w = w_s[chip_columns, :]
    gain_sum = jnp.zeros((1, 2 * own_rows), F32)
    for hb in range(length // HALF):
        at = slice(hb * HALF, (hb + 1) * HALF)
        scaled = x_ref[at, chip_columns].astype(F32) * rms(x_ref[at, :].astype(F32))
        gain_sum = gain_sum + jnp.sum(dot_t(dkv_s[at, :], chip_w[:, inner:]) * scaled, axis=0, keepdims=True)
    grad_q = dot_t(dq_s[...], chip_w[:, :inner])
    for slot, b in enumerate((first, second)):
        scaled = x_ref[own(b, BLOCK), chip_columns].astype(F32) * rms(x_ref[own(b, BLOCK), :].astype(F32))
        gain_sum = gain_sum + jnp.sum(grad_q[slot * BLOCK : (slot + 1) * BLOCK, :] * scaled, axis=0, keepdims=True)
    normed_mine = jnp.concatenate([normed_ref[own(b, BLOCK), chip_columns] for b in (first, second)], axis=0)
    chip_s[:, :inner] = t_dot(normed_mine, dq_s[...]).astype(BF16)
    chip_s[:, inner:] = t_dot(normed_ref[:, chip_columns], dkv_s[...]).astype(BF16)
    emit(keep_ref, send_ref, chip_s, 0, f, orders)
    gain_s[0:8, :] = gain2_ref[...]
    gain_s[8:16, :] = gain3_ref[...]
    buckets = BUCKETS // GROUP
    for which in range(2):
        owner = 2 * chip + which
        small = jnp.concatenate(
            [
                table_s[own(owner, buckets), :],
                gain_sum[:, which * own_rows : (which + 1) * own_rows],
                gain_s[0:1, own(owner, own_rows)],
                gain_s[8:9, own(owner, own_rows)],
                jnp.zeros((own_rows - buckets - 3, BLOCK), F32),
            ],
            axis=0,
        )
        small_s[which * own_rows : (which + 1) * own_rows, :] = small.astype(BF16)
    emit(keep_ref, send_ref, small_s, 3 * inner, f, orders)


def fold(keep_ref, arrived_ref, *out_refs):
    total = (keep_ref[...].astype(F32) + arrived_ref[...].astype(F32)).astype(BF16)
    rows = total.shape[0] // len(out_refs)
    for i, ref in enumerate(out_refs):
        ref[...] = total[i * rows : (i + 1) * rows, :]


def pieces_of(ids_ref, halves, mask=PIECES - 1):
    order = ids_ref[1] & mask
    for i, half in enumerate(halves):
        piece = half.shape[0] * len(halves) // PIECES
        here = PIECES // len(halves)
        for j in range(here):
            q = (i * here + j) ^ order
            yield q * piece, piece, half[j * piece : (j + 1) * piece, :].astype(F32)


def unpack_feed(ids_ref, low_ref, high_ref, gate_ref, up_ref, down_ref):
    units, width, own_rows = gate_ref.shape[1], down_ref.shape[1], gate_ref.shape[0]
    for at, size, rows in pieces_of(ids_ref, (low_ref, high_ref)):
        to = pl.ds(pl.multiple_of(at, size), size)
        gate_ref[to, :] = rows[:, :units]
        up_ref[to, :] = rows[:, units : 2 * units]
        for part in range(down_ref.shape[0] // own_rows):
            first = 2 * units + part * width
            down_ref[pl.ds(pl.multiple_of(part * own_rows + at, size), size), :] = rows[:, first : first + width]


def unpack_cross(ids_ref, low_ref, high_ref, cq_ref, ck_ref, cv_ref, co_ref, out_ref):
    own_rows, inner = cq_ref.shape
    for at, size, rows in pieces_of(ids_ref, (low_ref, high_ref)):
        to = pl.ds(pl.multiple_of(at, size), size)
        for i, ref in enumerate((cq_ref, ck_ref, cv_ref)):
            ref[to, :] = rows[:, i * inner : (i + 1) * inner]
        for i, ref in enumerate((co_ref, out_ref)):
            columns = ref.shape[1]
            for part in range(inner // own_rows):
                first = (3 + i) * inner + part * columns
                ref[pl.ds(pl.multiple_of(part * own_rows + at, size), size), :] = rows[:, first : first + columns]


def unpack_self(ids_ref, low_ref, high_ref, q_ref, k_ref, v_ref, g1_ref, g2_ref, g3_ref, table_ref, small_s):
    inner = q_ref.shape[1]
    for at, size, rows in pieces_of(ids_ref, (low_ref, high_ref), SELF_ORDER):
        to = pl.ds(pl.multiple_of(at, size), size)
        for i, ref in enumerate((q_ref, k_ref, v_ref)):
            ref[to, :] = rows[:, i * inner : (i + 1) * inner]
        small_s[to, :] = rows[:, 3 * inner :]
    buckets, heads = table_ref.shape
    table_ref[...] = small_s[0:buckets, 0:heads]
    for i, ref in enumerate((g1_ref, g2_ref, g3_ref)):
        ref[...] = small_s[buckets + i : buckets + i + 1, :]


VMEM = pl.BlockSpec(memory_space=pltpu.VMEM)
SMEM = pl.BlockSpec(memory_space=pltpu.SMEM)


def call(kernel, name, out_shapes, scratch, args, with_ids=True, place=VMEM):
    return pl.pallas_call(
        kernel,
        name=name,
        out_shape=[jax.ShapeDtypeStruct(s, d) for s, d in out_shapes],
        in_specs=([SMEM] if with_ids else []) + [place] * (len(args) - with_ids),
        out_specs=[place] * len(out_shapes),
        scratch_shapes=[pltpu.VMEM(*s) if isinstance(s, tuple) else s for s in scratch],
        compiler_params=pltpu.CompilerParams(vmem_limit_bytes=VMEM_BYTES if place is VMEM else 56 * 1024 * 1024),
        cost_estimate=pl.CostEstimate(flops=1, bytes_accessed=1, transcendentals=0),
    )(*args)


def hop(x, axis, bits):
    size = lax.axis_size(axis)
    return lax.ppermute(x, axis, [(i, i ^ bits) for i in range(size)])


def all_after(arrays, earlier):
    return lax.optimization_barrier((tuple(arrays), tuple(earlier)))[0]


def beside(pack, far):
    return pack, hop(pack, "fsdp", 1), far, hop(far, "fsdp", 1)


def beside_split(pack, far, far_other, *rest):
    parts = (far, far_other, *rest)
    return pack, hop(pack, "fsdp", 1), *parts, *(hop(a, "fsdp", 1) for a in parts)


def rep_hop(x, bits):
    replicas, group = lax.axis_size("rep"), lax.axis_size("fsdp")
    pairs = [(r * group + f, (r ^ bits[f & 1]) * group + f) for r in range(replicas) for f in range(group)]
    return lax.ppermute(x, ("rep", "fsdp"), pairs)


class Sum:
    def __init__(self, name, keep, send, halvings):
        bits = (lax.axis_size("rep") - 1).bit_length()
        self.name, self.keep, self.at = name, keep, 0
        self.arrived = hop(send, "fsdp", 1)
        self.steps = [(1, 2), (2, 1)] + [(1 << i, 1 << i) for i in range(2, bits)]
        self.back = self.steps[:halvings]
        self.halvings = halvings

    def fold(self, earlier):
        keep, arrived = all_after((self.keep, self.arrived), earlier)
        halving = self.at < self.halvings
        total = (keep.astype(F32) + arrived.astype(F32)).astype(BF16)
        middle = total.shape[0] // 2
        out = (total[:middle], total[middle:]) if halving else (total,)
        self.keep = out[0]
        if self.at < len(self.steps):
            self.arrived = rep_hop(out[-1], self.steps[self.at])
        else:
            self.arrived = rep_hop(self.keep, self.back[-1])
        self.at += 1
        return self.keep

    def widen(self, earlier):
        keep, arrived = all_after((self.keep, self.arrived), earlier)
        self.back.pop()
        self.keep = jnp.concatenate((keep, arrived))
        self.arrived = rep_hop(self.keep, self.back[-1])
        return self.keep

    def halves(self, earlier):
        return all_after((self.keep, self.arrived), earlier)

    def actions(self):
        return [self.fold] * (len(self.steps) + 1 - self.at) + [self.widen] * (len(self.back) - 1)


def per_device(
    tokens,
    states,
    query_w,
    key_w,
    value_w,
    out_w,
    cross_query_w,
    cross_key_w,
    cross_value_w,
    cross_out_w,
    gate_w,
    up_w,
    down_w,
    self_gain,
    cross_gain,
    mlp_gain,
    bias_table,
    cotangent,
):
    seq_count, rows, width = tokens.shape
    enc = states.shape[1]
    own_rows, inner = query_w.shape
    hidden_units = gate_w.shape[1]
    length, enc_all, mine = rows * GROUP, enc * GROUP, 2 * BLOCK
    f = lax.axis_index("fsdp").astype(jnp.int32)
    replica = lax.axis_index("rep").astype(jnp.int32)
    order_0 = ((replica & 1) << 1) | ((replica >> 1) & 1)
    order_1 = replica & 3
    core = f & 1
    ids = jnp.stack(
        [f, jnp.where(core == 0, order_0, order_1), replica & 1, jnp.where(core == 0, order_1, order_0), (replica >> 1) & 1]
    )

    hbm = pl.BlockSpec(memory_space=pl.ANY)
    first_columns = width + 3 * inner + enc * width // rows + BLOCK
    (first_pack,) = call(
        pack_first,
        "pack_first",
        [((rows, first_columns), BF16)],
        [
            ((rows, first_columns), BF16),
            ((1, own_rows), BF16),
            ((1, own_rows), BF16),
            ((1, own_rows), BF16),
            (bias_table.shape, BF16),
            ((16, BLOCK), F32),
            pltpu.SemaphoreType.DMA((8 + rows // enc,)),
        ],
        [tokens[0], query_w, key_w, value_w, states[0], self_gain[None], cross_gain[None], mlp_gain[None], bias_table],
        False,
        hbm,
    )
    (second_ids,) = all_after((ids,), (first_pack,))

    def packed(name, ids, weights, parts, bit):
        columns = sum(w.size for w in weights) // own_rows
        return call(
            functools.partial(pack_weights, len(weights), bit),
            name,
            [((rows, columns), BF16) for rows in (own_rows, *parts)],
            [
                ((own_rows, columns), BF16),
                pltpu.SemaphoreType.DMA((sum(w.shape[0] for w in weights) // own_rows,)),
                pltpu.SemaphoreType.DMA((1 + len(parts),)),
            ],
            [ids, *weights],
            place=hbm,
        )

    second_pack, second_half = packed(
        "pack_second", second_ids, [cross_query_w, cross_key_w, cross_value_w, out_w, cross_out_w], [own_rows // 2], 4
    )
    (third_ids,) = all_after((ids,), (second_pack,))
    part = 3 * own_rows // 8
    third_pack, third_part, third_rest = packed(
        "pack_third", third_ids, [gate_w, up_w, down_w], [part, own_rows - 2 * part], 2
    )
    first_far, second_far = hop(first_pack, "fsdp", 2), hop(second_half, "fsdp", 2)
    (first_far,) = all_after((first_far,), (third_pack,))
    first_packs = beside(first_pack, first_far)

    x, states_all, normed_one, q, kv, probs_a, probs_b, mixed, aux = call(
        self_forward,
        "self_forward",
        [
            ((length, width), BF16),
            ((enc_all, width), BF16),
            ((length, width), BF16),
            ((mine, inner), BF16),
            ((length, 2 * inner), BF16),
            ((PAIRS, 2 * BLOCK, 2 * BLOCK), BF16),
            ((PAIRS, 2 * BLOCK, length), BF16),
            ((mine, inner), BF16),
            ((8, width), F32),
        ],
        [
            ((width, 3 * inner), BF16),
            ((PAIRS, 2 * BLOCK, 3 * BLOCK), F32),
            ((PAIRS, 2 * BLOCK, length), F32),
            ((BUCKETS, BLOCK), F32),
        ],
        [ids, *first_packs],
    )
    (cot_own,) = all_after((cotangent[0],), (first_far,))
    second_far, second_pack, third_pack, third_part, third_rest = all_after(
        (second_far, second_pack, third_pack, third_part, third_rest), (aux,)
    )
    third_far = hop(third_part, "fsdp", 2)
    second_other = hop(second_far, "rep", 2)
    rest_far = hop(third_rest, "fsdp", 2)
    cot_far = hop(cot_own, "fsdp", 2)
    seconds = beside_split(second_pack, second_far, second_other)
    cots = beside(cot_own, cot_far)
    (cross_ids,) = all_after((ids,), (third_far, cots[3]))
    hidden_one, normed_two, cross_q, cross_kv, cross_probs, cross_mixed, hidden_two, normed_three = call(
        cross_forward,
        "cross_forward",
        [
            ((mine, width), F32),
            ((mine, width), BF16),
            ((mine, inner), BF16),
            ((enc_all, 2 * inner), BF16),
            ((PAIRS, 2 * mine, enc_all), BF16),
            ((mine, inner), BF16),
            ((mine, width), F32),
            ((mine, width), BF16),
        ],
        [
            ((width, 3 * inner), BF16),
            ((2 * inner, width), BF16),
        ],
        [cross_ids, x, mixed, aux, *seconds, states_all],
    )
    third_other = hop(third_far, "rep", 1)
    third_far, third_other, rest_far = all_after((third_far, third_other, rest_far), (normed_three,))
    thirds = beside_split(third_pack, third_far, third_other, rest_far)
    down_columns = down_w.size // own_rows
    result, grad_hidden_two, ff_keep, ff_send, mlp_gain_sum = call(
        feed_forward,
        "feed_forward",
        [
            ((rows, width), BF16),
            ((mine, width), F32),
            ((own_rows, 2 * hidden_units + down_columns), BF16),
            ((own_rows, 2 * hidden_units + down_columns), BF16),
            ((8, width), F32),
        ],
        [
            ((width, 2 * hidden_units), BF16),
            ((hidden_units, width), BF16),
            ((length, width), BF16),
            ((mine, width), BF16),
            ((mine, hidden_units), BF16),
            ((mine, hidden_units), BF16),
            ((mine, hidden_units), BF16),
            ((2 * own_rows, 2 * hidden_units), BF16),
            ((2 * own_rows, down_columns), BF16),
        ],
        [ids, hidden_two, normed_three, aux, *thirds, *cots],
    )
    ff_sum = Sum("feed", ff_keep, ff_send, 2)
    grad_hidden_one, grad_mixed, states_keep, states_send, cross_keep, cross_send, cross_gain_sum = call(
        cross_backward,
        "cross_backward",
        [
            ((mine, width), F32),
            ((mine, inner), BF16),
            ((enc, width), F32),
            ((enc, width), F32),
            ((own_rows, 5 * inner), BF16),
            ((own_rows, 5 * inner), BF16),
            ((8, width), F32),
        ],
        [
            ((width, 3 * inner), BF16),
            ((2 * inner, width), BF16),
            ((mine, width), BF16),
            ((mine, inner), BF16),
            ((enc_all, 2 * inner), BF16),
            ((2 * own_rows, 5 * inner), BF16),
            ((2 * enc, width), F32),
        ],
        [
            ids, grad_hidden_two, hidden_one, normed_two, cross_q, cross_kv, cross_probs, cross_mixed, mixed,
            aux, *seconds, states_all,
        ],
    )
    cross_sum = Sum("cross", cross_keep, cross_send, 2)
    sums = {"F": ff_sum, "C": cross_sum}
    done = ff_sum.fold((grad_hidden_one,))
    (grad_mixed,) = all_after((grad_mixed,), (done,))
    grad_q, grad_kv, table_sums = call(
        self_backward,
        "self_backward",
        [((mine, inner), BF16), ((length, 2 * inner), BF16), ((BLOCK, BLOCK), F32)],
        [((2 * BLOCK, 3 * BLOCK), F32), ((2 * BLOCK, length), F32)],
        [ids, grad_mixed, q, kv, probs_a, probs_b],
    )
    done = grad_q
    for turn in EARLY:
        done = sums[turn].fold((done,))
    done = cross_sum.fold((done,))
    (late_ids,) = all_after((ids,), (done,))
    tokens_keep, tokens_send, self_keep, self_send = call(
        self_gradients,
        "self_gradients",
        [
            ((rows, width), F32),
            ((rows, width), F32),
            ((own_rows, 3 * inner + BLOCK), BF16),
            ((own_rows, 3 * inner + BLOCK), BF16),
        ],
        [
            ((width, 3 * inner), BF16),
            ((2 * own_rows, 3 * inner), BF16),
            ((2 * own_rows, BLOCK), BF16),
            ((16, width), F32),
        ],
        [
            late_ids, grad_hidden_one, x, normed_one, aux, cross_gain_sum, mlp_gain_sum,
            grad_q, grad_kv, table_sums, *first_packs,
        ],
    )
    done = tokens_keep
    for turn in TURNS:
        if turn == "X":
            self_keep, self_send = all_after((self_keep, self_send), (done,))
            self_sum = sums["S"] = Sum("self", self_keep, self_send, SELF_HALVINGS)
        elif turn == "T":
            states_send, tokens_send = all_after((states_send, tokens_send), (done,))
            grad_states = states_keep + hop(states_send, "fsdp", 1)
            grad_tokens = tokens_keep + hop(tokens_send, "fsdp", 1)
        elif sums[turn].actions():
            done = sums[turn].actions()[0]((done,))
    while any(part.actions() for part in sums.values()):
        for part in sums.values():
            done = part.actions()[0]((done,)) if part.actions() else done
    grad_gate, grad_up, grad_down = call(
        unpack_feed,
        "unpack_feed",
        [(gate_w.shape, F32), (up_w.shape, F32), (down_w.shape, F32)],
        [],
        [ids, *ff_sum.halves((done,))],
    )
    grad_cross_query, grad_cross_key, grad_cross_value, grad_cross_out, grad_out = call(
        unpack_cross,
        "unpack_cross",
        [(query_w.shape, F32)] * 3 + [(out_w.shape, F32)] * 2,
        [],
        [ids, *cross_sum.halves((grad_gate,))],
    )
    grad_query, grad_key, grad_value, grad_g1, grad_g2, grad_g3, grad_table = call(
        unpack_self,
        "unpack_self",
        [(query_w.shape, F32)] * 3 + [((1, own_rows), F32)] * 3 + [(bias_table.shape, F32)],
        [((own_rows, BLOCK), F32)],
        [ids, *self_sum.halves((grad_cross_query,))],
    )
    return (
        result[None],
        grad_tokens[None],
        grad_states[None],
        grad_query,
        grad_key,
        grad_value,
        grad_out,
        grad_cross_query,
        grad_cross_key,
        grad_cross_value,
        grad_cross_out,
        grad_gate,
        grad_up,
        grad_down,
        grad_g1[0],
        grad_g2[0],
        grad_g3[0],
        grad_table,
    )


def solution(mesh):
    whole = P("rep", "fsdp", None)
    rows, columns, vector = P("fsdp", None), P(None, "fsdp"), P("fsdp")
    weights = (rows, rows, rows, columns, rows, rows, rows, columns, rows, rows, rows)
    small = (vector, vector, vector, rows)
    return jax.shard_map(
        per_device,
        mesh=mesh,
        in_specs=(whole, whole) + weights + small + (whole,),
        out_specs=(whole, whole, whole) + weights + small,
        check_vma=False,
    )
```

```python
import functools
import itertools
import math

import jax
import jax.numpy as jnp
from jax import lax
from jax.experimental import pallas as pl
from jax.experimental.pallas import tpu as pltpu
from jax.sharding import PartitionSpec as P

H = 6
DH = 64
PAIRS = H // 2
BUCKETS = 32
MAXDIST = 128
EPSILON = 1e-06
MASKED = -1000000000.0
BLOCK = 128
HALF = 256
GROUP = 4
PIECES = 4
EARLY = "F"
TURNS = "XFSCFCSSFTCSCS"
SELF_HALVINGS = 2
SELF_ORDER = PIECES - (PIECES >> SELF_HALVINGS)
VMEM_BYTES = 32 * 1024 * 1024
HIGHEST = lax.Precision.HIGHEST
F32 = jnp.float32
BF16 = jnp.bfloat16


def dot(a, b):
    return jnp.dot(a, b, preferred_element_type=F32)


def dot_t(a, b):
    return lax.dot_general(a, b, (((1,), (1,)), ((), ())), preferred_element_type=F32)


def t_dot(a, b):
    return lax.dot_general(a, b, (((0,), (0,)), ((), ())), preferred_element_type=F32)


def own(f, size):
    return pl.ds(pl.multiple_of(f * size, size), size)


def place_rows(dst, pieces, f, first, size):
    for k, piece in enumerate(pieces):
        dst[own(f ^ k, size), :] = piece[first : first + size, :].astype(dst.dtype)


def place_mine(ref, f):
    return jnp.concatenate([ref[own(b, BLOCK), :] for b in my_blocks(f)], axis=0)


def my_blocks(f):
    a = (f ^ (f >> 1)) & 1
    return a, 3 - a


def split_pieces(pieces, f, half):
    for k, piece in enumerate(pieces[:2]):
        yield f ^ k, 0, piece.shape[0], piece
    parts = (len(pieces) - 2) // 2
    for k in range(2):
        far = pieces[2 + k * parts : 2 + (k + 1) * parts]
        rows = far[0].shape[0]
        for i, start in enumerate((half * rows, (1 - half) * rows, 2 * rows)[:parts]):
            yield f ^ (2 + k), start, far[i].shape[0], far[i]


def place_rows_of(dst, start, size, piece):
    dst[pl.ds(pl.multiple_of(start, 16), size), :] = piece


def bucket_of(distance):
    exact_span = BUCKETS // 2
    bucket = jnp.minimum(distance, exact_span)
    for power in range(1, exact_span):
        threshold = math.ceil(exact_span * (MAXDIST / exact_span) ** (power / exact_span))
        bucket = bucket + (distance >= threshold).astype(jnp.int32)
    return bucket


def offset_onehot(rows, axis):
    shape = (rows, 4 * BLOCK) if axis == 1 else (4 * BLOCK, rows)
    m = lax.broadcasted_iota(jnp.int32, shape, axis)
    n = jnp.where(m < 2 * BLOCK, BLOCK - m, 5 * BLOCK - m)
    bucket = bucket_of(jnp.maximum(n, 0))
    return (bucket == lax.broadcasted_iota(jnp.int32, shape, 1 - axis)).astype(F32)


def rms(v):
    return lax.rsqrt(jnp.mean(v * v, axis=-1, keepdims=True) + EPSILON)


def head_lanes(rows):
    lane = lax.broadcasted_iota(jnp.int32, (rows, 2 * DH), 1)
    return lane < DH


def only_head(pair, hd):
    low = head_lanes(pair.shape[0])
    zero = jnp.zeros_like(pair)
    return jnp.where(low, pair, zero) if hd == 0 else jnp.where(low, zero, pair)


def softmax(s):
    lifted = jnp.exp(s - jnp.max(s, axis=-1, keepdims=True))
    return lifted * (1.0 / jnp.sum(lifted, axis=-1, keepdims=True))


def norm_back(v, gain, q):
    r = rms(v)
    u = q * gain
    vr = v * r
    return r * (u - vr * jnp.mean(vr * u, axis=-1, keepdims=True)), q * vr


def stack_heads(pair):
    low = head_lanes(pair.shape[0])
    zero = jnp.zeros_like(pair)
    return jnp.concatenate([jnp.where(low, pair, zero), jnp.where(low, zero, pair)], axis=0)


def unstack_heads(stacked):
    rows = stacked.shape[0] // 2
    return jnp.where(head_lanes(rows), stacked[:rows, :], stacked[rows:, :])


def emit(keep_ref, send_ref, chip_s, first, f, orders):
    core = f & 1
    rows = keep_ref.shape[0]
    piece = rows // PIECES
    columns = chip_s.shape[1]
    for q in range(PIECES):
        for ref, which, order in ((keep_ref, core, orders[0]), (send_ref, 1 - core, orders[1])):
            to = pl.ds(pl.multiple_of((q ^ order) * piece, piece), piece)
            at = pl.ds(pl.multiple_of(which * rows + q * piece, piece), piece)
            ref[to, first : first + columns] = chip_s[at, :]


def pack_first(
    tokens_ref, q_ref, k_ref, v_ref, states_ref, g1_ref, g2_ref, g3_ref, table_ref,
    pack_ref, pack_s, g1_s, g2_s, g3_s, table_s, wide_s, sems,
):
    rows = pack_s.shape[0]
    pairs = side_by_side((tokens_ref, q_ref, k_ref, v_ref), rows, pack_s)
    first = sum(ref.shape[1] for ref in (tokens_ref, q_ref, k_ref, v_ref))
    enc, columns = states_ref.shape[0], states_ref.shape[1] * states_ref.shape[0] // rows
    for i in range(rows // enc):
        pairs.append((
            states_ref.at[:, i * columns : (i + 1) * columns],
            pack_s.at[i * enc : (i + 1) * enc, first : first + columns],
        ))
    first += columns
    pairs += [(g1_ref, g1_s), (g2_ref, g2_s), (g3_ref, g3_s), (table_ref, table_s)]
    wide_s[...] = jnp.zeros_like(wide_s)
    run_copies(pairs, sems)
    for i, gain in enumerate((g1_s, g2_s, g3_s)):
        wide_s[i : i + 1, :] = gain[...].astype(F32)
    wide_s[8:16, 0 : table_s.shape[1]] = table_s[...].astype(F32)
    pack_s[0:16, first:] = wide_s[...].astype(BF16)
    run_copies([(pack_s, pack_ref)], sems)


def run_copies(pairs, sems):
    copies = [pltpu.make_async_copy(a, b, sems.at[i]) for i, (a, b) in enumerate(pairs)]
    for c in copies:
        c.start()
    for c in copies:
        c.wait()


def side_by_side(refs, rows, target):
    pairs, first = [], 0
    for ref in refs:
        for b in range(ref.shape[0] // rows):
            pairs.append((ref.at[b * rows : (b + 1) * rows, :], target.at[:, first : first + ref.shape[1]]))
            first += ref.shape[1]
    return pairs


def pack_weights(count, bit, ids_ref, *refs):
    weights, (whole_ref, *part_refs, whole_s, in_sems, out_sems) = refs[:count], refs[count:]
    run_copies(side_by_side(weights, whole_s.shape[0], whole_s), in_sems)
    rows = part_refs[0].shape[0]
    starts = (pl.multiple_of(ids_ref[bit] * rows, rows), 2 * rows)
    parts = [(whole_s.at[pl.ds(a, ref.shape[0]), :], ref) for a, ref in zip(starts, part_refs)]
    run_copies(parts + [(whole_s, whole_ref)], out_sems)


def self_forward(
    ids_ref, w0, w1, w2, w3,
    x_ref, states_ref, normed_ref, q_ref, kv_ref, pa_ref, pb_ref, mixed_ref, aux_ref,
    w_s, bias_a, bias_b, table_s,
):
    f = ids_ref[0]
    length, width = x_ref.shape
    inner = H * DH
    enc = states_ref.shape[0] // GROUP
    after_weights = width + w_s.shape[1]
    columns = width * enc // w0.shape[0]
    for k, piece in enumerate((w0, w1, w2, w3)):
        x_ref[own(f ^ k, w0.shape[0]), :] = piece[:, :width]
        w_s[own(f ^ k, w0.shape[0]), :] = piece[:, width:after_weights]
        for i in range(width // columns):
            states_ref[own(f ^ k, enc), i * columns : (i + 1) * columns] = (
                piece[i * enc : (i + 1) * enc, after_weights : after_weights + columns]
            )
        small = piece[0:16, after_weights + columns :].astype(F32)
        aux_ref[:, own(f ^ k, BLOCK)] = small[0:8, :]
        table_s[own(f ^ k, 8), :] = small[8:16, :]
    for hb in range(length // HALF):
        at = slice(hb * HALF, (hb + 1) * HALF)
        x = x_ref[at, :].astype(F32)
        normed = (x * rms(x) * aux_ref[0:1, :]).astype(BF16)
        normed_ref[at, :] = normed
        kv_ref[at, :] = dot(normed, w_s[:, inner:]).astype(BF16)
    q_ref[...] = dot(place_mine(normed_ref, f), w_s[:, :inner]).astype(BF16)
    per_offset = lax.dot_general(
        table_s[...], offset_onehot(BUCKETS, 1), (((0,), (0,)), ((), ())),
        precision=HIGHEST, preferred_element_type=F32,
    )
    first, second = my_blocks(f)
    row = lax.broadcasted_iota(jnp.int32, (BLOCK, 2 * BLOCK), 0)
    col = lax.broadcasted_iota(jnp.int32, (BLOCK, 2 * BLOCK), 1)
    lane = lax.broadcasted_iota(jnp.int32, (BLOCK, length), 1)
    is_far = lane < (second - 1) * BLOCK
    bias_a[:, :, 2 * BLOCK :] = jnp.full((PAIRS, 2 * BLOCK, BLOCK), MASKED, F32)
    for h in range(H):
        at = slice((h % 2) * BLOCK, (h % 2 + 1) * BLOCK)
        spread = jnp.broadcast_to(per_offset[h : h + 1, :], (BLOCK, 4 * BLOCK))
        skewed = pltpu.roll(spread, 0, 1, stride=1, stride_axis=0)[:, : 2 * BLOCK]
        band = jnp.where(col - BLOCK > row, MASKED, skewed)
        bias_a[h // 2, at, pl.ds(pl.multiple_of(first * BLOCK, BLOCK), 2 * BLOCK)] = band
        bias_b[h // 2, at, :] = jnp.where(is_far, per_offset[h : h + 1, 0:1], MASKED)
        bias_b[h // 2, at, pl.ds(pl.multiple_of((second - 1) * BLOCK, BLOCK), 2 * BLOCK)] = band
    for p in range(PAIRS):
        lanes = slice(p * BLOCK, (p + 1) * BLOCK)
        k2 = kv_ref[:, lanes]
        v2 = kv_ref[:, inner + p * BLOCK : inner + (p + 1) * BLOCK]
        for slot in range(2):
            at = slice(slot * BLOCK, (slot + 1) * BLOCK)
            bias = bias_a[p, :, BLOCK:] if slot == 0 else bias_b[p]
            seen = bias.shape[1]
            s = dot_t(stack_heads(q_ref[at, lanes]), k2[:seen, :]) + bias
            probs = softmax(s).astype(BF16)
            (pa_ref, pb_ref)[slot][p] = probs
            mixed_ref[at, lanes] = unstack_heads(dot(probs, v2[:seen, :])).astype(BF16)


def place_cross(w_s, outs_s, pieces, f, half):
    first = w_s.shape[1]
    own_rows = pieces[0].shape[0]
    for owner, start, rows, piece in split_pieces(pieces, f, half):
        place_rows_of(w_s, owner * own_rows + start, rows, piece[:, :first])
        for b in range(outs_s.shape[0] // own_rows):
            to = pl.ds(pl.multiple_of(b * own_rows + start, 16), rows)
            outs_s[to, own(owner, BLOCK)] = piece[:, first + b * BLOCK : first + (b + 1) * BLOCK]


def cross_forward(
    ids_ref, x_ref, mixed_ref, aux_ref,
    w0, w1, w2, w3, w4, w5, states_s,
    h1_ref, n2_ref, cq_ref, ckv_ref, probs_ref, cmixed_ref, h2_ref, n3_ref,
    w_s, outs_s,
):
    f = ids_ref[0]
    inner = H * DH
    half = ids_ref[4]
    place_cross(w_s, outs_s, (w0, w1, w2, w3, w4, w5), f, half)
    hidden = place_mine(x_ref, f).astype(F32) + dot(mixed_ref[...], outs_s[:inner, :])
    h1_ref[...] = hidden
    normed = (hidden * rms(hidden) * aux_ref[1:2, :]).astype(BF16)
    n2_ref[...] = normed
    cq_ref[...] = dot(normed, w_s[:, :inner]).astype(BF16)
    ckv_ref[...] = dot(states_s[...], w_s[:, inner:]).astype(BF16)
    for p in range(PAIRS):
        lanes = slice(p * BLOCK, (p + 1) * BLOCK)
        v2 = ckv_ref[:, inner + p * BLOCK : inner + (p + 1) * BLOCK]
        probs = softmax(dot_t(stack_heads(cq_ref[:, lanes]), ckv_ref[:, lanes])).astype(BF16)
        probs_ref[p] = probs
        cmixed_ref[:, lanes] = unstack_heads(dot(probs, v2)).astype(BF16)
    hidden = h1_ref[...] + dot(cmixed_ref[...], outs_s[inner:, :])
    h2_ref[...] = hidden
    n3_ref[...] = (hidden * rms(hidden) * aux_ref[2:3, :]).astype(BF16)


def feed_forward(
    ids_ref, h2_ref, n3_ref, aux_ref,
    g0, g1, g2, g3, g4, g5, g6, g7, c0, c1, c2, c3,
    result_ref, grad_h2_ref, keep_ref, send_ref, gain_ref,
    gu_s, down_s, cot_s, cot_mine, units_s, gate_s, up_s, chip_s, down_chip_s,
):
    f, orders = ids_ref[0], (ids_ref[1], ids_ref[3])
    chip = f >> 1
    mine_rows, width = h2_ref.shape
    rows = cot_s.shape[0] // GROUP
    hidden_units = down_s.shape[0]
    own_units = hidden_units // GROUP
    half = ids_ref[2]
    own_rows = g0.shape[0]
    for owner, start, size, piece in split_pieces((g0, g1, g2, g3, g4, g5, g6, g7), f, half):
        place_rows_of(gu_s, owner * own_rows + start, size, piece[:, : 2 * hidden_units])
        for b in range(own_units // own_rows):
            first = 2 * hidden_units + b * width
            place_rows_of(down_s, owner * own_units + b * own_rows + start, size, piece[:, first : first + width])
    place_rows(cot_s, (c0, c1, c2, c3), f, 0, rows)
    cot_mine[...] = place_mine(cot_s, f)
    grad_normed = jnp.zeros((mine_rows, width), F32)
    chunk = 256
    for c in range(hidden_units // chunk):
        gate_at, up_at = slice(c * chunk, (c + 1) * chunk), slice(hidden_units + c * chunk, hidden_units + (c + 1) * chunk)
        gate, up = dot(n3_ref[...], gu_s[:, gate_at]), dot(n3_ref[...], gu_s[:, up_at])
        grad_units = dot_t(cot_mine[...], down_s[gate_at, :])
        square = gate * gate
        tanh = jnp.tanh(0.7978845608028654 * (gate + 0.044715 * square * gate))
        half_gate = 0.5 * gate
        gelu = half_gate + half_gate * tanh
        slope = 0.5 + 0.5 * tanh + half_gate * (1.0 - tanh * tanh) * (
            0.7978845608028654 + (3 * 0.044715 * 0.7978845608028654) * square
        )
        units_s[:, gate_at] = (gelu * up).astype(BF16)
        grad_gate = (grad_units * up * slope).astype(BF16)
        grad_up = (grad_units * gelu).astype(BF16)
        gate_s[:, gate_at] = grad_gate
        up_s[:, gate_at] = grad_up
        grad_normed = grad_normed + dot_t(grad_gate, gu_s[:, gate_at]) + dot_t(grad_up, gu_s[:, up_at])
    piece, gain_part = norm_back(h2_ref[...], aux_ref[2:3, :], grad_normed)
    grad_h2_ref[...] = cot_mine[...].astype(F32) + piece
    gain_ref[...] = jnp.broadcast_to(jnp.sum(gain_part, axis=0, keepdims=True), gain_ref.shape)
    mine = own(chip, rows)
    result_ref[...] = (h2_ref[mine, :] + dot(units_s[mine, :], down_s[...])).astype(BF16)
    chip_rows = 2 * g0.shape[0]
    normed_chip = n3_ref[:, own(chip, chip_rows)]
    chip_s[:, :hidden_units] = t_dot(normed_chip, gate_s[...]).astype(BF16)
    chip_s[:, hidden_units:] = t_dot(normed_chip, up_s[...]).astype(BF16)
    emit(keep_ref, send_ref, chip_s, 0, f, orders)
    grad_down = t_dot(units_s[:, own(chip, 2 * own_units)], cot_mine[...]).astype(BF16)
    parts = own_units // g0.shape[0]
    for which in range(2):
        for part in range(parts):
            at = slice((which * parts + part) * g0.shape[0], (which * parts + part + 1) * g0.shape[0])
            down_chip_s[which * g0.shape[0] : (which + 1) * g0.shape[0], part * width : (part + 1) * width] = grad_down[at, :]
    emit(keep_ref, send_ref, down_chip_s, 2 * hidden_units, f, orders)


def put_columns(chip_s, first, grad, own_rows):
    columns = grad.shape[1] // 2
    for which in range(2):
        for part in range(grad.shape[0] // own_rows):
            chip_s[which * own_rows : (which + 1) * own_rows, first + part * columns : first + (part + 1) * columns] = (
                grad[part * own_rows : (part + 1) * own_rows, which * columns : (which + 1) * columns]
            )


def cross_backward(
    ids_ref, grad_h2_ref, h1_ref, n2_ref, cq_ref, ckv_ref, probs_ref, cmixed_ref, mixed_ref, aux_ref,
    w0, w1, w2, w3, w4, w5, states_s,
    grad_h1_ref, mix_ref, states_keep, states_send, keep_ref, send_ref, gain_ref,
    w_s, outs_s, low_s, dq_s, dkv_s, chip_s, states_chip,
):
    f, orders = ids_ref[0], (ids_ref[1], ids_ref[3])
    chip, core = f >> 1, f & 1
    inner = H * DH
    own_rows = w0.shape[0]
    chip_columns = own(chip, 2 * own_rows)
    half = ids_ref[4]
    place_cross(w_s, outs_s, (w0, w1, w2, w3, w4, w5), f, half)
    low = grad_h2_ref[...].astype(BF16)
    low_s[...] = low
    grad_mixed = dot_t(low, outs_s[inner:, :]).astype(BF16)
    put_columns(chip_s, 3 * inner, t_dot(cmixed_ref[...], low_s[:, chip_columns]).astype(BF16), own_rows)
    for p in range(PAIRS):
        lanes = slice(p * BLOCK, (p + 1) * BLOCK)
        v_lanes = slice(inner + p * BLOCK, inner + (p + 1) * BLOCK)
        stacked = stack_heads(grad_mixed[:, lanes])
        probs = probs_ref[p].astype(F32)
        weighted = probs * dot_t(stacked, ckv_ref[:, v_lanes])
        ds = (weighted - probs * jnp.sum(weighted, axis=-1, keepdims=True)).astype(BF16)
        dq_s[:, lanes] = unstack_heads(dot(ds, ckv_ref[:, lanes])).astype(BF16)
        dkv_s[:, lanes] = t_dot(ds, stack_heads(cq_ref[:, lanes])).astype(BF16)
        dkv_s[:, v_lanes] = t_dot(probs_ref[p], stacked).astype(BF16)
    grad_normed = dot_t(dq_s[...], w_s[:, :inner])
    piece, gain_part = norm_back(h1_ref[...], aux_ref[1:2, :], grad_normed)
    grad_h1 = grad_h2_ref[...] + piece
    grad_h1_ref[...] = grad_h1
    gain_ref[...] = jnp.broadcast_to(jnp.sum(gain_part, axis=0, keepdims=True), gain_ref.shape)
    low = grad_h1.astype(BF16)
    low_s[...] = low
    mix_ref[...] = dot_t(low, outs_s[:inner, :]).astype(BF16)
    put_columns(chip_s, 4 * inner, t_dot(mixed_ref[...], low_s[:, chip_columns]).astype(BF16), own_rows)
    chip_s[:, :inner] = t_dot(n2_ref[:, chip_columns], dq_s[...]).astype(BF16)
    chip_s[:, inner : 3 * inner] = t_dot(states_s[:, chip_columns], dkv_s[...]).astype(BF16)
    emit(keep_ref, send_ref, chip_s, 0, f, orders)
    enc = states_s.shape[0] // GROUP
    states_chip[...] = dot_t(dkv_s[own(chip, 2 * enc), :], w_s[:, inner:])
    states_keep[...] = states_chip[own(core, enc), :]
    states_send[...] = states_chip[own(1 - core, enc), :]


def self_backward(ids_ref, mix_ref, q_ref, kv_ref, pa_ref, pb_ref, dq_s, dkv_s, table_s, ds_a, ds_b):
    inner = H * DH
    first, second = my_blocks(ids_ref[0])
    row = lax.broadcasted_iota(jnp.int32, (2 * BLOCK, 4 * BLOCK), 0)
    ds_a[:, 0:BLOCK] = jnp.zeros((2 * BLOCK, BLOCK), F32)
    offset_sums, far_sums = [], []
    for p in range(PAIRS):
        lanes = slice(p * BLOCK, (p + 1) * BLOCK)
        v_lanes = slice(inner + p * BLOCK, inner + (p + 1) * BLOCK)
        k2, v2 = kv_ref[:, lanes], kv_ref[:, v_lanes]
        dk, dv = [], []
        for slot in range(2):
            at = slice(slot * BLOCK, (slot + 1) * BLOCK)
            probs_low = (pa_ref, pb_ref)[slot][p]
            seen = probs_low.shape[1]
            stacked = stack_heads(mix_ref[at, lanes])
            probs = probs_low.astype(F32)
            weighted = probs * dot_t(stacked, v2[:seen, :])
            ds = weighted - probs * jnp.sum(weighted, axis=-1, keepdims=True)
            if slot == 0:
                ds_a[:, BLOCK:] = ds
            else:
                ds_b[...] = ds
            low = ds.astype(BF16)
            dq_s[at, lanes] = unstack_heads(dot(low, k2[:seen, :])).astype(BF16)
            dk.append(t_dot(low, stack_heads(q_ref[at, lanes])))
            dv.append(t_dot(probs_low, stacked))
        for total, to in ((dk, lanes), (dv, v_lanes)):
            seen = total[0].shape[0]
            dkv_s[:seen, to] = (total[0] + total[1][:seen, :]).astype(BF16)
            dkv_s[seen:, to] = total[1][seen:, :].astype(BF16)
        band_b = ds_b[:, pl.ds(pl.multiple_of((second - 1) * BLOCK, BLOCK), 2 * BLOCK)]
        band_a = ds_a[:, pl.ds(pl.multiple_of(first * BLOCK, BLOCK), 2 * BLOCK)]
        far = jnp.sum(ds_b[...], axis=1, keepdims=True) - jnp.sum(band_b, axis=1, keepdims=True)
        skew = jnp.concatenate([band_a + band_b, jnp.zeros((2 * BLOCK, 2 * BLOCK), F32)], axis=1)
        for bit in range(BLOCK.bit_length() - 1):
            moved = pltpu.roll(skew, 4 * BLOCK - (1 << bit), 1)
            skew = jnp.where((row & (1 << bit)) != 0, moved, skew)
        for hd in range(2):
            at = slice(hd * BLOCK, (hd + 1) * BLOCK)
            offset_sums.append(jnp.sum(skew[at, :], axis=0, keepdims=True))
            far_sums.append(jnp.sum(far[at, :], axis=0, keepdims=True))
    per_offset = jnp.concatenate(offset_sums + [jnp.zeros((BLOCK - H, 4 * BLOCK), F32)], axis=0)
    far_all = jnp.concatenate(far_sums + [jnp.zeros((BLOCK - H, 1), F32)], axis=0)
    per_offset = per_offset + jnp.where(
        lax.broadcasted_iota(jnp.int32, (BLOCK, 4 * BLOCK), 1) == 0, far_all, 0.0
    )
    table_s[...] = lax.dot_general(
        offset_onehot(BLOCK, 1), per_offset, (((1,), (1,)), ((), ())),
        precision=HIGHEST, preferred_element_type=F32,
    )


def self_gradients(
    ids_ref, grad_h1_ref, x_ref, normed_ref, aux_ref, gain2_ref, gain3_ref, dq_s, dkv_s, table_s, w0, w1, w2, w3,
    tokens_keep, tokens_send, keep_ref, send_ref,
    w_s, chip_s, small_s, gain_s,
):
    f, orders = ids_ref[0], (ids_ref[1] & SELF_ORDER, ids_ref[3] & SELF_ORDER)
    chip = f >> 1
    length, width = x_ref.shape
    rows = length // GROUP
    inner = H * DH
    own_rows = w0.shape[0]
    chip_columns = own(chip, 2 * own_rows)
    first, second = my_blocks(f)
    for k, piece in enumerate((w0, w1, w2, w3)):
        w_s[own(f ^ k, own_rows), :] = piece[:, width : width + 3 * inner]
    gain = aux_ref[0:1, :]
    mine, block = own(chip, rows), own(f, rows)
    others = own(f ^ 1, rows)
    grad_normed = dot_t(dq_s[mine, :], w_s[:, :inner]) + dot_t(dkv_s[block, :], w_s[:, inner:])
    piece, _ = norm_back(x_ref[block, :].astype(F32), gain, grad_normed)
    tokens_keep[...] = grad_h1_ref[mine, :] + piece
    piece, _ = norm_back(x_ref[others, :].astype(F32), gain, dot_t(dkv_s[others, :], w_s[:, inner:]))
    tokens_send[...] = piece
    chip_w = w_s[chip_columns, :]
    gain_sum = jnp.zeros((1, 2 * own_rows), F32)
    for hb in range(length // HALF):
        at = slice(hb * HALF, (hb + 1) * HALF)
        scaled = x_ref[at, chip_columns].astype(F32) * rms(x_ref[at, :].astype(F32))
        gain_sum = gain_sum + jnp.sum(dot_t(dkv_s[at, :], chip_w[:, inner:]) * scaled, axis=0, keepdims=True)
    grad_q = dot_t(dq_s[...], chip_w[:, :inner])
    for slot, b in enumerate((first, second)):
        scaled = x_ref[own(b, BLOCK), chip_columns].astype(F32) * rms(x_ref[own(b, BLOCK), :].astype(F32))
        gain_sum = gain_sum + jnp.sum(grad_q[slot * BLOCK : (slot + 1) * BLOCK, :] * scaled, axis=0, keepdims=True)
    normed_mine = jnp.concatenate([normed_ref[own(b, BLOCK), chip_columns] for b in (first, second)], axis=0)
    chip_s[:, :inner] = t_dot(normed_mine, dq_s[...]).astype(BF16)
    chip_s[:, inner:] = t_dot(normed_ref[:, chip_columns], dkv_s[...]).astype(BF16)
    emit(keep_ref, send_ref, chip_s, 0, f, orders)
    gain_s[0:8, :] = gain2_ref[...]
    gain_s[8:16, :] = gain3_ref[...]
    buckets = BUCKETS // GROUP
    for which in range(2):
        owner = 2 * chip + which
        small = jnp.concatenate(
            [
                table_s[own(owner, buckets), :],
                gain_sum[:, which * own_rows : (which + 1) * own_rows],
                gain_s[0:1, own(owner, own_rows)],
                gain_s[8:9, own(owner, own_rows)],
                jnp.zeros((own_rows - buckets - 3, BLOCK), F32),
            ],
            axis=0,
        )
        small_s[which * own_rows : (which + 1) * own_rows, :] = small.astype(BF16)
    emit(keep_ref, send_ref, small_s, 3 * inner, f, orders)


def fold(keep_ref, arrived_ref, *out_refs):
    total = (keep_ref[...].astype(F32) + arrived_ref[...].astype(F32)).astype(BF16)
    rows = total.shape[0] // len(out_refs)
    for i, ref in enumerate(out_refs):
        ref[...] = total[i * rows : (i + 1) * rows, :]


def pieces_of(ids_ref, halves, mask=PIECES - 1):
    order = ids_ref[1] & mask
    for i, half in enumerate(halves):
        piece = half.shape[0] * len(halves) // PIECES
        here = PIECES // len(halves)
        for j in range(here):
            q = (i * here + j) ^ order
            yield q * piece, piece, half[j * piece : (j + 1) * piece, :].astype(F32)


def unpack_feed(ids_ref, low_ref, high_ref, gate_ref, up_ref, down_ref):
    units, width, own_rows = gate_ref.shape[1], down_ref.shape[1], gate_ref.shape[0]
    for at, size, rows in pieces_of(ids_ref, (low_ref, high_ref)):
        to = pl.ds(pl.multiple_of(at, size), size)
        gate_ref[to, :] = rows[:, :units]
        up_ref[to, :] = rows[:, units : 2 * units]
        for part in range(down_ref.shape[0] // own_rows):
            first = 2 * units + part * width
            down_ref[pl.ds(pl.multiple_of(part * own_rows + at, size), size), :] = rows[:, first : first + width]


def unpack_cross(ids_ref, low_ref, high_ref, cq_ref, ck_ref, cv_ref, co_ref, out_ref):
    own_rows, inner = cq_ref.shape
    for at, size, rows in pieces_of(ids_ref, (low_ref, high_ref)):
        to = pl.ds(pl.multiple_of(at, size), size)
        for i, ref in enumerate((cq_ref, ck_ref, cv_ref)):
            ref[to, :] = rows[:, i * inner : (i + 1) * inner]
        for i, ref in enumerate((co_ref, out_ref)):
            columns = ref.shape[1]
            for part in range(inner // own_rows):
                first = (3 + i) * inner + part * columns
                ref[pl.ds(pl.multiple_of(part * own_rows + at, size), size), :] = rows[:, first : first + columns]


def unpack_self(ids_ref, low_ref, high_ref, q_ref, k_ref, v_ref, g1_ref, g2_ref, g3_ref, table_ref, small_s):
    inner = q_ref.shape[1]
    for at, size, rows in pieces_of(ids_ref, (low_ref, high_ref), SELF_ORDER):
        to = pl.ds(pl.multiple_of(at, size), size)
        for i, ref in enumerate((q_ref, k_ref, v_ref)):
            ref[to, :] = rows[:, i * inner : (i + 1) * inner]
        small_s[to, :] = rows[:, 3 * inner :]
    buckets, heads = table_ref.shape
    table_ref[...] = small_s[0:buckets, 0:heads]
    for i, ref in enumerate((g1_ref, g2_ref, g3_ref)):
        ref[...] = small_s[buckets + i : buckets + i + 1, :]


VMEM = pl.BlockSpec(memory_space=pltpu.VMEM)
SMEM = pl.BlockSpec(memory_space=pltpu.SMEM)


def call(kernel, name, out_shapes, scratch, args, with_ids=True, place=VMEM):
    return pl.pallas_call(
        kernel,
        name=name,
        out_shape=[jax.ShapeDtypeStruct(s, d) for s, d in out_shapes],
        in_specs=([SMEM] if with_ids else []) + [place] * (len(args) - with_ids),
        out_specs=[place] * len(out_shapes),
        scratch_shapes=[pltpu.VMEM(*s) if isinstance(s, tuple) else s for s in scratch],
        compiler_params=pltpu.CompilerParams(vmem_limit_bytes=VMEM_BYTES if place is VMEM else 56 * 1024 * 1024),
        cost_estimate=pl.CostEstimate(flops=1, bytes_accessed=1, transcendentals=0),
    )(*args)


def hop(x, axis, bits):
    size = lax.axis_size(axis)
    return lax.ppermute(x, axis, [(i, i ^ bits) for i in range(size)])


def all_after(arrays, earlier):
    return lax.optimization_barrier((tuple(arrays), tuple(earlier)))[0]


def beside(pack, far):
    return pack, hop(pack, "fsdp", 1), far, hop(far, "fsdp", 1)


def beside_split(pack, far, far_other, *rest):
    parts = (far, far_other, *rest)
    return pack, hop(pack, "fsdp", 1), *parts, *(hop(a, "fsdp", 1) for a in parts)


def rep_hop(x, bits):
    replicas, group = lax.axis_size("rep"), lax.axis_size("fsdp")
    pairs = [(r * group + f, (r ^ bits[f & 1]) * group + f) for r in range(replicas) for f in range(group)]
    return lax.ppermute(x, ("rep", "fsdp"), pairs)


class Sum:
    def __init__(self, name, keep, send, halvings):
        bits = (lax.axis_size("rep") - 1).bit_length()
        self.name, self.keep, self.at = name, keep, 0
        self.arrived = hop(send, "fsdp", 1)
        self.steps = [(1, 2), (2, 1)] + [(1 << i, 1 << i) for i in range(2, bits)]
        self.back = self.steps[:halvings]
        self.halvings = halvings

    def fold(self, earlier):
        keep, arrived = all_after((self.keep, self.arrived), earlier)
        halving = self.at < self.halvings
        total = (keep.astype(F32) + arrived.astype(F32)).astype(BF16)
        middle = total.shape[0] // 2
        out = (total[:middle], total[middle:]) if halving else (total,)
        self.keep = out[0]
        if self.at < len(self.steps):
            self.arrived = rep_hop(out[-1], self.steps[self.at])
        else:
            self.arrived = rep_hop(self.keep, self.back[-1])
        self.at += 1
        return self.keep

    def widen(self, earlier):
        keep, arrived = all_after((self.keep, self.arrived), earlier)
        self.back.pop()
        self.keep = jnp.concatenate((keep, arrived))
        self.arrived = rep_hop(self.keep, self.back[-1])
        return self.keep

    def halves(self, earlier):
        return all_after((self.keep, self.arrived), earlier)

    def actions(self):
        return [self.fold] * (len(self.steps) + 1 - self.at) + [self.widen] * (len(self.back) - 1)


def per_device(
    tokens,
    states,
    query_w,
    key_w,
    value_w,
    out_w,
    cross_query_w,
    cross_key_w,
    cross_value_w,
    cross_out_w,
    gate_w,
    up_w,
    down_w,
    self_gain,
    cross_gain,
    mlp_gain,
    bias_table,
    cotangent,
):
    seq_count, rows, width = tokens.shape
    enc = states.shape[1]
    own_rows, inner = query_w.shape
    hidden_units = gate_w.shape[1]
    length, enc_all, mine = rows * GROUP, enc * GROUP, 2 * BLOCK
    f = lax.axis_index("fsdp").astype(jnp.int32)
    replica = lax.axis_index("rep").astype(jnp.int32)
    order_0 = ((replica & 1) << 1) | ((replica >> 1) & 1)
    order_1 = replica & 3
    core = f & 1
    ids = jnp.stack(
        [f, jnp.where(core == 0, order_0, order_1), replica & 1, jnp.where(core == 0, order_1, order_0), (replica >> 1) & 1]
    )

    hbm = pl.BlockSpec(memory_space=pl.ANY)
    first_columns = width + 3 * inner + enc * width // rows + BLOCK
    (first_pack,) = call(
        pack_first,
        "pack_first",
        [((rows, first_columns), BF16)],
        [
            ((rows, first_columns), BF16),
            ((1, own_rows), BF16),
            ((1, own_rows), BF16),
            ((1, own_rows), BF16),
            (bias_table.shape, BF16),
            ((16, BLOCK), F32),
            pltpu.SemaphoreType.DMA((8 + rows // enc,)),
        ],
        [tokens[0], query_w, key_w, value_w, states[0], self_gain[None], cross_gain[None], mlp_gain[None], bias_table],
        False,
        hbm,
    )
    (second_ids,) = all_after((ids,), (first_pack,))

    def packed(name, ids, weights, parts, bit):
        columns = sum(w.size for w in weights) // own_rows
        return call(
            functools.partial(pack_weights, len(weights), bit),
            name,
            [((rows, columns), BF16) for rows in (own_rows, *parts)],
            [
                ((own_rows, columns), BF16),
                pltpu.SemaphoreType.DMA((sum(w.shape[0] for w in weights) // own_rows,)),
                pltpu.SemaphoreType.DMA((1 + len(parts),)),
            ],
            [ids, *weights],
            place=hbm,
        )

    second_pack, second_half = packed(
        "pack_second", second_ids, [cross_query_w, cross_key_w, cross_value_w, out_w, cross_out_w], [own_rows // 2], 4
    )
    (third_ids,) = all_after((ids,), (second_pack,))
    part = 3 * own_rows // 8
    third_pack, third_part, third_rest = packed(
        "pack_third", third_ids, [gate_w, up_w, down_w], [part, own_rows - 2 * part], 2
    )
    first_far, second_far = hop(first_pack, "fsdp", 2), hop(second_half, "fsdp", 2)
    (first_far,) = all_after((first_far,), (third_pack,))
    first_packs = beside(first_pack, first_far)

    x, states_all, normed_one, q, kv, probs_a, probs_b, mixed, aux = call(
        self_forward,
        "self_forward",
        [
            ((length, width), BF16),
            ((enc_all, width), BF16),
            ((length, width), BF16),
            ((mine, inner), BF16),
            ((length, 2 * inner), BF16),
            ((PAIRS, 2 * BLOCK, 2 * BLOCK), BF16),
            ((PAIRS, 2 * BLOCK, length), BF16),
            ((mine, inner), BF16),
            ((8, width), F32),
        ],
        [
            ((width, 3 * inner), BF16),
            ((PAIRS, 2 * BLOCK, 3 * BLOCK), F32),
            ((PAIRS, 2 * BLOCK, length), F32),
            ((BUCKETS, BLOCK), F32),
        ],
        [ids, *first_packs],
    )
    (cot_own,) = all_after((cotangent[0],), (first_far,))
    second_far, second_pack, third_pack, third_part, third_rest = all_after(
        (second_far, second_pack, third_pack, third_part, third_rest), (aux,)
    )
    third_far = hop(third_part, "fsdp", 2)
    second_other = hop(second_far, "rep", 2)
    rest_far = hop(third_rest, "fsdp", 2)
    cot_far = hop(cot_own, "fsdp", 2)
    seconds = beside_split(second_pack, second_far, second_other)
    cots = beside(cot_own, cot_far)
    (cross_ids,) = all_after((ids,), (third_far, cots[3]))
    hidden_one, normed_two, cross_q, cross_kv, cross_probs, cross_mixed, hidden_two, normed_three = call(
        cross_forward,
        "cross_forward",
        [
            ((mine, width), F32),
            ((mine, width), BF16),
            ((mine, inner), BF16),
            ((enc_all, 2 * inner), BF16),
            ((PAIRS, 2 * mine, enc_all), BF16),
            ((mine, inner), BF16),
            ((mine, width), F32),
            ((mine, width), BF16),
        ],
        [
            ((width, 3 * inner), BF16),
            ((2 * inner, width), BF16),
        ],
        [cross_ids, x, mixed, aux, *seconds, states_all],
    )
    third_other = hop(third_far, "rep", 1)
    third_far, third_other, rest_far = all_after((third_far, third_other, rest_far), (normed_three,))
    thirds = beside_split(third_pack, third_far, third_other, rest_far)
    down_columns = down_w.size // own_rows
    result, grad_hidden_two, ff_keep, ff_send, mlp_gain_sum = call(
        feed_forward,
        "feed_forward",
        [
            ((rows, width), BF16),
            ((mine, width), F32),
            ((own_rows, 2 * hidden_units + down_columns), BF16),
            ((own_rows, 2 * hidden_units + down_columns), BF16),
            ((8, width), F32),
        ],
        [
            ((width, 2 * hidden_units), BF16),
            ((hidden_units, width), BF16),
            ((length, width), BF16),
            ((mine, width), BF16),
            ((mine, hidden_units), BF16),
            ((mine, hidden_units), BF16),
            ((mine, hidden_units), BF16),
            ((2 * own_rows, 2 * hidden_units), BF16),
            ((2 * own_rows, down_columns), BF16),
        ],
        [ids, hidden_two, normed_three, aux, *thirds, *cots],
    )
    ff_sum = Sum("feed", ff_keep, ff_send, 2)
    grad_hidden_one, grad_mixed, states_keep, states_send, cross_keep, cross_send, cross_gain_sum = call(
        cross_backward,
        "cross_backward",
        [
            ((mine, width), F32),
            ((mine, inner), BF16),
            ((enc, width), F32),
            ((enc, width), F32),
            ((own_rows, 5 * inner), BF16),
            ((own_rows, 5 * inner), BF16),
            ((8, width), F32),
        ],
        [
            ((width, 3 * inner), BF16),
            ((2 * inner, width), BF16),
            ((mine, width), BF16),
            ((mine, inner), BF16),
            ((enc_all, 2 * inner), BF16),
            ((2 * own_rows, 5 * inner), BF16),
            ((2 * enc, width), F32),
        ],
        [
            ids, grad_hidden_two, hidden_one, normed_two, cross_q, cross_kv, cross_probs, cross_mixed, mixed,
            aux, *seconds, states_all,
        ],
    )
    cross_sum = Sum("cross", cross_keep, cross_send, 2)
    sums = {"F": ff_sum, "C": cross_sum}
    done = ff_sum.fold((grad_hidden_one,))
    (grad_mixed,) = all_after((grad_mixed,), (done,))
    grad_q, grad_kv, table_sums = call(
        self_backward,
        "self_backward",
        [((mine, inner), BF16), ((length, 2 * inner), BF16), ((BLOCK, BLOCK), F32)],
        [((2 * BLOCK, 3 * BLOCK), F32), ((2 * BLOCK, length), F32)],
        [ids, grad_mixed, q, kv, probs_a, probs_b],
    )
    done = grad_q
    for turn in EARLY:
        done = sums[turn].fold((done,))
    done = cross_sum.fold((done,))
    (late_ids,) = all_after((ids,), (done,))
    tokens_keep, tokens_send, self_keep, self_send = call(
        self_gradients,
        "self_gradients",
        [
            ((rows, width), F32),
            ((rows, width), F32),
            ((own_rows, 3 * inner + BLOCK), BF16),
            ((own_rows, 3 * inner + BLOCK), BF16),
        ],
        [
            ((width, 3 * inner), BF16),
            ((2 * own_rows, 3 * inner), BF16),
            ((2 * own_rows, BLOCK), BF16),
            ((16, width), F32),
        ],
        [
            late_ids, grad_hidden_one, x, normed_one, aux, cross_gain_sum, mlp_gain_sum,
            grad_q, grad_kv, table_sums, *first_packs,
        ],
    )
    done = tokens_keep
    for turn in TURNS:
        if turn == "X":
            self_keep, self_send = all_after((self_keep, self_send), (done,))
            self_sum = sums["S"] = Sum("self", self_keep, self_send, SELF_HALVINGS)
        elif turn == "T":
            states_send, tokens_send = all_after((states_send, tokens_send), (done,))
            grad_states = states_keep + hop(states_send, "fsdp", 1)
            grad_tokens = tokens_keep + hop(tokens_send, "fsdp", 1)
        elif sums[turn].actions():
            done = sums[turn].actions()[0]((done,))
    while any(part.actions() for part in sums.values()):
        for part in sums.values():
            done = part.actions()[0]((done,)) if part.actions() else done
    grad_gate, grad_up, grad_down = call(
        unpack_feed,
        "unpack_feed",
        [(gate_w.shape, F32), (up_w.shape, F32), (down_w.shape, F32)],
        [],
        [ids, *ff_sum.halves((done,))],
    )
    grad_cross_query, grad_cross_key, grad_cross_value, grad_cross_out, grad_out = call(
        unpack_cross,
        "unpack_cross",
        [(query_w.shape, F32)] * 3 + [(out_w.shape, F32)] * 2,
        [],
        [ids, *cross_sum.halves((grad_gate,))],
    )
    grad_query, grad_key, grad_value, grad_g1, grad_g2, grad_g3, grad_table = call(
        unpack_self,
        "unpack_self",
        [(query_w.shape, F32)] * 3 + [((1, own_rows), F32)] * 3 + [(bias_table.shape, F32)],
        [((own_rows, BLOCK), F32)],
        [ids, *self_sum.halves((grad_cross_query,))],
    )
    return (
        result[None],
        grad_tokens[None],
        grad_states[None],
        grad_query,
        grad_key,
        grad_value,
        grad_out,
        grad_cross_query,
        grad_cross_key,
        grad_cross_value,
        grad_cross_out,
        grad_gate,
        grad_up,
        grad_down,
        grad_g1[0],
        grad_g2[0],
        grad_g3[0],
        grad_table,
    )


def solution(mesh):
    whole = P("rep", "fsdp", None)
    rows, columns, vector = P("fsdp", None), P(None, "fsdp"), P("fsdp")
    weights = (rows, rows, rows, columns, rows, rows, rows, columns, rows, rows, rows)
    small = (vector, vector, vector, rows)
    return jax.shard_map(
        per_device,
        mesh=mesh,
        in_specs=(whole, whole) + weights + small + (whole,),
        out_specs=(whole, whole, whole) + weights + small,
        check_vma=False,
    )
```
